128 devices in a mesh: dp: 8 (over x, core), depth: 2 (over y_lo), height: 8 (over z, y_hi).
Axes of the slice: x: 4, y: 4 (y_hi: 2, y_lo: 2; y = y_hi * 2 + y_lo), z: 4, core: 2. Of those that a mesh axis runs over, the one named last changes fastest.
Arguments:
- act_one: bfloat16 [8, 32, 8, 128, 128], P('dp', None, 'depth', 'height'), may hold values from -6 to 6
- pre_two: bfloat16 [8, 64, 8, 128, 128], P('dp', None, 'depth', 'height'), may hold values from -6 to 6
- cot_three: bfloat16 [8, 128, 4, 4096], P('dp', None, 'depth', 'height'), may hold values from -24 to 24
- weight_two: float32 [64, 864], replicated, may hold values from -6 to 6
- weight_three: float32 [128, 1728], replicated, may hold values from -6 to 6
- moment_two: float32 [55296], P(('dp', 'depth', 'height')), may hold values from -1.2 to 1.2
- moment_three: float32 [221184], P(('dp', 'depth', 'height')), may hold values from -1.2 to 1.2
Outputs:
- grad_input: bfloat16 [8, 32, 8, 128, 128], P('dp', None, 'depth', 'height')
- new_weight_two: float32 [64, 864], replicated
- new_weight_three: float32 [128, 1728], replicated
- new_moment_two: float32 [55296], P(('dp', 'depth', 'height'))
- new_moment_three: float32 [221184], P(('dp', 'depth', 'height'))
The draws below stay inside these ranges and needn't reach their ends.
All inputs are finite; a program needn't handle non-finite values.
Results may differ from the reference program's by a relative error of at most 0.007.
Values may be sent and summed in bfloat16 or wider, within the bound.
No kernel may reach another device: no remote copies, remote signals or barrier semaphores. Data moves between devices by JAX's collectives and lax.ppermute only.
A program may use at most 128 MiB of HBM per device.

```python
import jax
import jax.numpy as jnp
from jax import lax

C1 = 32
C2 = 64
C3 = 128
CW = 128
VOLUMES = 8
D1 = 8
H1 = 128
P2 = 55296
P3 = 221184
N_DP = 8


def levels(rng, shape, shards, low, largest):
    def one(axis_at, parts):
        steps = jax.random.uniform(jax.random.fold_in(jax.random.fold_in(rng, 6), axis_at), (parts,), jnp.float32, low / len(shards), largest / len(shards))
        return jnp.repeat(jnp.exp(steps), shape[axis_at] // parts).reshape((-1,) + (1,) * (len(shape) - axis_at - 1))

    level = one(*shards[0])
    for cut in shards[1:]:
        level = level * one(*cut)
    return level


def bell_draw(key, dims, deviation, reach, pieces=(), held_as=jnp.bfloat16):
    values = deviation * jax.random.normal(key, dims, jnp.float32)
    if pieces:
        values = values * levels(key, dims, pieces, -0.22, 0.18)
    return jnp.clip(values, -reach, reach).astype(held_as)


def setup_inputs(seed: int = 0) -> dict:
    arg_keys = jax.random.split(jax.random.key(seed), 8)
    act_one = bell_draw(arg_keys[0], (VOLUMES, C1, D1, H1, CW), 1.0, 6.0, ((0, 8), (2, 2), (3, 8)))
    pre_two = bell_draw(arg_keys[1], (VOLUMES, C2, D1, H1, CW), 1.0, 6.0, ((0, 8), (2, 2), (3, 8)))
    cot_three = bell_draw(arg_keys[2], (VOLUMES, C3, D1 // 2, (H1 // 2) * (CW // 2)), 4.0, 24.0, ((0, 8), (2, 2), (3, 8)))
    weight_two = bell_draw(arg_keys[3], (C2, C1 * 27), 1.0, 6.0, (), jnp.float32)
    weight_three = bell_draw(arg_keys[4], (C3, C2 * 27), 1.0, 6.0, (), jnp.float32)
    moment_two = bell_draw(arg_keys[5], (P2,), 0.2, 1.2, ((0, 128),), jnp.float32)
    moment_three = bell_draw(arg_keys[6], (P3,), 0.2, 1.2, ((0, 128),), jnp.float32)
    return dict(act_one=act_one, pre_two=pre_two, cot_three=cot_three, weight_two=weight_two, weight_three=weight_three, moment_two=moment_two, moment_three=moment_three)


SLOPE = 0.3
LEARN = 4.0
TRUST = 0.05
MOMENTUM = 0.9
EPSILON = 1e-06

def leaky(value):
    return jnp.where(value > 0, value, SLOPE * value)

def slope_of(value):
    return jnp.where(value > 0, 1.0, SLOPE).astype(jnp.float32)

def lars(weight, grad, moment):
    flat_grad = grad.reshape(-1)
    trust = TRUST * jnp.sqrt(jnp.sum(weight * weight)) / (jnp.sqrt(jnp.sum(flat_grad * flat_grad)) + EPSILON)
    new_moment = MOMENTUM * moment + LEARN * trust * flat_grad
    return (weight - new_moment.reshape(weight.shape), new_moment)

def reference(act_one, pre_two, cot_three, weight_two, weight_three, moment_two, moment_three):
    deep = D1 // 2
    tall = H1 // 2
    broad = CW // 2
    scale_two = (C1 * 27) ** (-0.5)
    scale_three = (C2 * 27) ** (-0.5)
    wb_two = weight_two.astype(jnp.bfloat16).astype(jnp.float32).reshape(C2, C1, 27)
    wb_three = weight_three.astype(jnp.bfloat16).astype(jnp.float32).reshape(C3, C2, 27)

    def one_volume(inputs):
        act, pre, cot = inputs
        pre_f = pre.astype(jnp.float32)
        pooled = leaky(pre_f).reshape(C2, deep, 2, tall, 2, broad, 2).mean(axis=(2, 4, 6)).astype(jnp.bfloat16)
        pooled_f = pooled.astype(jnp.float32)
        cot_f = cot.reshape(C3, deep, tall, broad).astype(jnp.float32)
        cot_pad = jnp.pad(cot_f, ((0, 0), (1, 1), (1, 1), (1, 1)))
        back = jnp.zeros((C2, deep, tall, broad), jnp.float32)
        grads_three = []
        for k in range(27):
            kd, kh, kw = (k // 9, k // 3 % 3, k % 3)
            od, oh, ow = (2 - kd, 2 - kh, 2 - kw)
            piece = cot_pad[:, od:od + deep, oh:oh + tall, ow:ow + broad]
            back = back + jnp.einsum('oi,odhw->idhw', wb_three[:, :, k], piece)
            grads_three.append(jnp.einsum('odhw,idhw->oi', piece, pooled_f))
        back = (scale_three * back).astype(jnp.bfloat16).astype(jnp.float32)
        upper = jnp.broadcast_to(back.reshape(C2, deep, 1, tall, 1, broad, 1), (C2, deep, 2, tall, 2, broad, 2))
        upper = upper.reshape(C2, D1, H1, CW)
        cot_two = (upper * 0.125 * slope_of(pre_f)).astype(jnp.bfloat16).astype(jnp.float32)
        two_pad = jnp.pad(cot_two, ((0, 0), (1, 1), (1, 1), (1, 1)))
        act_f = act.astype(jnp.float32)
        into = jnp.zeros((C1, D1, H1, CW), jnp.float32)
        grads_two = []
        for k in range(27):
            kd, kh, kw = (k // 9, k // 3 % 3, k % 3)
            od, oh, ow = (2 - kd, 2 - kh, 2 - kw)
            piece = two_pad[:, od:od + D1, oh:oh + H1, ow:ow + CW]
            into = into + jnp.einsum('oi,odhw->idhw', wb_two[:, :, k], piece)
            grads_two.append(jnp.einsum('odhw,idhw->oi', piece, act_f))
        grad_in = (scale_two * into).astype(jnp.bfloat16)
        return (grad_in, jnp.stack(grads_two, -1).reshape(C2, C1 * 27), jnp.stack(grads_three, -1).reshape(C3, C2 * 27))
    grad_input, part_two, part_three = lax.map(one_volume, (act_one, pre_two, cot_three))
    grad_two = lax.optimization_barrier(jnp.sum(part_two, axis=0)) * (scale_two / N_DP)
    grad_three = lax.optimization_barrier(jnp.sum(part_three, axis=0)) * (scale_three / N_DP)
    new_weight_two, new_moment_two = lars(weight_two, grad_two, moment_two)
    new_weight_three, new_moment_three = lars(weight_three, grad_three, moment_three)
    return (grad_input, new_weight_two, new_weight_three, new_moment_two, new_moment_three)
```

```python
import jax
import jax.numpy as jnp
from jax import lax
from jax.sharding import PartitionSpec as P

SLOPE = 0.3
LEARN = 4.0
TRUST = 0.05
MOMENTUM = 0.9
EPSILON = 1e-06


def padded_2(x, sides, width):
    for axis, dim in sides:
        devices, length = (lax.axis_size(axis), x.shape[dim])
        up = [(i, (i + 1) % devices) for i in range(devices - 1)]
        down = [(j, i) for i, j in up]
        last = lax.slice_in_dim(x, length - width, length, axis=dim)
        initial = lax.slice_in_dim(x, 0, width, axis=dim)
        before = lax.ppermute(last, axis, up)
        after = lax.ppermute(initial, axis, down)
        x = jnp.concatenate([before, x, after], axis=dim)
    return x


def leaky(value):
    return jnp.where(value > 0, value, SLOPE * value)


def slope_of(value):
    return jnp.where(value > 0, 1.0, SLOPE).astype(jnp.float32)


def local(act_one, pre_two, cot_three, weight_two, weight_three, moment_two, moment_three):
    chan_one = act_one.shape[1]
    chan_two = pre_two.shape[1]
    chan_three = cot_three.shape[1]
    local_d, local_h, local_w = (pre_two.shape[2], pre_two.shape[3], pre_two.shape[4])
    half_d, half_h, half_w = (local_d // 2, local_h // 2, local_w // 2)
    flat_len = half_h * half_w
    volumes = lax.axis_size("dp")
    scale_two = (chan_one * 27) ** (-0.5)
    scale_three = (chan_two * 27) ** (-0.5)
    pre_f = pre_two[0].astype(jnp.float32)
    pooled = leaky(pre_f).reshape(chan_two, half_d, 2, half_h, 2, half_w, 2).mean(axis=(2, 4, 6))
    pooled = pooled.astype(jnp.bfloat16).reshape(chan_two, half_d, flat_len)
    wb_three = weight_three.astype(jnp.bfloat16).reshape(chan_three, chan_two, 27)
    wb_two = weight_two.astype(jnp.bfloat16).reshape(chan_two, chan_one, 27)
    rim_depth = padded_2(cot_three, (("depth", 2),), 1)
    rim_both = padded_2(rim_depth, (("height", 3),), half_w)
    flat = jnp.pad(rim_both[0], ((0, 0), (0, 0), (1, 1)))
    column = lax.broadcasted_iota(jnp.int32, (1, 1, flat_len), 2) % half_w
    back = jnp.zeros((chan_two, half_d, flat_len), jnp.float32)
    grads_three = []
    for k in range(27):
        kd, kh, kw = (k // 9, k // 3 % 3, k % 3)
        od, oh, ow = (2 - kd, 2 - kh, 2 - kw)
        begin = oh * half_w + ow
        piece = flat[:, od : od + half_d, begin : begin + flat_len]
        inside = (column + ow - 1 >= 0) & (column + ow - 1 < half_w)
        piece = jnp.where(inside, piece, jnp.zeros_like(piece))
        back = back + jnp.einsum(
            "oi,odn->idn", wb_three[:, :, k], piece, preferred_element_type=jnp.float32
        )
        grads_three.append(
            jnp.einsum("odn,idn->oi", piece, pooled, preferred_element_type=jnp.float32)
        )
    back = (scale_three * back).astype(jnp.bfloat16).astype(jnp.float32)
    upper = jnp.broadcast_to(
        back.reshape(chan_two, half_d, 1, half_h, 1, half_w, 1),
        (chan_two, half_d, 2, half_h, 2, half_w, 2),
    )
    upper = upper.reshape(chan_two, local_d, local_h, local_w)
    cot_two = (upper * 0.125 * slope_of(pre_f)).astype(jnp.bfloat16)
    grads_two = []
    rim_fine = padded_2(cot_two[None], (("depth", 2), ("height", 3)), 1)[0]
    padded = jnp.pad(rim_fine, ((0, 0), (0, 0), (0, 0), (1, 1)))
    act_local = act_one[0]
    into = jnp.zeros((chan_one, local_d, local_h, local_w), jnp.float32)
    for k in range(27):
        kd, kh, kw = (k // 9, k // 3 % 3, k % 3)
        od, oh, ow = (2 - kd, 2 - kh, 2 - kw)
        piece = padded[:, od : od + local_d, oh : oh + local_h, ow : ow + local_w]
        into = into + jnp.einsum(
            "oi,odhw->idhw", wb_two[:, :, k], piece, preferred_element_type=jnp.float32
        )
        grads_two.append(
            jnp.einsum("odhw,idhw->oi", piece, act_local, preferred_element_type=jnp.float32)
        )
    grad_input = (scale_two * into).astype(jnp.bfloat16)[None]
    axes = ("dp", "depth", "height")
    devices = lax.axis_size(axes)
    shard_two = moment_two.shape[0]
    shard_three = moment_three.shape[0]
    part_two = jnp.stack(grads_two, -1).reshape(devices, shard_two)
    part_three = jnp.stack(grads_three, -1).reshape(devices, shard_three)
    norm_w_two = jnp.sqrt(jnp.sum(weight_two * weight_two))
    norm_w_three = jnp.sqrt(jnp.sum(weight_three * weight_three))
    parts = jnp.concatenate([part_two, part_three], axis=1).astype(jnp.bfloat16)
    parts = lax.all_to_all(parts, axes, 0, 0, tiled=True)
    own = jnp.sum(parts.astype(jnp.float32), axis=0)
    own_two = own[:shard_two] * (scale_two / volumes)
    own_three = own[shard_two:] * (scale_three / volumes)
    send = jnp.concatenate([own_two, own_three, moment_two, moment_three]).astype(jnp.bfloat16)
    send = jnp.broadcast_to(send[None], (devices, send.shape[0]))
    full = lax.all_to_all(send, axes, 0, 0, tiled=True).astype(jnp.float32)
    shard = shard_two + shard_three
    grad_two = full[:, :shard_two]
    grad_three = full[:, shard_two:shard]
    all_two = full[:, shard : shard + shard_two]
    all_three = full[:, shard + shard_two :]
    trust_two = TRUST * norm_w_two / (jnp.sqrt(jnp.sum(grad_two * grad_two)) + EPSILON)
    trust_three = TRUST * norm_w_three / (jnp.sqrt(jnp.sum(grad_three * grad_three)) + EPSILON)
    new_moment_two = MOMENTUM * moment_two + LEARN * trust_two * own_two
    new_moment_three = MOMENTUM * moment_three + LEARN * trust_three * own_three
    full_two = MOMENTUM * all_two + LEARN * trust_two * grad_two
    full_three = MOMENTUM * all_three + LEARN * trust_three * grad_three
    new_weight_two = weight_two - full_two.reshape(weight_two.shape)
    new_weight_three = weight_three - full_three.reshape(weight_three.shape)
    return (grad_input, new_weight_two, new_weight_three, new_moment_two, new_moment_three)


def solution(mesh):
    in_specs = (
        P("dp", None, "depth", "height", None),
        P("dp", None, "depth", "height", None),
        P("dp", None, "depth", "height"),
        P(),
        P(),
        P(("dp", "depth", "height")),
        P(("dp", "depth", "height")),
    )
    out_specs = (
        P("dp", None, "depth", "height", None),
        P(),
        P(),
        P(("dp", "depth", "height")),
        P(("dp", "depth", "height")),
    )
    return jax.shard_map(local, mesh=mesh, in_specs=in_specs, out_specs=out_specs, check_vma=False)
```

```python
import jax
import jax.numpy as jnp
from jax import lax
from jax.experimental import pallas as pl
from jax.experimental.pallas import tpu as pltpu
from jax.sharding import PartitionSpec as P

SLOPE = 0.3
LEARN = 4.0
TRUST = 0.05
MOMENTUM = 0.9
EPSILON = 1e-06
AXES = ("dp", "depth", "height")
F32 = jnp.float32
BF16 = jnp.bfloat16


def call(body, outs, scratch=(), flops=0, moved=0):
    return pl.pallas_call(
        body,
        out_shape=[jax.ShapeDtypeStruct(shape, dtype) for shape, dtype in outs],
        scratch_shapes=list(scratch),
        compiler_params=pltpu.CompilerParams(vmem_limit_bytes=48 * 1024 * 1024),
        cost_estimate=pl.CostEstimate(flops=flops, bytes_accessed=moved, transcendentals=0),
    )


def dot_nt(a, b):
    return lax.dot_general(a, b, (((1,), (1,)), ((), ())), preferred_element_type=F32)


def dot_nn(a, b):
    return lax.dot_general(a, b, (((1,), (0,)), ((), ())), preferred_element_type=F32)


def shifted(x, amount):
    size = x.shape[-1]
    amount = amount % size
    if amount == 0:
        return x
    return jnp.concatenate([x[..., amount:], x[..., :amount]], axis=-1)


def arrange(cot_ref, pre_ref, cot_out, pre_out, up_out, down_out, side_out, diag_up_out, diag_down_out):
    last = lax.axis_index("depth") == 0
    for d in range(2):
        cot = cot_ref[:, d, :]
        cot_out[d] = cot
        for out in (up_out, diag_up_out):
            out[128 * d : 128 * d + 128] = cot[:, :128]
        for out in (down_out, diag_down_out):
            out[128 * d : 128 * d + 128] = cot[:, 384:]
    for d in range(4):
        rows = jnp.swapaxes(pre_ref[:, d].astype(F32), 0, 1).astype(BF16)
        pre_out[d] = rows
        up_out[256 + 64 * d : 320 + 64 * d] = rows[0]
        down_out[256 + 64 * d : 320 + 64 * d] = rows[15]
        if d in (0, 3):
            @pl.when(last == (d == 3))
            def _():
                side_out[...] = rows
                diag_up_out[256:] = rows[0]
                diag_down_out[256:] = rows[15]


def prepare(pre_ref, act_ref, w2_ref, w3_ref, pooled_out, act_out, w2_out, w3_out, norm_out, t2, t3):
    row = lax.broadcasted_iota(jnp.int32, (256, 128), 0)
    col = lax.broadcasted_iota(jnp.int32, (256, 128), 1)
    pool = jnp.where(row // 2 == col, 0.125, 0.0).astype(BF16)
    for d in range(2):
        for t in range(4):
            halves = []
            for half in range(2):
                total = None
                for i in range(2):
                    for j in range(2):
                        x = pre_ref[2 * d + i, 4 * t + 2 * half + j].astype(F32)
                        x = jnp.where(x > 0, x, SLOPE * x)
                        total = x if total is None else total + x
                halves.append(total)
            total = jnp.concatenate(halves, axis=1)
            high = total.astype(BF16)
            low = (total - high.astype(F32)).astype(BF16)
            mean = dot_nn(high, pool) + dot_nn(low, pool)
            pooled_out[64 * d : 64 * d + 64, 128 * t : 128 * t + 128] = mean.astype(BF16)
    lane = lax.broadcasted_iota(jnp.int32, (16, 32, 128), 2)
    for d in range(4):
        rows = jnp.swapaxes(act_ref[:, d].astype(F32), 0, 1)
        before = jnp.where(lane < 127, shifted(rows, 1), 0.0)
        after = jnp.where(lane > 0, shifted(rows, -1), 0.0)
        for ow, value in enumerate((before, rows, after)):
            start = 96 * d + 32 * ow
            act_out[:, start : start + 32, :] = value.astype(BF16)
    w2 = w2_ref[...]
    w3 = w3_ref[...]
    norm_out[0] = jnp.sqrt(jnp.sum(w2 * w2))
    norm_out[1] = jnp.sqrt(jnp.sum(w3 * w3))
    t2[...] = jnp.transpose(w2)
    t3[...] = jnp.transpose(w3)
    for kd in range(3):
        for oh in range(3):
            for ow in range(3):
                k = kd * 9 + (2 - oh) * 3 + (2 - ow)
                block = t3[pl.ds(k, 64, stride=27), :].astype(BF16)
                tap = oh * 3 + ow
                w3_out[64 * kd : 64 * kd + 64, 128 * tap : 128 * tap + 128] = block
    zero = jnp.zeros((32, 64), F32)
    for kd in range(3):
        for ow in range(3):
            taps = []
            for oh in range(3):
                k = kd * 9 + (2 - oh) * 3 + (2 - ow)
                taps.append(t2[pl.ds(k, 32, stride=27), :])
            for r in range(2):
                blocks = taps + [zero] if r == 0 else [zero] + taps
                start = 64 * kd + 32 * r
                w2_out[start : start + 32, 256 * ow : 256 * ow + 256] = jnp.concatenate(blocks, axis=1).astype(BF16)


def coarse(scale, own_ref, side_ref, up_ref, down_ref, dup_ref, ddown_ref, w3_ref, pooled_ref,
           back_out, grad_out, x_buf, s_buf, t3):
    dep = lax.axis_index("depth")
    hgt = lax.axis_index("height")
    x_buf[0] = jnp.zeros((128, 768), BF16)
    x_buf[5] = jnp.zeros((128, 768), BF16)
    own = 1 + 2 * dep
    other = 3 - 2 * dep
    for d in range(2):
        x_buf[own + d, :, 128:640] = own_ref[d]
        x_buf[own + d, :, :128] = up_ref[128 * d : 128 * d + 128]
        x_buf[own + d, :, 640:] = down_ref[128 * d : 128 * d + 128]
        x_buf[other + d, :, 128:640] = side_ref[d]
        x_buf[other + d, :, :128] = dup_ref[128 * d : 128 * d + 128]
        x_buf[other + d, :, 640:] = ddown_ref[128 * d : 128 * d + 128]
    column = lax.broadcasted_iota(jnp.int32, (128, 768), 1) % 64
    back = [None, None, None]
    for z in range(5):
        x = x_buf[dep + z]
        for ow in range(3):
            if ow == 0:
                moved = jnp.where(column > 0, shifted(x, -1), jnp.zeros_like(x))
            elif ow == 1:
                moved = x
            else:
                moved = jnp.where(column < 63, shifted(x, 1), jnp.zeros_like(x))
            for oh in range(3):
                tap = oh * 3 + ow
                s_buf[z, 128 * tap : 128 * tap + 128, :] = shifted(moved, (oh - 1) * 64)
        outs = [i for i in range(3) if 0 <= z - i <= 2]
        low = 2 - z + outs[0]
        y = dot_nn(w3_ref[64 * low : 64 * (low + len(outs)), :], s_buf[z])
        for n, i in enumerate(outs):
            part = y[64 * n : 64 * n + 64]
            back[i] = part if back[i] is None else back[i] + part
    lane = lax.broadcasted_iota(jnp.int32, (64, 768), 1)
    keep = ((lane >= 128) | (hgt > 0)) & ((lane < 640) | (hgt < 7))
    for i in range(3):
        back_out[i + 1 - dep] = jnp.where(keep, scale * back[i], 0.0).astype(BF16)
    back_out[3 * dep] = jnp.zeros((64, 768), BF16)
    parts = [None, None, None]
    for z in range(4):
        s = s_buf[dep + z, :, 128:640]
        ds = [d for d in range(2) if 0 <= z - d <= 2]
        r = dot_nt(pooled_ref[64 * ds[0] : 64 * (ds[-1] + 1), :], s)
        for n, d in enumerate(ds):
            part = r[64 * n : 64 * n + 64]
            od = z - d
            parts[od] = part if parts[od] is None else parts[od] + part
    for od in range(3):
        for oh in range(3):
            for ow in range(3):
                k = (2 - od) * 9 + (2 - oh) * 3 + (2 - ow)
                tap = oh * 3 + ow
                t3[pl.ds(k, 64, stride=27), :] = parts[od][:, 128 * tap : 128 * tap + 128]
    grad_out[...] = jnp.transpose(t3[...]).astype(BF16)


def fine(back_ref, pre_ref, side_ref, up_ref, down_ref, dup_ref, ddown_ref, act_ref,
         z_out, grad_out, upper, t2):
    dep = lax.axis_index("depth")
    row = lax.broadcasted_iota(jnp.int32, (128, 256), 0)
    col = lax.broadcasted_iota(jnp.int32, (128, 256), 1)
    spread = jnp.where(row == col // 2, 0.125, 0.0).astype(BF16)
    for t in range(6):
        x = back_ref[:, :, 128 * t : 128 * t + 128].reshape(256, 128)
        y = dot_nn(x, spread).reshape(4, 64, 256)
        if t > 0:
            upper[:, 2 * t - 1] = y[:, :, :128]
        if t < 5:
            upper[:, 2 * t] = y[:, :, 128:]

    def cot(up, pre):
        return jnp.where(pre.astype(F32) > 0, up, SLOPE * up).astype(BF16)

    for f in range(1, 5):
        slot = (f + 1) // 2
        for h in range(18):
            parent = (h + 1) // 2
            if h == 0:
                pre = up_ref[256 + 64 * (f - 1) : 320 + 64 * (f - 1)]
            elif h == 17:
                pre = down_ref[256 + 64 * (f - 1) : 320 + 64 * (f - 1)]
            else:
                pre = pre_ref[f - 1, h - 1]
            z_out[f, h] = cot(upper[slot, parent], pre)
    edge = 5 * (1 - dep)
    slot = 3 * (1 - dep)
    z_out[5 * dep] = jnp.zeros((18, 64, 128), BF16)
    for h in range(18):
        parent = (h + 1) // 2
        if h == 0:
            pre = dup_ref[256:]
        elif h == 17:
            pre = ddown_ref[256:]
        else:
            pre = side_ref[h - 1]
        z_out[edge, h] = cot(upper[slot, parent], pre)
    parts = [None, None, None]
    for z in range(6):
        first, final = max(0, z - 2), min(3, z)
        total = None
        for h in range(4):
            lhs = jnp.concatenate([act_ref[h + 4 * i, 96 * first : 96 * (final + 1), :] for i in range(4)], axis=1)
            rhs = jnp.concatenate(
                [z_out[z, h + 4 * i : h + 4 * i + 3].reshape(192, 128) for i in range(4)], axis=1
            )
            r = dot_nt(lhs, rhs)
            total = r if total is None else total + r
        for d in range(first, final + 1):
            part = total[96 * (d - first) : 96 * (d - first + 1)]
            parts[z - d] = part if parts[z - d] is None else parts[z - d] + part
    for od in range(3):
        for oh in range(3):
            for ow in range(3):
                k = (2 - od) * 9 + (2 - oh) * 3 + (2 - ow)
                t2[pl.ds(k, 32, stride=27), :] = parts[od][32 * ow : 32 * ow + 32, 64 * oh : 64 * oh + 64]
    grad_out[...] = jnp.transpose(t2[...]).astype(BF16)


def into(scale, z_ref, w2_ref, out_ref, rows):
    lane = lax.broadcasted_iota(jnp.int32, (256, 128), 1)
    for jp in range(4):
        acc = [None] * 4
        for z in range(6):
            blocks = []
            for j in (2 * jp, 2 * jp + 1):
                x = z_ref[z, 2 * j : 2 * j + 4].reshape(256, 128)
                left = jnp.where(lane > 0, shifted(x, -1), jnp.zeros_like(x))
                right = jnp.where(lane < 127, shifted(x, 1), jnp.zeros_like(x))
                blocks.append(jnp.concatenate([left, x, right], axis=0))
            rhs = jnp.concatenate(blocks, axis=1)
            first, final = max(0, z - 2), min(3, z)
            low = 2 - z + first
            y = dot_nn(w2_ref[64 * low : 64 * (low + final - first + 1), :], rhs)
            for d in range(first, final + 1):
                part = y[64 * (d - first) : 64 * (d - first + 1)]
                acc[d] = part if acc[d] is None else acc[d] + part
        for d in range(4):
            for j in range(2):
                for r in range(2):
                    rows[d, 4 * jp + 2 * j + r] = acc[d][32 * r : 32 * r + 32, 128 * j : 128 * j + 128]
    for d in range(4):
        out_ref[:, d] = (scale * jnp.swapaxes(rows[d], 0, 1)).astype(BF16)


def local(act_one, pre_two, cot_three, weight_two, weight_three, moment_two, moment_three):
    scale_two = (act_one.shape[1] * 27) ** (-0.5)
    scale_three = (pre_two.shape[1] * 27) ** (-0.5)
    volumes = lax.axis_size("dp")
    devices = lax.axis_size(AXES)
    pre, act, cot = pre_two[0], act_one[0], cot_three[0]

    cot_rows, pre_rows, send_up, send_down, send_side, send_dup, send_ddown = call(
        arrange,
        [((2, 128, 512), BF16), ((4, 16, 64, 128), BF16), ((512, 128), BF16), ((512, 128), BF16),
         ((16, 64, 128), BF16), ((320, 128), BF16), ((320, 128), BF16)],
        moved=4_000_000,
    )(cot, pre)
    pair = ("depth", "height")
    tall = lax.axis_size("height")
    swap = [(0, 1), (1, 0)]
    lower = [(h, h - 1) for h in range(1, tall)]
    raise_ = [(h, h + 1) for h in range(tall - 1)]
    cross_lower = [(d * tall + h, (1 - d) * tall + h - 1) for d in range(2) for h in range(1, tall)]
    cross_raise = [(d * tall + h, (1 - d) * tall + h + 1) for d in range(2) for h in range(tall - 1)]
    cot_side = lax.ppermute(cot_rows, "depth", swap)
    from_down = lax.ppermute(send_up, "height", lower)
    from_up = lax.ppermute(send_down, "height", raise_)
    from_ddown = lax.ppermute(send_dup, pair, cross_lower)
    from_dup = lax.ppermute(send_ddown, pair, cross_raise)
    pre_side = lax.ppermute(send_side, "depth", swap)

    pooled, acts, wide_two, wide_three, norms = pl.pallas_call(
        prepare,
        out_shape=[
            jax.ShapeDtypeStruct((128, 512), BF16),
            jax.ShapeDtypeStruct((16, 384, 128), BF16),
            jax.ShapeDtypeStruct((192, 768), BF16),
            jax.ShapeDtypeStruct((192, 1152), BF16),
            jax.ShapeDtypeStruct((2,), F32),
        ],
        out_specs=[pl.BlockSpec(memory_space=pltpu.VMEM)] * 4 + [pl.BlockSpec(memory_space=pltpu.SMEM)],
        scratch_shapes=[pltpu.VMEM((864, 64), F32), pltpu.VMEM((1728, 128), F32)],
        compiler_params=pltpu.CompilerParams(vmem_limit_bytes=48 * 1024 * 1024),
        cost_estimate=pl.CostEstimate(flops=100_000_000, bytes_accessed=8_000_000, transcendentals=0),
    )(pre_rows, act, weight_two, weight_three)

    back, part_three = call(
        lambda *refs: coarse(scale_three, *refs),
        [((4, 64, 768), BF16), ((128, 1728), BF16)],
        [pltpu.VMEM((6, 128, 768), BF16), pltpu.VMEM((5, 1152, 768), BF16), pltpu.VMEM((1728, 128), F32)],
        flops=2_000_000_000, moved=4_000_000,
    )(cot_rows, cot_side, from_up, from_down, from_dup, from_ddown, wide_three, pooled)

    cot_two, part_two = call(
        fine,
        [((6, 18, 64, 128), BF16), ((64, 864), BF16)],
        [pltpu.VMEM((4, 10, 64, 128), F32), pltpu.VMEM((864, 64), F32)],
        flops=2_000_000_000, moved=6_000_000,
    )(back, pre_rows, pre_side, from_up, from_down, from_dup, from_ddown, acts)

    grad_input, = call(
        lambda *refs: into(scale_two, *refs),
        [((32, 4, 16, 128), BF16)],
        [pltpu.VMEM((4, 16, 32, 128), F32)],
        flops=4_000_000_000, moved=6_000_000,
    )(cot_two, wide_two)

    shard_two = moment_two.shape[0]
    shard_three = moment_three.shape[0]
    parts = jnp.concatenate([part_two.reshape(devices, shard_two), part_three], axis=1)
    parts = lax.all_to_all(parts, AXES, 0, 0, tiled=True)
    own = jnp.sum(parts.astype(F32), axis=0)
    own_two = own[:shard_two] * (scale_two / volumes)
    own_three = own[shard_two:] * (scale_three / volumes)
    send = jnp.concatenate([own_two, own_three, moment_two, moment_three]).astype(BF16)
    send = jnp.broadcast_to(send[None], (devices, send.shape[0]))
    full = lax.all_to_all(send, AXES, 0, 0, tiled=True).astype(F32)
    shard = shard_two + shard_three
    grad_two = full[:, :shard_two]
    grad_three = full[:, shard_two:shard]
    all_two = full[:, shard : shard + shard_two]
    all_three = full[:, shard + shard_two :]
    trust_two = TRUST * norms[0] / (jnp.sqrt(jnp.sum(grad_two * grad_two)) + EPSILON)
    trust_three = TRUST * norms[1] / (jnp.sqrt(jnp.sum(grad_three * grad_three)) + EPSILON)
    new_moment_two = MOMENTUM * moment_two + LEARN * trust_two * own_two
    new_moment_three = MOMENTUM * moment_three + LEARN * trust_three * own_three
    full_two = MOMENTUM * all_two + LEARN * trust_two * grad_two
    full_three = MOMENTUM * all_three + LEARN * trust_three * grad_three
    new_weight_two = weight_two - full_two.reshape(weight_two.shape)
    new_weight_three = weight_three - full_three.reshape(weight_three.shape)
    return (grad_input[None], new_weight_two, new_weight_three, new_moment_two, new_moment_three)


def solution(mesh):
    in_specs = (
        P("dp", None, "depth", "height", None),
        P("dp", None, "depth", "height", None),
        P("dp", None, "depth", "height"),
        P(),
        P(),
        P(AXES),
        P(AXES),
    )
    out_specs = (
        P("dp", None, "depth", "height", None),
        P(),
        P(),
        P(AXES),
        P(AXES),
    )
    return jax.shard_map(local, mesh=mesh, in_specs=in_specs, out_specs=out_specs, check_vma=False)
```

```python
import jax
import jax.numpy as jnp
from jax import lax
from jax.experimental import pallas as pl
from jax.experimental.pallas import tpu as pltpu
from jax.sharding import PartitionSpec as P

SLOPE = 0.3
LEARN = 4.0
TRUST = 0.05
MOMENTUM = 0.9
EPSILON = 1e-06
AXES = ("dp", "depth", "height")
F32 = jnp.float32
BF16 = jnp.bfloat16


def call(body, outs, scratch=(), flops=0, moved=0):
    return pl.pallas_call(
        body,
        out_shape=[jax.ShapeDtypeStruct(shape, dtype) for shape, dtype in outs],
        scratch_shapes=list(scratch),
        compiler_params=pltpu.CompilerParams(vmem_limit_bytes=48 * 1024 * 1024),
        cost_estimate=pl.CostEstimate(flops=flops, bytes_accessed=moved, transcendentals=0),
    )


def dot_nt(a, b):
    return lax.dot_general(a, b, (((1,), (1,)), ((), ())), preferred_element_type=F32)


def dot_nn(a, b):
    return lax.dot_general(a, b, (((1,), (0,)), ((), ())), preferred_element_type=F32)


def shifted(x, amount):
    size = x.shape[-1]
    amount = amount % size
    if amount == 0:
        return x
    return jnp.concatenate([x[..., amount:], x[..., :amount]], axis=-1)


def arrange(cot_ref, pre_ref, cot_out, pre_out, up_out, down_out, side_out, diag_up_out, diag_down_out):
    last = lax.axis_index("depth") == 0
    for d in range(2):
        cot = cot_ref[:, d, :]
        cot_out[d] = cot
        for out in (up_out, diag_up_out):
            out[128 * d : 128 * d + 128] = cot[:, :128]
        for out in (down_out, diag_down_out):
            out[128 * d : 128 * d + 128] = cot[:, 384:]
    for d in range(4):
        rows = jnp.swapaxes(pre_ref[:, d].astype(F32), 0, 1).astype(BF16)
        pre_out[d] = rows
        up_out[256 + 64 * d : 320 + 64 * d] = rows[0]
        down_out[256 + 64 * d : 320 + 64 * d] = rows[15]
        if d in (0, 3):
            @pl.when(last == (d == 3))
            def _():
                side_out[...] = rows
                diag_up_out[256:] = rows[0]
                diag_down_out[256:] = rows[15]


def prepare(pre_ref, act_ref, w2_ref, w3_ref, pooled_out, act_out, w2_out, w3_out, t2, t3):
    row = lax.broadcasted_iota(jnp.int32, (256, 128), 0)
    col = lax.broadcasted_iota(jnp.int32, (256, 128), 1)
    pool = jnp.where(row // 2 == col, 0.125, 0.0).astype(BF16)
    for d in range(2):
        for t in range(4):
            halves = []
            for half in range(2):
                total = None
                for i in range(2):
                    for j in range(2):
                        x = pre_ref[2 * d + i, 4 * t + 2 * half + j].astype(F32)
                        x = jnp.where(x > 0, x, SLOPE * x)
                        total = x if total is None else total + x
                halves.append(total)
            total = jnp.concatenate(halves, axis=1)
            high = total.astype(BF16)
            low = (total - high.astype(F32)).astype(BF16)
            mean = dot_nn(high, pool) + dot_nn(low, pool)
            pooled_out[64 * d : 64 * d + 64, 128 * t : 128 * t + 128] = mean.astype(BF16)
    lane = lax.broadcasted_iota(jnp.int32, (16, 32, 128), 2)
    for d in range(4):
        rows = jnp.swapaxes(act_ref[:, d].astype(F32), 0, 1)
        before = jnp.where(lane < 127, shifted(rows, 1), 0.0)
        after = jnp.where(lane > 0, shifted(rows, -1), 0.0)
        for ow, value in enumerate((before, rows, after)):
            start = 96 * d + 32 * ow
            act_out[:, start : start + 32, :] = value.astype(BF16)
    t2[...] = jnp.transpose(w2_ref[...])
    t3[...] = jnp.transpose(w3_ref[...])
    for kd in range(3):
        for oh in range(3):
            for ow in range(3):
                k = kd * 9 + (2 - oh) * 3 + (2 - ow)
                block = t3[pl.ds(k, 64, stride=27), :].astype(BF16)
                tap = oh * 3 + ow
                w3_out[64 * kd : 64 * kd + 64, 128 * tap : 128 * tap + 128] = block
    zero = jnp.zeros((32, 64), F32)
    for kd in range(3):
        for ow in range(3):
            taps = []
            for oh in range(3):
                k = kd * 9 + (2 - oh) * 3 + (2 - ow)
                taps.append(t2[pl.ds(k, 32, stride=27), :])
            for r in range(2):
                blocks = taps + [zero] if r == 0 else [zero] + taps
                start = 64 * kd + 32 * r
                w2_out[start : start + 32, 256 * ow : 256 * ow + 256] = jnp.concatenate(blocks, axis=1).astype(BF16)


def coarse(scale, own_ref, side_ref, up_ref, down_ref, dup_ref, ddown_ref, w3_ref, pooled_ref,
           back_out, grad_out, x_buf, s_buf, t3):
    dep = lax.axis_index("depth")
    hgt = lax.axis_index("height")
    x_buf[0] = jnp.zeros((128, 768), BF16)
    x_buf[5] = jnp.zeros((128, 768), BF16)
    own = 1 + 2 * dep
    other = 3 - 2 * dep
    for d in range(2):
        x_buf[own + d, :, 128:640] = own_ref[d]
        x_buf[own + d, :, :128] = up_ref[128 * d : 128 * d + 128]
        x_buf[own + d, :, 640:] = down_ref[128 * d : 128 * d + 128]
        x_buf[other + d, :, 128:640] = side_ref[d]
        x_buf[other + d, :, :128] = dup_ref[128 * d : 128 * d + 128]
        x_buf[other + d, :, 640:] = ddown_ref[128 * d : 128 * d + 128]
    column = lax.broadcasted_iota(jnp.int32, (128, 768), 1) % 64
    back = [None, None, None]
    for z in range(5):
        x = x_buf[dep + z]
        for ow in range(3):
            if ow == 0:
                moved = jnp.where(column > 0, shifted(x, -1), jnp.zeros_like(x))
            elif ow == 1:
                moved = x
            else:
                moved = jnp.where(column < 63, shifted(x, 1), jnp.zeros_like(x))
            for oh in range(3):
                tap = oh * 3 + ow
                s_buf[z, 128 * tap : 128 * tap + 128, :] = shifted(moved, (oh - 1) * 64)
        outs = [i for i in range(3) if 0 <= z - i <= 2]
        low = 2 - z + outs[0]
        y = dot_nn(w3_ref[64 * low : 64 * (low + len(outs)), :], s_buf[z])
        for n, i in enumerate(outs):
            part = y[64 * n : 64 * n + 64]
            back[i] = part if back[i] is None else back[i] + part
    lane = lax.broadcasted_iota(jnp.int32, (64, 768), 1)
    keep = ((lane >= 128) | (hgt > 0)) & ((lane < 640) | (hgt < 7))
    for i in range(3):
        back_out[i + 1 - dep] = jnp.where(keep, scale * back[i], 0.0).astype(BF16)
    back_out[3 * dep] = jnp.zeros((64, 768), BF16)
    parts = [None, None, None]
    for z in range(4):
        s = s_buf[dep + z, :, 128:640]
        ds = [d for d in range(2) if 0 <= z - d <= 2]
        r = dot_nt(pooled_ref[64 * ds[0] : 64 * (ds[-1] + 1), :], s)
        for n, d in enumerate(ds):
            part = r[64 * n : 64 * n + 64]
            od = z - d
            parts[od] = part if parts[od] is None else parts[od] + part
    for od in range(3):
        for oh in range(3):
            for ow in range(3):
                k = (2 - od) * 9 + (2 - oh) * 3 + (2 - ow)
                tap = oh * 3 + ow
                t3[pl.ds(k, 64, stride=27), :] = parts[od][:, 128 * tap : 128 * tap + 128]
    t3[1728:] = jnp.zeros((64, 128), F32)
    for b in range(14):
        grad_out[b] = jnp.transpose(t3[128 * b : 128 * b + 128, :])


def fine(back_ref, pre_ref, side_ref, up_ref, down_ref, dup_ref, ddown_ref, act_ref, three_ref,
         z_out, parts_out, upper, t2, stage):
    dep = lax.axis_index("depth")
    row = lax.broadcasted_iota(jnp.int32, (128, 256), 0)
    col = lax.broadcasted_iota(jnp.int32, (128, 256), 1)
    spread = jnp.where(row == col // 2, 0.125, 0.0).astype(BF16)
    for t in range(6):
        x = back_ref[:, :, 128 * t : 128 * t + 128].reshape(256, 128)
        y = dot_nn(x, spread).reshape(4, 64, 256)
        if t > 0:
            upper[:, 2 * t - 1] = y[:, :, :128]
        if t < 5:
            upper[:, 2 * t] = y[:, :, 128:]

    def cot(up, pre):
        return jnp.where(pre.astype(F32) > 0, up, SLOPE * up).astype(BF16)

    for f in range(1, 5):
        slot = (f + 1) // 2
        for h in range(18):
            parent = (h + 1) // 2
            if h == 0:
                pre = up_ref[256 + 64 * (f - 1) : 320 + 64 * (f - 1)]
            elif h == 17:
                pre = down_ref[256 + 64 * (f - 1) : 320 + 64 * (f - 1)]
            else:
                pre = pre_ref[f - 1, h - 1]
            z_out[f, h] = cot(upper[slot, parent], pre)
    edge = 5 * (1 - dep)
    slot = 3 * (1 - dep)
    z_out[5 * dep] = jnp.zeros((18, 64, 128), BF16)
    for h in range(18):
        parent = (h + 1) // 2
        if h == 0:
            pre = dup_ref[256:]
        elif h == 17:
            pre = ddown_ref[256:]
        else:
            pre = side_ref[h - 1]
        z_out[edge, h] = cot(upper[slot, parent], pre)
    parts = [None, None, None]
    for z in range(6):
        first, final = max(0, z - 2), min(3, z)
        total = None
        for h in range(4):
            lhs = jnp.concatenate([act_ref[h + 4 * i, 96 * first : 96 * (final + 1), :] for i in range(4)], axis=1)
            rhs = jnp.concatenate(
                [z_out[z, h + 4 * i : h + 4 * i + 3].reshape(192, 128) for i in range(4)], axis=1
            )
            r = dot_nt(lhs, rhs)
            total = r if total is None else total + r
        for d in range(first, final + 1):
            part = total[96 * (d - first) : 96 * (d - first + 1)]
            parts[z - d] = part if parts[z - d] is None else parts[z - d] + part
    for od in range(3):
        for oh in range(3):
            for ow in range(3):
                k = (2 - od) * 9 + (2 - oh) * 3 + (2 - ow)
                t2[pl.ds(k, 32, stride=27), :] = parts[od][32 * ow : 32 * ow + 32, 64 * oh : 64 * oh + 64]
    t2[864:] = jnp.zeros((80, 64), F32)
    tail = lax.broadcasted_iota(jnp.int32, (64, 128), 1) < 48
    for half in range(2):
        for b in range(4):
            start = 432 * half + 128 * b
            block = jnp.transpose(t2[start : start + 128, :])
            if b == 3:
                block = jnp.where(tail, block, 0.0)
            stage[pl.ds(half, 64, stride=2), b, :] = block
    for b in range(14):
        stage[:, 4 + b, :] = three_ref[b]
    stage[:, 18:, :] = jnp.zeros((128, 6, 128), F32)
    parts_out[...] = stage[...].astype(BF16)


def into(scale, z_ref, w2_ref, out_ref, rows):
    lane = lax.broadcasted_iota(jnp.int32, (256, 128), 1)
    for jp in range(4):
        acc = [None] * 4
        for z in range(6):
            blocks = []
            for j in (2 * jp, 2 * jp + 1):
                x = z_ref[z, 2 * j : 2 * j + 4].reshape(256, 128)
                left = jnp.where(lane > 0, shifted(x, -1), jnp.zeros_like(x))
                right = jnp.where(lane < 127, shifted(x, 1), jnp.zeros_like(x))
                blocks.append(jnp.concatenate([left, x, right], axis=0))
            rhs = jnp.concatenate(blocks, axis=1)
            first, final = max(0, z - 2), min(3, z)
            low = 2 - z + first
            y = dot_nn(w2_ref[64 * low : 64 * (low + final - first + 1), :], rhs)
            for d in range(first, final + 1):
                part = y[64 * (d - first) : 64 * (d - first + 1)]
                acc[d] = part if acc[d] is None else acc[d] + part
        for d in range(4):
            for j in range(2):
                for r in range(2):
                    rows[d, 4 * jp + 2 * j + r] = acc[d][32 * r : 32 * r + 32, 128 * j : 128 * j + 128]
    for d in range(4):
        out_ref[:, d] = (scale * jnp.swapaxes(rows[d], 0, 1)).astype(BF16)


def reduce(scale_two, scale_three, parts_ref, m2_ref, m3_ref, send_out, own_out, rows):
    total = jnp.sum(parts_ref[...].astype(F32), axis=0)
    row = lax.broadcasted_iota(jnp.int32, (24, 128), 0)
    total = total * jnp.where(row < 4, scale_two, scale_three)
    own_out[...] = total
    rows[...] = jnp.zeros((40, 128), F32)
    rows[:18] = total[:18]
    for b in range(3):
        rows[18 + b, :] = m2_ref[pl.ds(128 * b, 128)]
    rows[21, :48] = m2_ref[pl.ds(384, 48)]
    for b in range(13):
        rows[22 + b, :] = m3_ref[pl.ds(128 * b, 128)]
    rows[35, :64] = m3_ref[pl.ds(1664, 64)]
    send_out[...] = jnp.broadcast_to(rows[...].astype(BF16)[None], (128, 40, 128))


def update(full_ref, own_ref, w2_ref, w3_ref, m2_ref, m3_ref, w2_out, w3_out, m2_out, m3_out, stage):
    w2 = w2_ref[...]
    w3 = w3_ref[...]
    grad = full_ref[:, :18, :].astype(F32)
    square = jnp.sum(grad * grad, axis=0)
    row = lax.broadcasted_iota(jnp.int32, (18, 128), 0)
    norm_two = jnp.sqrt(jnp.sum(jnp.where(row < 4, square, 0.0), keepdims=True))
    norm_three = jnp.sqrt(jnp.sum(jnp.where(row < 4, 0.0, square), keepdims=True))
    rate_two = LEARN * (TRUST * jnp.sqrt(jnp.sum(w2 * w2, keepdims=True)) / (norm_two + EPSILON))
    rate_three = LEARN * (TRUST * jnp.sqrt(jnp.sum(w3 * w3, keepdims=True)) / (norm_three + EPSILON))
    rate = jnp.where(row < 4, rate_two, rate_three)
    stage[...] = MOMENTUM * full_ref[:, 18:36, :].astype(F32) + rate[None] * grad
    for b in range(13):
        cols = slice(128 * b, 128 * b + 128)
        w3_out[:, cols] = w3[:, cols] - stage[:, 4 + b, :]
    w3_out[:, 1664:] = w3[:, 1664:] - stage[:, 17, :64]
    halves = []
    for half in range(2):
        blocks = [stage[pl.ds(half, 64, stride=2), b, :] for b in range(4)]
        halves.append(jnp.concatenate(blocks, axis=1)[:, :432])
    w2_out[...] = w2 - jnp.concatenate(halves, axis=1)
    own = rate * own_ref[:18]
    for b in range(3):
        m2_out[pl.ds(128 * b, 128)] = MOMENTUM * m2_ref[pl.ds(128 * b, 128)] + own[b]
    m2_out[pl.ds(384, 48)] = MOMENTUM * m2_ref[pl.ds(384, 48)] + own[3, :48]
    for b in range(13):
        m3_out[pl.ds(128 * b, 128)] = MOMENTUM * m3_ref[pl.ds(128 * b, 128)] + own[4 + b]
    m3_out[pl.ds(1664, 64)] = MOMENTUM * m3_ref[pl.ds(1664, 64)] + own[17, :64]


def local(act_one, pre_two, cot_three, weight_two, weight_three, moment_two, moment_three):
    scale_two = (act_one.shape[1] * 27) ** (-0.5)
    scale_three = (pre_two.shape[1] * 27) ** (-0.5)
    volumes = lax.axis_size("dp")
    pre, act, cot = pre_two[0], act_one[0], cot_three[0]

    cot_rows, pre_rows, send_up, send_down, send_side, send_dup, send_ddown = call(
        arrange,
        [((2, 128, 512), BF16), ((4, 16, 64, 128), BF16), ((512, 128), BF16), ((512, 128), BF16),
         ((16, 64, 128), BF16), ((320, 128), BF16), ((320, 128), BF16)],
        moved=4_000_000,
    )(cot, pre)
    pair = ("depth", "height")
    tall = lax.axis_size("height")
    swap = [(0, 1), (1, 0)]
    lower = [(h, h - 1) for h in range(1, tall)]
    raise_ = [(h, h + 1) for h in range(tall - 1)]
    cross_lower = [(d * tall + h, (1 - d) * tall + h - 1) for d in range(2) for h in range(1, tall)]
    cross_raise = [(d * tall + h, (1 - d) * tall + h + 1) for d in range(2) for h in range(tall - 1)]
    cot_side = lax.ppermute(cot_rows, "depth", swap)
    from_down = lax.ppermute(send_up, "height", lower)
    from_up = lax.ppermute(send_down, "height", raise_)
    from_ddown = lax.ppermute(send_dup, pair, cross_lower)
    from_dup = lax.ppermute(send_ddown, pair, cross_raise)
    pre_side = lax.ppermute(send_side, "depth", swap)

    pooled, acts, wide_two, wide_three = call(
        prepare,
        [((128, 512), BF16), ((16, 384, 128), BF16), ((192, 768), BF16), ((192, 1152), BF16)],
        [pltpu.VMEM((864, 64), F32), pltpu.VMEM((1728, 128), F32)],
        flops=100_000_000, moved=8_000_000,
    )(pre_rows, act, weight_two, weight_three)

    back, part_three = call(
        lambda *refs: coarse(scale_three, *refs),
        [((4, 64, 768), BF16), ((14, 128, 128), F32)],
        [pltpu.VMEM((6, 128, 768), BF16), pltpu.VMEM((5, 1152, 768), BF16), pltpu.VMEM((1792, 128), F32)],
        flops=2_000_000_000, moved=4_000_000,
    )(cot_rows, cot_side, from_up, from_down, from_dup, from_ddown, wide_three, pooled)

    cot_two, parts = call(
        fine,
        [((6, 18, 64, 128), BF16), ((128, 24, 128), BF16)],
        [pltpu.VMEM((4, 10, 64, 128), F32), pltpu.VMEM((944, 64), F32), pltpu.VMEM((128, 24, 128), F32)],
        flops=2_000_000_000, moved=6_000_000,
    )(back, pre_rows, pre_side, from_up, from_down, from_dup, from_ddown, acts, part_three)

    grad_input, = call(
        lambda *refs: into(scale_two, *refs),
        [((32, 4, 16, 128), BF16)],
        [pltpu.VMEM((4, 16, 32, 128), F32)],
        flops=4_000_000_000, moved=6_000_000,
    )(cot_two, wide_two)

    parts = lax.all_to_all(parts, AXES, 0, 0, tiled=True)
    send, own = call(
        lambda *refs: reduce(scale_two / volumes, scale_three / volumes, *refs),
        [((128, 40, 128), BF16), ((24, 128), F32)],
        [pltpu.VMEM((40, 128), F32)],
        moved=2_000_000,
    )(parts, moment_two, moment_three)
    full = lax.all_to_all(send, AXES, 0, 0, tiled=True)
    new_weight_two, new_weight_three, new_moment_two, new_moment_three = call(
        update,
        [(weight_two.shape, F32), (weight_three.shape, F32), (moment_two.shape, F32), (moment_three.shape, F32)],
        [pltpu.VMEM((128, 18, 128), F32)],
        moved=4_000_000,
    )(full, own, weight_two, weight_three, moment_two, moment_three)
    return (grad_input[None], new_weight_two, new_weight_three, new_moment_two, new_moment_three)


def solution(mesh):
    in_specs = (
        P("dp", None, "depth", "height", None),
        P("dp", None, "depth", "height", None),
        P("dp", None, "depth", "height"),
        P(),
        P(),
        P(AXES),
        P(AXES),
    )
    out_specs = (
        P("dp", None, "depth", "height", None),
        P(),
        P(),
        P(AXES),
        P(AXES),
    )
    return jax.shard_map(local, mesh=mesh, in_specs=in_specs, out_specs=out_specs, check_vma=False)
```

```python
import jax
import jax.numpy as jnp
from jax import lax
from jax.experimental import pallas as pl
from jax.experimental.pallas import tpu as pltpu
from jax.sharding import PartitionSpec as P

SLOPE = 0.3
LEARN = 4.0
TRUST = 0.05
MOMENTUM = 0.9
EPSILON = 1e-06
AXES = ("dp", "depth", "height")
F32 = jnp.float32
BF16 = jnp.bfloat16


def call(body, outs, scratch=(), flops=0, moved=0):
    return pl.pallas_call(
        body,
        out_shape=[jax.ShapeDtypeStruct(shape, dtype) for shape, dtype in outs],
        scratch_shapes=list(scratch),
        compiler_params=pltpu.CompilerParams(vmem_limit_bytes=48 * 1024 * 1024),
        cost_estimate=pl.CostEstimate(flops=flops, bytes_accessed=moved, transcendentals=0),
    )


def dot_nt(a, b):
    return lax.dot_general(a, b, (((1,), (1,)), ((), ())), preferred_element_type=F32)


def dot_nn(a, b):
    return lax.dot_general(a, b, (((1,), (0,)), ((), ())), preferred_element_type=F32)


def shifted(x, amount):
    size = x.shape[-1]
    amount = amount % size
    if amount == 0:
        return x
    return jnp.concatenate([x[..., amount:], x[..., :amount]], axis=-1)


def arrange(cot_ref, pre_ref, act_ref, cot_out, pre_out, side_out, a_out, b_out, diag_a_out, diag_b_out):
    dep = lax.axis_index("depth")
    odd = lax.rem(lax.axis_index("height"), 2) == 1
    cots = [cot_ref[:, d, :] for d in range(2)]
    for d in range(2):
        cot_out[d] = cots[d]
        top, bottom = cots[d][:, :128], cots[d][:, 384:]
        a_out[128 * d : 128 * d + 128] = jnp.where(odd, top, bottom)
        b_out[128 * d : 128 * d + 128] = jnp.where(odd, bottom, top)
    near = jnp.where(dep == 0, cots[1], cots[0])
    diag_a_out[...] = jnp.where(odd, near[:, :128], near[:, 384:])
    diag_b_out[...] = jnp.where(odd, near[:, 384:], near[:, :128])
    for t in range(4):
        side_out[128 * t : 128 * t + 128] = near[:, 128 * t : 128 * t + 128]
    layer = jnp.swapaxes(act_ref[:, 3 * (1 - dep)].astype(F32), 0, 1).astype(BF16)
    side_out[512:] = layer.reshape(512, 128)
    for d in range(4):
        rows = jnp.swapaxes(pre_ref[:, d].astype(F32), 0, 1).astype(BF16)
        pre_out[d] = rows
        place = slice(256 + 64 * d, 320 + 64 * d)
        a_out[place] = jnp.where(odd, rows[0], rows[15])
        b_out[place] = jnp.where(odd, rows[15], rows[0])


def shifts(rows):
    lane = lax.broadcasted_iota(jnp.int32, rows.shape, rows.ndim - 1)
    before = jnp.where(lane < 127, shifted(rows, 1), 0.0)
    after = jnp.where(lane > 0, shifted(rows, -1), 0.0)
    return before, rows, after


def prepare(pre_ref, act_ref, w2_ref, w3_ref, pooled_out, act_out, w2_out, w3_out, t2, t3):
    row = lax.broadcasted_iota(jnp.int32, (256, 128), 0)
    col = lax.broadcasted_iota(jnp.int32, (256, 128), 1)
    pool = jnp.where(row // 2 == col, 0.125, 0.0).astype(BF16)
    for d in range(2):
        for t in range(4):
            halves = []
            for half in range(2):
                total = None
                for i in range(2):
                    for j in range(2):
                        x = pre_ref[2 * d + i, 4 * t + 2 * half + j].astype(F32)
                        x = jnp.where(x > 0, x, SLOPE * x)
                        total = x if total is None else total + x
                halves.append(total)
            total = jnp.concatenate(halves, axis=1)
            high = total.astype(BF16)
            low = (total - high.astype(F32)).astype(BF16)
            mean = dot_nn(high, pool) + dot_nn(low, pool)
            pooled_out[64 * d : 64 * d + 64, 128 * t : 128 * t + 128] = mean.astype(BF16)
    for d in range(4):
        rows = jnp.swapaxes(act_ref[:, d].astype(F32), 0, 1)
        for ow, value in enumerate(shifts(rows)):
            start = 96 * d + 32 * ow
            act_out[:, start : start + 32, :] = value.astype(BF16)
    t2[...] = jnp.transpose(w2_ref[...])
    t3[...] = jnp.transpose(w3_ref[...])
    for kd in range(3):
        for oh in range(3):
            for ow in range(3):
                k = kd * 9 + (2 - oh) * 3 + (2 - ow)
                block = t3[pl.ds(k, 64, stride=27), :].astype(BF16)
                tap = oh * 3 + ow
                w3_out[64 * kd : 64 * kd + 64, 128 * tap : 128 * tap + 128] = block
    zero = jnp.zeros((32, 64), F32)
    for kd in range(3):
        for ow in range(3):
            taps = []
            for oh in range(3):
                k = kd * 9 + (2 - oh) * 3 + (2 - ow)
                taps.append(t2[pl.ds(k, 32, stride=27), :])
            for r in range(2):
                blocks = taps + [zero] if r == 0 else [zero] + taps
                start = 64 * kd + 32 * r
                w2_out[start : start + 32, 256 * ow : 256 * ow + 256] = jnp.concatenate(blocks, axis=1).astype(BF16)


def coarse(scale, own_ref, side_ref, a_ref, b_ref, da_ref, db_ref, w3_ref, pooled_ref,
           back_out, grad_out, s_buf, back, parts, t3):
    dep = lax.axis_index("depth")
    hgt = lax.axis_index("height")
    odd = lax.rem(hgt, 2) == 1

    def slice_of(rows, a, b):
        return jnp.concatenate([jnp.where(odd, a, b)] + rows + [jnp.where(odd, b, a)], axis=1)

    column = lax.broadcasted_iota(jnp.int32, (128, 768), 1) % 64

    def taps(n, x):
        for ow in range(3):
            if ow == 0:
                moved = jnp.where(column > 0, shifted(x, -1), jnp.zeros_like(x))
            elif ow == 1:
                moved = x
            else:
                moved = jnp.where(column < 63, shifted(x, 1), jnp.zeros_like(x))
            for oh in range(3):
                tap = oh * 3 + ow
                s_buf[n, 128 * tap : 128 * tap + 128, :] = shifted(moved, (oh - 1) * 64)

    for z in range(2):
        rows = slice(128 * z, 128 * z + 128)
        taps(z, slice_of([own_ref[z]], a_ref[rows], b_ref[rows]))
    taps(2, slice_of([side_ref[128 * t : 128 * t + 128] for t in range(4)], da_ref[...], db_ref[...]))
    y0 = dot_nn(w3_ref[64:192, :], s_buf[0])
    y1 = dot_nn(w3_ref[0:128, :], s_buf[1])
    back[0] = y0[:64] + y1[:64]
    back[1] = y0[64:] + y1[64:]
    kd = pl.multiple_of(128 * dep, 128)
    back[1 - dep] += dot_nn(w3_ref[pl.ds(kd, 64), :], s_buf[2])
    lane = lax.broadcasted_iota(jnp.int32, (64, 768), 1)
    keep = ((lane >= 128) | (hgt > 0)) & ((lane < 640) | (hgt < 7))
    for d in range(2):
        back_out[d] = jnp.where(keep, scale * back[d], 0.0).astype(BF16)
    r0 = dot_nt(pooled_ref[...], s_buf[0, :, 128:640])
    r1 = dot_nt(pooled_ref[...], s_buf[1, :, 128:640])
    parts[0] = r0[64:]
    parts[1] = r0[:64] + r1[64:]
    parts[2] = r1[:64]
    d = pl.multiple_of(64 * (1 - dep), 64)
    parts[2 * (1 - dep)] += dot_nt(pooled_ref[pl.ds(d, 64), :], s_buf[2, :, 128:640])
    for od in range(3):
        for oh in range(3):
            for ow in range(3):
                k = (2 - od) * 9 + (2 - oh) * 3 + (2 - ow)
                tap = oh * 3 + ow
                t3[pl.ds(k, 64, stride=27), :] = parts[od, :, 128 * tap : 128 * tap + 128]
    t3[1728:] = jnp.zeros((64, 128), F32)
    for b in range(14):
        grad_out[b] = jnp.transpose(t3[128 * b : 128 * b + 128, :])


def fine(back_ref, pre_ref, a_ref, b_ref, act_ref, side_ref, three_ref,
         z_out, parts_out, upper, near, parts, t2, stage):
    dep = lax.axis_index("depth")
    odd = lax.rem(lax.axis_index("height"), 2) == 1
    row = lax.broadcasted_iota(jnp.int32, (128, 256), 0)
    col = lax.broadcasted_iota(jnp.int32, (128, 256), 1)
    spread = jnp.where(row == col // 2, 0.125, 0.0).astype(BF16)
    for t in range(6):
        x = back_ref[:, :, 128 * t : 128 * t + 128].reshape(128, 128)
        y = dot_nn(x, spread).reshape(2, 64, 256)
        if t > 0:
            upper[:, 2 * t - 1] = y[:, :, :128]
        if t < 5:
            upper[:, 2 * t] = y[:, :, 128:]
    for f in range(4):
        place = slice(256 + 64 * f, 320 + 64 * f)
        for h in range(18):
            if h == 0:
                pre = jnp.where(odd, a_ref[place], b_ref[place])
            elif h == 17:
                pre = jnp.where(odd, b_ref[place], a_ref[place])
            else:
                pre = pre_ref[f, h - 1]
            up = upper[f // 2, (h + 1) // 2]
            z_out[f, h] = jnp.where(pre.astype(F32) > 0, up, SLOPE * up).astype(BF16)
    layer = side_ref[512:].astype(F32).reshape(16, 32, 128)
    for ow, value in enumerate(shifts(layer)):
        near[:, 32 * ow : 32 * ow + 32, :] = value.astype(BF16)

    def correlate(z, lhs):
        total = None
        for h in range(4):
            left = jnp.concatenate([lhs(h + 4 * i) for i in range(4)], axis=1)
            right = jnp.concatenate(
                [z_out[z, h + 4 * i : h + 4 * i + 3].reshape(192, 128) for i in range(4)], axis=1
            )
            r = dot_nt(left, right)
            total = r if total is None else total + r
        return total

    sums = [None, None, None]
    for z in range(4):
        first, final = max(0, z - 1), min(3, z + 1)
        total = correlate(z, lambda h: act_ref[h, 96 * first : 96 * (final + 1), :])
        for d in range(first, final + 1):
            part = total[96 * (d - first) : 96 * (d - first + 1)]
            od = z - d + 1
            sums[od] = part if sums[od] is None else sums[od] + part
    for od in range(3):
        parts[od] = sums[od]
    parts[2 * dep] += correlate(3 * (1 - dep), lambda h: near[h])
    for od in range(3):
        for oh in range(3):
            for ow in range(3):
                k = (2 - od) * 9 + (2 - oh) * 3 + (2 - ow)
                t2[pl.ds(k, 32, stride=27), :] = parts[od, 32 * ow : 32 * ow + 32, 64 * oh : 64 * oh + 64]
    t2[864:] = jnp.zeros((80, 64), F32)
    tail = lax.broadcasted_iota(jnp.int32, (64, 128), 1) < 48
    for half in range(2):
        for b in range(4):
            start = 432 * half + 128 * b
            block = jnp.transpose(t2[start : start + 128, :])
            if b == 3:
                block = jnp.where(tail, block, 0.0)
            stage[pl.ds(half, 64, stride=2), b, :] = block
    for b in range(14):
        stage[:, 4 + b, :] = three_ref[b]
    stage[:, 18:, :] = jnp.zeros((128, 6, 128), F32)
    parts_out[...] = stage[...].astype(BF16)


def into(z_ref, w2_ref, rows, ship):
    dep = lax.axis_index("depth")
    lane = lax.broadcasted_iota(jnp.int32, (256, 128), 1)
    for jp in range(4):
        acc = [None] * 6
        for z in range(4):
            blocks = []
            for j in (2 * jp, 2 * jp + 1):
                x = z_ref[z, 2 * j : 2 * j + 4].reshape(256, 128)
                left = jnp.where(lane > 0, shifted(x, -1), jnp.zeros_like(x))
                right = jnp.where(lane < 127, shifted(x, 1), jnp.zeros_like(x))
                blocks.append(jnp.concatenate([left, x, right], axis=0))
            y = dot_nn(w2_ref[...], jnp.concatenate(blocks, axis=1))
            for kd in range(3):
                d = z + kd
                part = y[64 * kd : 64 * kd + 64]
                acc[d] = part if acc[d] is None else acc[d] + part
        for j in range(2):
            for r in range(2):
                h = 4 * jp + 2 * j + r
                block = (slice(32 * r, 32 * r + 32), slice(128 * j, 128 * j + 128))
                ship[h] = jnp.where(dep == 0, acc[5][block], acc[0][block])
                for d in range(4):
                    rows[d, h] = acc[d + 1][block]


def finish(scale, rows_ref, ship_ref, out_ref):
    dep = lax.axis_index("depth")
    for d in range(4):
        rows = rows_ref[d]
        if d in (0, 3):
            rows = rows + jnp.where(dep == (0 if d == 3 else 1), ship_ref[...], 0.0)
        out_ref[:, d] = (scale * jnp.swapaxes(rows, 0, 1)).astype(BF16)


def reduce(scale_two, scale_three, parts_ref, m2_ref, m3_ref, send_out, own_out, rows):
    total = jnp.sum(parts_ref[...].astype(F32), axis=0)
    row = lax.broadcasted_iota(jnp.int32, (24, 128), 0)
    total = total * jnp.where(row < 4, scale_two, scale_three)
    own_out[...] = total
    rows[...] = jnp.zeros((40, 128), F32)
    rows[:18] = total[:18]
    for b in range(3):
        rows[18 + b, :] = m2_ref[pl.ds(128 * b, 128)]
    rows[21, :48] = m2_ref[pl.ds(384, 48)]
    for b in range(13):
        rows[22 + b, :] = m3_ref[pl.ds(128 * b, 128)]
    rows[35, :64] = m3_ref[pl.ds(1664, 64)]
    send_out[...] = jnp.broadcast_to(rows[...].astype(BF16)[None], (128, 40, 128))


def update(full_ref, own_ref, w2_ref, w3_ref, m2_ref, m3_ref, w2_out, w3_out, m2_out, m3_out, stage):
    w2 = w2_ref[...]
    w3 = w3_ref[...]
    grad = full_ref[:, :18, :].astype(F32)
    square = jnp.sum(grad * grad, axis=0)
    row = lax.broadcasted_iota(jnp.int32, (18, 128), 0)
    norm_two = jnp.sqrt(jnp.sum(jnp.where(row < 4, square, 0.0), keepdims=True))
    norm_three = jnp.sqrt(jnp.sum(jnp.where(row < 4, 0.0, square), keepdims=True))
    rate_two = LEARN * (TRUST * jnp.sqrt(jnp.sum(w2 * w2, keepdims=True)) / (norm_two + EPSILON))
    rate_three = LEARN * (TRUST * jnp.sqrt(jnp.sum(w3 * w3, keepdims=True)) / (norm_three + EPSILON))
    rate = jnp.where(row < 4, rate_two, rate_three)
    stage[...] = MOMENTUM * full_ref[:, 18:36, :].astype(F32) + rate[None] * grad
    for b in range(13):
        cols = slice(128 * b, 128 * b + 128)
        w3_out[:, cols] = w3[:, cols] - stage[:, 4 + b, :]
    w3_out[:, 1664:] = w3[:, 1664:] - stage[:, 17, :64]
    halves = []
    for half in range(2):
        blocks = [stage[pl.ds(half, 64, stride=2), b, :] for b in range(4)]
        halves.append(jnp.concatenate(blocks, axis=1)[:, :432])
    w2_out[...] = w2 - jnp.concatenate(halves, axis=1)
    own = rate * own_ref[:18]
    for b in range(3):
        m2_out[pl.ds(128 * b, 128)] = MOMENTUM * m2_ref[pl.ds(128 * b, 128)] + own[b]
    m2_out[pl.ds(384, 48)] = MOMENTUM * m2_ref[pl.ds(384, 48)] + own[3, :48]
    for b in range(13):
        m3_out[pl.ds(128 * b, 128)] = MOMENTUM * m3_ref[pl.ds(128 * b, 128)] + own[4 + b]
    m3_out[pl.ds(1664, 64)] = MOMENTUM * m3_ref[pl.ds(1664, 64)] + own[17, :64]


def local(act_one, pre_two, cot_three, weight_two, weight_three, moment_two, moment_three):
    scale_two = (act_one.shape[1] * 27) ** (-0.5)
    scale_three = (pre_two.shape[1] * 27) ** (-0.5)
    volumes = lax.axis_size("dp")
    pre, act, cot = pre_two[0], act_one[0], cot_three[0]

    cot_rows, pre_rows, send_side, send_a, send_b, send_da, send_db = call(
        arrange,
        [((2, 128, 512), BF16), ((4, 16, 64, 128), BF16), ((1024, 128), BF16), ((512, 128), BF16),
         ((512, 128), BF16), ((128, 128), BF16), ((128, 128), BF16)],
        moved=4_000_000,
    )(cot, pre, act)
    tall = lax.axis_size("height")
    swap = [(0, 1), (1, 0)]
    pairs_a = [(h, h ^ 1) for h in range(tall)]
    pairs_b = [(h, ((h + 1) ^ 1) - 1) for h in range(1, tall - 1)]
    cross_a, cross_b = (
        [(d * tall + i, (1 - d) * tall + j) for d in range(2) for i, j in pairs] for pairs in (pairs_a, pairs_b)
    )
    side = lax.ppermute(send_side, "depth", swap)
    got_a = lax.ppermute(send_a, "height", pairs_a)
    got_b = lax.ppermute(send_b, "height", pairs_b)
    got_da = lax.ppermute(send_da, ("depth", "height"), cross_a)
    got_db = lax.ppermute(send_db, ("depth", "height"), cross_b)

    pooled, acts, wide_two, wide_three = call(
        prepare,
        [((128, 512), BF16), ((16, 384, 128), BF16), ((192, 768), BF16), ((192, 1152), BF16)],
        [pltpu.VMEM((864, 64), F32), pltpu.VMEM((1728, 128), F32)],
        flops=100_000_000, moved=8_000_000,
    )(pre_rows, act, weight_two, weight_three)

    back, part_three = call(
        lambda *refs: coarse(scale_three, *refs),
        [((2, 64, 768), BF16), ((14, 128, 128), F32)],
        [pltpu.VMEM((3, 1152, 768), BF16), pltpu.VMEM((2, 64, 768), F32), pltpu.VMEM((3, 64, 1152), F32),
         pltpu.VMEM((1792, 128), F32)],
        flops=2_000_000_000, moved=4_000_000,
    )(cot_rows, side, got_a, got_b, got_da, got_db, wide_three, pooled)

    cot_two, parts = call(
        fine,
        [((4, 18, 64, 128), BF16), ((128, 24, 128), BF16)],
        [pltpu.VMEM((2, 10, 64, 128), F32), pltpu.VMEM((16, 96, 128), BF16), pltpu.VMEM((3, 96, 192), F32),
         pltpu.VMEM((944, 64), F32), pltpu.VMEM((128, 24, 128), F32)],
        flops=2_000_000_000, moved=6_000_000,
    )(back, pre_rows, got_a, got_b, acts, side, part_three)

    into_rows, ship = call(
        into,
        [((4, 16, 32, 128), F32), ((16, 32, 128), F32)],
        flops=4_000_000_000, moved=6_000_000,
    )(cot_two, wide_two)
    ship = lax.ppermute(ship, "depth", swap)
    grad_input, = call(
        lambda *refs: finish(scale_two, *refs),
        [((32, 4, 16, 128), BF16)],
        moved=2_000_000,
    )(into_rows, ship)

    parts = lax.all_to_all(parts, AXES, 0, 0, tiled=True)
    send, own = call(
        lambda *refs: reduce(scale_two / volumes, scale_three / volumes, *refs),
        [((128, 40, 128), BF16), ((24, 128), F32)],
        [pltpu.VMEM((40, 128), F32)],
        moved=2_000_000,
    )(parts, moment_two, moment_three)
    full = lax.all_to_all(send, AXES, 0, 0, tiled=True)
    new_weight_two, new_weight_three, new_moment_two, new_moment_three = call(
        update,
        [(weight_two.shape, F32), (weight_three.shape, F32), (moment_two.shape, F32), (moment_three.shape, F32)],
        [pltpu.VMEM((128, 18, 128), F32)],
        moved=4_000_000,
    )(full, own, weight_two, weight_three, moment_two, moment_three)
    return (grad_input[None], new_weight_two, new_weight_three, new_moment_two, new_moment_three)


def solution(mesh):
    in_specs = (
        P("dp", None, "depth", "height", None),
        P("dp", None, "depth", "height", None),
        P("dp", None, "depth", "height"),
        P(),
        P(),
        P(AXES),
        P(AXES),
    )
    out_specs = (
        P("dp", None, "depth", "height", None),
        P(),
        P(),
        P(AXES),
        P(AXES),
    )
    return jax.shard_map(local, mesh=mesh, in_specs=in_specs, out_specs=out_specs, check_vma=False)
```

```python
import jax
import jax.numpy as jnp
from jax import lax
from jax.experimental import pallas as pl
from jax.experimental.pallas import tpu as pltpu
from jax.sharding import PartitionSpec as P

SLOPE = 0.3
LEARN = 4.0
TRUST = 0.05
MOMENTUM = 0.9
EPSILON = 1e-06
AXES = ("dp", "depth", "height")
F32 = jnp.float32
BF16 = jnp.bfloat16


def call(body, outs, scratch=(), flops=0, moved=0, limit=20):
    return pl.pallas_call(
        body,
        out_shape=[jax.ShapeDtypeStruct(shape, dtype) for shape, dtype in outs],
        scratch_shapes=list(scratch),
        compiler_params=pltpu.CompilerParams(vmem_limit_bytes=limit * 1024 * 1024),
        cost_estimate=pl.CostEstimate(flops=flops, bytes_accessed=moved, transcendentals=0),
    )


def dot_nt(a, b):
    return lax.dot_general(a, b, (((1,), (1,)), ((), ())), preferred_element_type=F32)


def dot_nn(a, b):
    return lax.dot_general(a, b, (((1,), (0,)), ((), ())), preferred_element_type=F32)


def shifted(x, amount):
    size = x.shape[-1]
    amount = amount % size
    if amount == 0:
        return x
    return jnp.concatenate([x[..., amount:], x[..., :amount]], axis=-1)


def arrange(cot_ref, pre_ref, act_ref, cot_out, side_out, a_out, b_out, diag_a_out, diag_b_out):
    dep = lax.axis_index("depth")
    odd = lax.rem(lax.axis_index("height"), 2) == 1
    cots = [cot_ref[:, d, :] for d in range(2)]
    for d in range(2):
        cot_out[d] = cots[d]
        top, bottom = cots[d][:, :128], cots[d][:, 384:]
        a_out[128 * d : 128 * d + 128] = jnp.where(odd, top, bottom)
        b_out[128 * d : 128 * d + 128] = jnp.where(odd, bottom, top)
    near = jnp.where(dep == 0, cots[1], cots[0])
    diag_a_out[...] = jnp.where(odd, near[:, :128], near[:, 384:])
    diag_b_out[...] = jnp.where(odd, near[:, 384:], near[:, :128])
    for t in range(4):
        side_out[128 * t : 128 * t + 128] = near[:, 128 * t : 128 * t + 128]
    layer = jnp.swapaxes(act_ref[:, 3 * (1 - dep)].astype(F32), 0, 1).astype(BF16)
    side_out[512:] = layer.reshape(512, 128)
    for d in range(4):
        first, final = pre_ref[:, d, 0, :], pre_ref[:, d, 15, :]
        place = slice(256 + 64 * d, 320 + 64 * d)
        a_out[place] = jnp.where(odd, first, final)
        b_out[place] = jnp.where(odd, final, first)


def shifts(rows):
    lane = lax.broadcasted_iota(jnp.int32, rows.shape, rows.ndim - 1)
    before = jnp.where(lane < 127, shifted(rows, 1), 0.0)
    after = jnp.where(lane > 0, shifted(rows, -1), 0.0)
    return before, rows, after


def prepare(pre_ref, act_ref, w2_ref, w3_ref, m2_ref, m3_ref, pre_out, pooled_out, act_out, w2_out, w3_out, m_out, t2):
    for d in range(4):
        pre_out[d] = jnp.swapaxes(pre_ref[:, d].astype(F32), 0, 1).astype(BF16)
    m_out[...] = jnp.zeros((24, 128), F32)
    for b in range(3):
        m_out[b, :] = m2_ref[pl.ds(128 * b, 128)]
    m_out[3, :48] = m2_ref[pl.ds(384, 48)]
    for b in range(13):
        m_out[4 + b, :] = m3_ref[pl.ds(128 * b, 128)]
    m_out[17, :64] = m3_ref[pl.ds(1664, 64)]
    row = lax.broadcasted_iota(jnp.int32, (256, 128), 0)
    col = lax.broadcasted_iota(jnp.int32, (256, 128), 1)
    pool = jnp.where(row // 2 == col, 0.125, 0.0).astype(BF16)
    for d in range(2):
        for t in range(4):
            halves = []
            for half in range(2):
                total = None
                for i in range(2):
                    for j in range(2):
                        x = pre_out[2 * d + i, 4 * t + 2 * half + j].astype(F32)
                        x = jnp.where(x > 0, x, SLOPE * x)
                        total = x if total is None else total + x
                halves.append(total)
            total = jnp.concatenate(halves, axis=1)
            high = total.astype(BF16)
            low = (total - high.astype(F32)).astype(BF16)
            mean = dot_nn(high, pool) + dot_nn(low, pool)
            pooled_out[64 * d : 64 * d + 64, 128 * t : 128 * t + 128] = mean.astype(BF16)
    for d in range(4):
        rows = jnp.swapaxes(act_ref[:, d].astype(F32), 0, 1)
        for ow, value in enumerate(shifts(rows)):
            start = 96 * d + 32 * ow
            act_out[:, start : start + 32, :] = value.astype(BF16)
    t2[...] = jnp.transpose(w2_ref[...])
    for kd in range(3):
        for oh in range(3):
            for ow in range(3):
                k = kd * 9 + (2 - oh) * 3 + (2 - ow)
                block = w3_ref[pl.ds(k, 64, stride=27), :].astype(BF16)
                tap = oh * 3 + ow
                w3_out[64 * kd : 64 * kd + 64, 128 * tap : 128 * tap + 128] = block
    zero = jnp.zeros((32, 64), F32)
    for kd in range(3):
        for ow in range(3):
            taps = []
            for oh in range(3):
                k = kd * 9 + (2 - oh) * 3 + (2 - ow)
                taps.append(t2[pl.ds(k, 32, stride=27), :])
            for r in range(2):
                blocks = taps + [zero] if r == 0 else [zero] + taps
                start = 64 * kd + 32 * r
                w2_out[start : start + 32, 256 * ow : 256 * ow + 256] = jnp.concatenate(blocks, axis=1).astype(BF16)


def coarse(scale, own_ref, side_ref, a_ref, b_ref, da_ref, db_ref, w3_ref, pooled_ref,
           back_out, grad_out, s_buf, back, parts, t3):
    dep = lax.axis_index("depth")
    hgt = lax.axis_index("height")
    odd = lax.rem(hgt, 2) == 1

    def slice_of(rows, a, b):
        return jnp.concatenate([jnp.where(odd, a, b)] + rows + [jnp.where(odd, b, a)], axis=1)

    column = lax.broadcasted_iota(jnp.int32, (128, 768), 1) % 64

    def taps(n, x):
        for ow in range(3):
            if ow == 0:
                moved = jnp.where(column > 0, shifted(x, -1), jnp.zeros_like(x))
            elif ow == 1:
                moved = x
            else:
                moved = jnp.where(column < 63, shifted(x, 1), jnp.zeros_like(x))
            for oh in range(3):
                tap = oh * 3 + ow
                s_buf[n, 128 * tap : 128 * tap + 128, :] = shifted(moved, (oh - 1) * 64)

    for z in range(2):
        rows = slice(128 * z, 128 * z + 128)
        taps(z, slice_of([own_ref[z]], a_ref[rows], b_ref[rows]))
    taps(2, slice_of([side_ref[128 * t : 128 * t + 128] for t in range(4)], da_ref[...], db_ref[...]))
    y0 = dot_nn(w3_ref[64:192, :], s_buf[0])
    y1 = dot_nn(w3_ref[0:128, :], s_buf[1])
    back[0] = y0[:64] + y1[:64]
    back[1] = y0[64:] + y1[64:]
    kd = pl.multiple_of(128 * dep, 128)
    back[1 - dep] += dot_nn(w3_ref[pl.ds(kd, 64), :], s_buf[2])
    lane = lax.broadcasted_iota(jnp.int32, (64, 768), 1)
    keep = ((lane >= 128) | (hgt > 0)) & ((lane < 640) | (hgt < 7))
    for d in range(2):
        back_out[d] = jnp.where(keep, scale * back[d], 0.0).astype(BF16)
    r0 = dot_nt(pooled_ref[...], s_buf[0, :, 128:640])
    r1 = dot_nt(pooled_ref[...], s_buf[1, :, 128:640])
    parts[0] = r0[64:]
    parts[1] = r0[:64] + r1[64:]
    parts[2] = r1[:64]
    d = pl.multiple_of(64 * (1 - dep), 64)
    parts[2 * (1 - dep)] += dot_nt(pooled_ref[pl.ds(d, 64), :], s_buf[2, :, 128:640])
    for od in range(3):
        for oh in range(3):
            for ow in range(3):
                k = (2 - od) * 9 + (2 - oh) * 3 + (2 - ow)
                tap = oh * 3 + ow
                t3[pl.ds(k, 64, stride=27), :] = parts[od, :, 128 * tap : 128 * tap + 128]
    t3[1728:] = jnp.zeros((64, 128), F32)
    for b in range(14):
        grad_out[b] = jnp.transpose(t3[128 * b : 128 * b + 128, :])


def cotangent(back_ref, a_ref, b_ref, pre_rows, upper, z_out):
    odd = lax.rem(lax.axis_index("height"), 2) == 1
    row = lax.broadcasted_iota(jnp.int32, (128, 256), 0)
    col = lax.broadcasted_iota(jnp.int32, (128, 256), 1)
    spread = jnp.where(row == col // 2, 0.125, 0.0).astype(BF16)
    for t in range(6):
        x = back_ref[:, :, 128 * t : 128 * t + 128].reshape(128, 128)
        y = dot_nn(x, spread).reshape(2, 64, 256)
        if t > 0:
            upper[:, 2 * t - 1] = y[:, :, :128]
        if t < 5:
            upper[:, 2 * t] = y[:, :, 128:]
    for f in range(4):
        place = slice(256 + 64 * f, 320 + 64 * f)
        rows = pre_rows(f)
        for h in range(18):
            if h == 0:
                pre = jnp.where(odd, a_ref[place], b_ref[place])
            elif h == 17:
                pre = jnp.where(odd, b_ref[place], a_ref[place])
            else:
                pre = rows[h - 1]
            up = upper[f // 2, (h + 1) // 2]
            z_out[f, h] = jnp.where(pre.astype(F32) > 0, up, SLOPE * up).astype(BF16)


def fine(back_ref, pre_ref, a_ref, b_ref, act_ref, side_ref, three_ref, m_ref,
         parts_out, z_out, upper, near, parts, t2, stage):
    dep = lax.axis_index("depth")
    cotangent(back_ref, a_ref, b_ref, lambda f: pre_ref.at[f], upper, z_out)
    layer = side_ref[512:].astype(F32).reshape(16, 32, 128)
    for ow, value in enumerate(shifts(layer)):
        near[:, 32 * ow : 32 * ow + 32, :] = value.astype(BF16)

    def correlate(z, lhs):
        total = None
        for h in range(4):
            left = jnp.concatenate([lhs(h + 4 * i) for i in range(4)], axis=1)
            right = jnp.concatenate(
                [z_out[z, h + 4 * i : h + 4 * i + 3].reshape(192, 128) for i in range(4)], axis=1
            )
            r = dot_nt(left, right)
            total = r if total is None else total + r
        return total

    sums = [None, None, None]
    for z in range(4):
        first, final = max(0, z - 1), min(3, z + 1)
        total = correlate(z, lambda h: act_ref[h, 96 * first : 96 * (final + 1), :])
        for d in range(first, final + 1):
            part = total[96 * (d - first) : 96 * (d - first + 1)]
            od = z - d + 1
            sums[od] = part if sums[od] is None else sums[od] + part
    for od in range(3):
        parts[od] = sums[od]
    parts[2 * dep] += correlate(3 * (1 - dep), lambda h: near[h])
    for od in range(3):
        for oh in range(3):
            for ow in range(3):
                k = (2 - od) * 9 + (2 - oh) * 3 + (2 - ow)
                t2[pl.ds(k, 32, stride=27), :] = parts[od, 32 * ow : 32 * ow + 32, 64 * oh : 64 * oh + 64]
    t2[864:] = jnp.zeros((80, 64), F32)
    tail = lax.broadcasted_iota(jnp.int32, (64, 128), 1) < 48
    for half in range(2):
        for b in range(4):
            start = 432 * half + 128 * b
            block = jnp.transpose(t2[start : start + 128, :])
            if b == 3:
                block = jnp.where(tail, block, 0.0)
            stage[pl.ds(half, 64, stride=2), b, :] = block
    for b in range(14):
        stage[:, 4 + b, :] = three_ref[b]
    stage[:, 18:, :] = jnp.broadcast_to(m_ref[:6][None], (128, 6, 128))
    parts_out[...] = stage[...].astype(BF16)


def into(back_ref, pre_ref, a_ref, b_ref, w2_ref, rows, ship, z_ref, upper):
    dep = lax.axis_index("depth")
    cotangent(back_ref, a_ref, b_ref, lambda f: jnp.swapaxes(pre_ref[:, f].astype(F32), 0, 1), upper, z_ref)
    lane = lax.broadcasted_iota(jnp.int32, (256, 128), 1)
    for jp in range(4):
        acc = [None] * 6
        for z in range(4):
            blocks = []
            for j in (2 * jp, 2 * jp + 1):
                x = z_ref[z, 2 * j : 2 * j + 4].reshape(256, 128)
                left = jnp.where(lane > 0, shifted(x, -1), jnp.zeros_like(x))
                right = jnp.where(lane < 127, shifted(x, 1), jnp.zeros_like(x))
                blocks.append(jnp.concatenate([left, x, right], axis=0))
            y = dot_nn(w2_ref[...], jnp.concatenate(blocks, axis=1))
            for kd in range(3):
                d = z + kd
                part = y[64 * kd : 64 * kd + 64]
                acc[d] = part if acc[d] is None else acc[d] + part
        for j in range(2):
            for r in range(2):
                h = 4 * jp + 2 * j + r
                block = (slice(32 * r, 32 * r + 32), slice(128 * j, 128 * j + 128))
                ship[h] = jnp.where(dep == 0, acc[5][block], acc[0][block]).astype(BF16)
                for d in range(4):
                    rows[d, h] = acc[d + 1][block]


def finish(scale, rows_ref, ship_ref, out_ref):
    dep = lax.axis_index("depth")
    for d in range(4):
        rows = rows_ref[d]
        if d in (0, 3):
            rows = rows + jnp.where(dep == (0 if d == 3 else 1), ship_ref[...].astype(F32), 0.0)
        out_ref[:, d] = (scale * jnp.swapaxes(rows, 0, 1)).astype(BF16)


def reduce(scale_two, scale_three, parts_ref, m_ref, send_out, own_out, rows):
    total = jnp.sum(parts_ref[:, :18, :].astype(F32), axis=0)
    row = lax.broadcasted_iota(jnp.int32, (18, 128), 0)
    total = total * jnp.where(row < 4, scale_two, scale_three)
    own_out[...] = total
    rows[:18] = total
    rows[18:30] = m_ref[6:18]
    rows[30:] = jnp.zeros((2, 128), F32)
    send_out[...] = jnp.broadcast_to(rows[...].astype(BF16)[None], (128, 32, 128))


def update(full_ref, first_ref, own_ref, w2_ref, w3_ref, m2_ref, m3_ref, w2_out, w3_out, m2_out, m3_out, stage):
    w2 = w2_ref[...]
    w3 = w3_ref[...]
    grad = full_ref[:, :18, :].astype(F32)
    square = jnp.sum(grad * grad, axis=0)
    row = lax.broadcasted_iota(jnp.int32, (18, 128), 0)
    norm_two = jnp.sqrt(jnp.sum(jnp.where(row < 4, square, 0.0), keepdims=True))
    norm_three = jnp.sqrt(jnp.sum(jnp.where(row < 4, 0.0, square), keepdims=True))
    rate_two = LEARN * (TRUST * jnp.sqrt(jnp.sum(w2 * w2, keepdims=True)) / (norm_two + EPSILON))
    rate_three = LEARN * (TRUST * jnp.sqrt(jnp.sum(w3 * w3, keepdims=True)) / (norm_three + EPSILON))
    rate = jnp.where(row < 4, rate_two, rate_three)
    stage[:, :6, :] = MOMENTUM * first_ref[:, 18:, :].astype(F32)
    stage[:, 6:, :] = MOMENTUM * full_ref[:, 18:30, :].astype(F32)
    stage[...] += rate[None] * grad
    for b in range(13):
        rows = slice(128 * b, 128 * b + 128)
        w3_out[rows] = w3[rows] - jnp.transpose(stage[:, 4 + b, :])
    w3_out[1664:] = w3[1664:] - jnp.transpose(stage[:, 17, :])[:64]
    halves = []
    for half in range(2):
        blocks = [stage[pl.ds(half, 64, stride=2), b, :] for b in range(4)]
        halves.append(jnp.concatenate(blocks, axis=1)[:, :432])
    w2_out[...] = w2 - jnp.concatenate(halves, axis=1)
    own = rate * own_ref[...]
    for b in range(3):
        m2_out[pl.ds(128 * b, 128)] = MOMENTUM * m2_ref[pl.ds(128 * b, 128)] + own[b]
    m2_out[pl.ds(384, 48)] = MOMENTUM * m2_ref[pl.ds(384, 48)] + own[3, :48]
    for b in range(13):
        m3_out[pl.ds(128 * b, 128)] = MOMENTUM * m3_ref[pl.ds(128 * b, 128)] + own[4 + b]
    m3_out[pl.ds(1664, 64)] = MOMENTUM * m3_ref[pl.ds(1664, 64)] + own[17, :64]


def local(act_one, pre_two, cot_three, weight_two, weight_three, moment_two, moment_three):
    scale_two = (act_one.shape[1] * 27) ** (-0.5)
    scale_three = (pre_two.shape[1] * 27) ** (-0.5)
    volumes = lax.axis_size("dp")
    pre, act, cot = pre_two[0], act_one[0], cot_three[0]

    cot_rows, send_side, send_a, send_b, send_da, send_db = call(
        arrange,
        [((2, 128, 512), BF16), ((1024, 128), BF16), ((512, 128), BF16),
         ((512, 128), BF16), ((128, 128), BF16), ((128, 128), BF16)],
        moved=4_000_000,
    )(cot, pre, act)
    tall = lax.axis_size("height")
    swap = [(0, 1), (1, 0)]
    pairs_a = [(h, h ^ 1) for h in range(tall)]
    pairs_b = [(h, ((h + 1) ^ 1) - 1) for h in range(1, tall - 1)]
    cross_a, cross_b = (
        [(d * tall + i, (1 - d) * tall + j) for d in range(2) for i, j in pairs] for pairs in (pairs_a, pairs_b)
    )
    side = lax.ppermute(send_side, "depth", swap)
    got_a = lax.ppermute(send_a, "height", pairs_a)
    got_b = lax.ppermute(send_b, "height", pairs_b)
    got_da = lax.ppermute(send_da, ("depth", "height"), cross_a)
    got_db = lax.ppermute(send_db, ("depth", "height"), cross_b)

    pre_rows, pooled, acts, wide_two, wide_three, moments = call(
        prepare,
        [((4, 16, 64, 128), BF16), ((128, 512), BF16), ((16, 384, 128), BF16), ((192, 768), BF16), ((192, 1152), BF16), ((24, 128), F32)],
        [pltpu.VMEM((864, 64), F32)],
        flops=100_000_000, moved=8_000_000,
    )(pre, act, weight_two, weight_three.T, moment_two, moment_three)

    back, part_three = call(
        lambda *refs: coarse(scale_three, *refs),
        [((2, 64, 768), BF16), ((14, 128, 128), F32)],
        [pltpu.VMEM((3, 1152, 768), BF16), pltpu.VMEM((2, 64, 768), F32), pltpu.VMEM((3, 64, 1152), F32),
         pltpu.VMEM((1792, 128), F32)],
        flops=2_000_000_000, moved=4_000_000,
    )(cot_rows, side, got_a, got_b, got_da, got_db, wide_three, pooled)

    parts, = call(
        fine,
        [((128, 24, 128), BF16)],
        [pltpu.VMEM((4, 18, 64, 128), BF16), pltpu.VMEM((2, 10, 64, 128), F32), pltpu.VMEM((16, 96, 128), BF16), pltpu.VMEM((3, 96, 192), F32),
         pltpu.VMEM((944, 64), F32), pltpu.VMEM((128, 24, 128), F32)],
        flops=2_000_000_000, moved=6_000_000,
    )(back, pre_rows, got_a, got_b, acts, side, part_three, moments)

    parts = lax.all_to_all(parts, AXES, 0, 0, tiled=True)
    into_rows, ship = call(
        into,
        [((4, 16, 32, 128), F32), ((16, 32, 128), BF16)],
        [pltpu.VMEM((4, 18, 64, 128), BF16), pltpu.VMEM((2, 10, 64, 128), F32)],
        flops=4_000_000_000, moved=6_000_000,
    )(back, pre, got_a, got_b, wide_two)
    ship = lax.ppermute(ship, "depth", swap)
    parts, into_rows, ship = lax.optimization_barrier((parts, into_rows, ship))
    grad_input, = call(
        lambda *refs: finish(scale_two, *refs),
        [((32, 4, 16, 128), BF16)],
        moved=2_000_000,
    )(into_rows, ship)

    send, own = call(
        lambda *refs: reduce(scale_two / volumes, scale_three / volumes, *refs),
        [((128, 32, 128), BF16), ((18, 128), F32)],
        [pltpu.VMEM((32, 128), F32)],
        moved=2_000_000,
    )(parts, moments)
    own, w2, w3 = lax.optimization_barrier((own, weight_two, weight_three))
    full = lax.all_to_all(send, AXES, 0, 0, tiled=True)
    new_weight_two, new_weight_three, new_moment_two, new_moment_three = call(
        update,
        [(weight_two.shape, F32), (weight_three.shape[::-1], F32), (moment_two.shape, F32), (moment_three.shape, F32)],
        [pltpu.VMEM((128, 18, 128), F32)],
        moved=4_000_000,
    )(full, parts, own, w2, w3.T, moment_two, moment_three)
    return (grad_input[None], new_weight_two, new_weight_three.T, new_moment_two, new_moment_three)


def solution(mesh):
    in_specs = (
        P("dp", None, "depth", "height", None),
        P("dp", None, "depth", "height", None),
        P("dp", None, "depth", "height"),
        P(),
        P(),
        P(AXES),
        P(AXES),
    )
    out_specs = (
        P("dp", None, "depth", "height", None),
        P(),
        P(),
        P(AXES),
        P(AXES),
    )
    return jax.shard_map(local, mesh=mesh, in_specs=in_specs, out_specs=out_specs, check_vma=False)
```

```python
import jax
import jax.numpy as jnp
from jax import lax
from jax.experimental import pallas as pl
from jax.experimental.pallas import tpu as pltpu
from jax.sharding import PartitionSpec as P

SLOPE = 0.3
LEARN = 4.0
TRUST = 0.05
MOMENTUM = 0.9
EPSILON = 1e-06
AXES = ("dp", "depth", "height")
F32 = jnp.float32
BF16 = jnp.bfloat16


def call(body, outs, scratch=(), flops=0, moved=0, limit=20, far=None):
    extra = {} if far is None else dict(in_specs=[pl.BlockSpec(memory_space=pl.ANY)] * far)
    return pl.pallas_call(
        body,
        **extra,
        out_shape=[jax.ShapeDtypeStruct(shape, dtype) for shape, dtype in outs],
        scratch_shapes=list(scratch),
        compiler_params=pltpu.CompilerParams(vmem_limit_bytes=limit * 1024 * 1024),
        cost_estimate=pl.CostEstimate(flops=flops, bytes_accessed=moved, transcendentals=0),
    )


def dot_nt(a, b):
    return lax.dot_general(a, b, (((1,), (1,)), ((), ())), preferred_element_type=F32)


def dot_nn(a, b):
    return lax.dot_general(a, b, (((1,), (0,)), ((), ())), preferred_element_type=F32)


def shifted(x, amount):
    size = x.shape[-1]
    amount = amount % size
    if amount == 0:
        return x
    return jnp.concatenate([x[..., amount:], x[..., :amount]], axis=-1)


def arrange(cot_far, pre_far, act_far, cot_out, side_out, a_out, b_out, diag_a_out, diag_b_out,
            cot_ref, pre_ref, act_ref, sems):
    dep = lax.axis_index("depth")
    loads = [
        pltpu.make_async_copy(cot_far, cot_ref, sems.at[0]),
        pltpu.make_async_copy(act_far.at[:, 3 * (1 - dep)], act_ref, sems.at[1]),
        pltpu.make_async_copy(pre_far, pre_ref, sems.at[2]),
    ]
    for load in loads:
        load.start()
    loads[0].wait()
    odd = lax.rem(lax.axis_index("height"), 2) == 1
    cots = [cot_ref[:, d, :] for d in range(2)]
    for d in range(2):
        cot_out[d] = cots[d]
        top, bottom = cots[d][:, :128], cots[d][:, 384:]
        a_out[128 * d : 128 * d + 128] = jnp.where(odd, top, bottom)
        b_out[128 * d : 128 * d + 128] = jnp.where(odd, bottom, top)
    near = jnp.where(dep == 0, cots[1], cots[0])
    diag_a_out[...] = jnp.where(odd, near[:, :128], near[:, 384:])
    diag_b_out[...] = jnp.where(odd, near[:, 384:], near[:, :128])
    for t in range(4):
        side_out[128 * t : 128 * t + 128] = near[:, 128 * t : 128 * t + 128]
    loads[1].wait()
    layer = jnp.swapaxes(act_ref[...].astype(F32), 0, 1).astype(BF16)
    side_out[512:] = layer.reshape(512, 128)
    loads[2].wait()
    for d in range(4):
        first, final = pre_ref[:, d, 0, :], pre_ref[:, d, 15, :]
        place = slice(256 + 64 * d, 320 + 64 * d)
        a_out[place] = jnp.where(odd, first, final)
        b_out[place] = jnp.where(odd, final, first)


def shifts(rows):
    lane = lax.broadcasted_iota(jnp.int32, rows.shape, rows.ndim - 1)
    before = jnp.where(lane < 127, shifted(rows, 1), 0.0)
    after = jnp.where(lane > 0, shifted(rows, -1), 0.0)
    return before, rows, after


def prepare(pre_ref, act_ref, w2_ref, w3_ref, m2_ref, m3_ref, pre_out, pooled_out, act_out, w2_out, w3_out, m_out, t2):
    for d in range(4):
        pre_out[d] = jnp.swapaxes(pre_ref[:, d].astype(F32), 0, 1).astype(BF16)
    m_out[...] = jnp.zeros((24, 128), F32)
    for b in range(3):
        m_out[b, :] = m2_ref[pl.ds(128 * b, 128)]
    m_out[3, :48] = m2_ref[pl.ds(384, 48)]
    for b in range(13):
        m_out[4 + b, :] = m3_ref[pl.ds(128 * b, 128)]
    m_out[17, :64] = m3_ref[pl.ds(1664, 64)]
    row = lax.broadcasted_iota(jnp.int32, (256, 128), 0)
    col = lax.broadcasted_iota(jnp.int32, (256, 128), 1)
    pool = jnp.where(row // 2 == col, 0.125, 0.0).astype(BF16)
    for d in range(2):
        for t in range(4):
            halves = []
            for half in range(2):
                total = None
                for i in range(2):
                    for j in range(2):
                        x = pre_out[2 * d + i, 4 * t + 2 * half + j].astype(F32)
                        x = jnp.where(x > 0, x, SLOPE * x)
                        total = x if total is None else total + x
                halves.append(total)
            total = jnp.concatenate(halves, axis=1)
            high = total.astype(BF16)
            low = (total - high.astype(F32)).astype(BF16)
            mean = dot_nn(high, pool) + dot_nn(low, pool)
            pooled_out[64 * d : 64 * d + 64, 128 * t : 128 * t + 128] = mean.astype(BF16)
    for d in range(4):
        rows = jnp.swapaxes(act_ref[:, d].astype(F32), 0, 1)
        for ow, value in enumerate(shifts(rows)):
            start = 96 * d + 32 * ow
            act_out[:, start : start + 32, :] = value.astype(BF16)
    t2[...] = jnp.transpose(w2_ref[...])
    for kd in range(3):
        for oh in range(3):
            for ow in range(3):
                k = kd * 9 + (2 - oh) * 3 + (2 - ow)
                block = w3_ref[pl.ds(k, 64, stride=27), :].astype(BF16)
                tap = oh * 3 + ow
                w3_out[64 * kd : 64 * kd + 64, 128 * tap : 128 * tap + 128] = block
    zero = jnp.zeros((32, 64), F32)
    for kd in range(3):
        for ow in range(3):
            taps = []
            for oh in range(3):
                k = kd * 9 + (2 - oh) * 3 + (2 - ow)
                taps.append(t2[pl.ds(k, 32, stride=27), :])
            for r in range(2):
                blocks = taps + [zero] if r == 0 else [zero] + taps
                start = 64 * kd + 32 * r
                w2_out[start : start + 32, 256 * ow : 256 * ow + 256] = jnp.concatenate(blocks, axis=1).astype(BF16)


def coarse(scale, own_ref, side_ref, a_ref, b_ref, da_ref, db_ref, w3_ref, pooled_ref,
           back_out, grad_out, s_buf, back, parts, t3):
    dep = lax.axis_index("depth")
    hgt = lax.axis_index("height")
    odd = lax.rem(hgt, 2) == 1

    def slice_of(rows, a, b):
        return jnp.concatenate([jnp.where(odd, a, b)] + rows + [jnp.where(odd, b, a)], axis=1)

    column = lax.broadcasted_iota(jnp.int32, (128, 768), 1) % 64

    def taps(n, x):
        for ow in range(3):
            if ow == 0:
                moved = jnp.where(column > 0, shifted(x, -1), jnp.zeros_like(x))
            elif ow == 1:
                moved = x
            else:
                moved = jnp.where(column < 63, shifted(x, 1), jnp.zeros_like(x))
            for oh in range(3):
                tap = oh * 3 + ow
                s_buf[n, 128 * tap : 128 * tap + 128, :] = shifted(moved, (oh - 1) * 64)

    for z in range(2):
        rows = slice(128 * z, 128 * z + 128)
        taps(z, slice_of([own_ref[z]], a_ref[rows], b_ref[rows]))
    taps(2, slice_of([side_ref[128 * t : 128 * t + 128] for t in range(4)], da_ref[...], db_ref[...]))
    y0 = dot_nn(w3_ref[64:192, :], s_buf[0])
    y1 = dot_nn(w3_ref[0:128, :], s_buf[1])
    back[0] = y0[:64] + y1[:64]
    back[1] = y0[64:] + y1[64:]
    kd = pl.multiple_of(128 * dep, 128)
    back[1 - dep] += dot_nn(w3_ref[pl.ds(kd, 64), :], s_buf[2])
    lane = lax.broadcasted_iota(jnp.int32, (64, 768), 1)
    keep = ((lane >= 128) | (hgt > 0)) & ((lane < 640) | (hgt < 7))
    for d in range(2):
        back_out[d] = jnp.where(keep, scale * back[d], 0.0).astype(BF16)
    r0 = dot_nt(pooled_ref[...], s_buf[0, :, 128:640])
    r1 = dot_nt(pooled_ref[...], s_buf[1, :, 128:640])
    parts[0] = r0[64:]
    parts[1] = r0[:64] + r1[64:]
    parts[2] = r1[:64]
    d = pl.multiple_of(64 * (1 - dep), 64)
    parts[2 * (1 - dep)] += dot_nt(pooled_ref[pl.ds(d, 64), :], s_buf[2, :, 128:640])
    for od in range(3):
        for oh in range(3):
            for ow in range(3):
                k = (2 - od) * 9 + (2 - oh) * 3 + (2 - ow)
                tap = oh * 3 + ow
                t3[pl.ds(k, 64, stride=27), :] = parts[od, :, 128 * tap : 128 * tap + 128]
    t3[1728:] = jnp.zeros((64, 128), F32)
    for b in range(14):
        grad_out[b] = jnp.transpose(t3[128 * b : 128 * b + 128, :])


def cotangent(back_ref, a_ref, b_ref, pre_rows, upper, z_out):
    odd = lax.rem(lax.axis_index("height"), 2) == 1
    row = lax.broadcasted_iota(jnp.int32, (128, 256), 0)
    col = lax.broadcasted_iota(jnp.int32, (128, 256), 1)
    spread = jnp.where(row == col // 2, 0.125, 0.0).astype(BF16)
    for t in range(6):
        x = back_ref[:, :, 128 * t : 128 * t + 128].reshape(128, 128)
        y = dot_nn(x, spread).reshape(2, 64, 256)
        if t > 0:
            upper[:, 2 * t - 1] = y[:, :, :128]
        if t < 5:
            upper[:, 2 * t] = y[:, :, 128:]
    for f in range(4):
        place = slice(256 + 64 * f, 320 + 64 * f)
        rows = pre_rows(f)
        for h in range(18):
            if h == 0:
                pre = jnp.where(odd, a_ref[place], b_ref[place])
            elif h == 17:
                pre = jnp.where(odd, b_ref[place], a_ref[place])
            else:
                pre = rows[h - 1]
            up = upper[f // 2, (h + 1) // 2]
            z_out[f, h] = jnp.where(pre.astype(F32) > 0, up, SLOPE * up).astype(BF16)


def fine(back_ref, pre_ref, a_ref, b_ref, act_ref, side_ref, three_ref, m_ref,
         parts_out, z_out, upper, near, parts, t2, stage):
    dep = lax.axis_index("depth")
    cotangent(back_ref, a_ref, b_ref, lambda f: pre_ref.at[f], upper, z_out)
    layer = side_ref[512:].astype(F32).reshape(16, 32, 128)
    for ow, value in enumerate(shifts(layer)):
        near[:, 32 * ow : 32 * ow + 32, :] = value.astype(BF16)

    def correlate(z, lhs):
        total = None
        for h in range(4):
            left = jnp.concatenate([lhs(h + 4 * i) for i in range(4)], axis=1)
            right = jnp.concatenate(
                [z_out[z, h + 4 * i : h + 4 * i + 3].reshape(192, 128) for i in range(4)], axis=1
            )
            r = dot_nt(left, right)
            total = r if total is None else total + r
        return total

    sums = [None, None, None]
    for z in range(4):
        first, final = max(0, z - 1), min(3, z + 1)
        total = correlate(z, lambda h: act_ref[h, 96 * first : 96 * (final + 1), :])
        for d in range(first, final + 1):
            part = total[96 * (d - first) : 96 * (d - first + 1)]
            od = z - d + 1
            sums[od] = part if sums[od] is None else sums[od] + part
    for od in range(3):
        parts[od] = sums[od]
    parts[2 * dep] += correlate(3 * (1 - dep), lambda h: near[h])
    for od in range(3):
        for oh in range(3):
            for ow in range(3):
                k = (2 - od) * 9 + (2 - oh) * 3 + (2 - ow)
                t2[pl.ds(k, 32, stride=27), :] = parts[od, 32 * ow : 32 * ow + 32, 64 * oh : 64 * oh + 64]
    t2[864:] = jnp.zeros((80, 64), F32)
    tail = lax.broadcasted_iota(jnp.int32, (64, 128), 1) < 48
    for half in range(2):
        for b in range(4):
            start = 432 * half + 128 * b
            block = jnp.transpose(t2[start : start + 128, :])
            if b == 3:
                block = jnp.where(tail, block, 0.0)
            stage[pl.ds(half, 64, stride=2), b, :] = block
    for b in range(14):
        stage[:, 4 + b, :] = three_ref[b]
    stage[:, 18:, :] = jnp.broadcast_to(m_ref[:6][None], (128, 6, 128))
    parts_out[...] = stage[...].astype(BF16)


def into(back_ref, pre_ref, a_ref, b_ref, w2_ref, rows, ship, z_ref, upper):
    dep = lax.axis_index("depth")
    cotangent(back_ref, a_ref, b_ref, lambda f: jnp.swapaxes(pre_ref[:, f].astype(F32), 0, 1), upper, z_ref)
    lane = lax.broadcasted_iota(jnp.int32, (256, 128), 1)
    for jp in range(4):
        acc = [None] * 6
        for z in range(4):
            blocks = []
            for j in (2 * jp, 2 * jp + 1):
                x = z_ref[z, 2 * j : 2 * j + 4].reshape(256, 128)
                left = jnp.where(lane > 0, shifted(x, -1), jnp.zeros_like(x))
                right = jnp.where(lane < 127, shifted(x, 1), jnp.zeros_like(x))
                blocks.append(jnp.concatenate([left, x, right], axis=0))
            y = dot_nn(w2_ref[...], jnp.concatenate(blocks, axis=1))
            for kd in range(3):
                d = z + kd
                part = y[64 * kd : 64 * kd + 64]
                acc[d] = part if acc[d] is None else acc[d] + part
        for j in range(2):
            for r in range(2):
                h = 4 * jp + 2 * j + r
                block = (slice(32 * r, 32 * r + 32), slice(128 * j, 128 * j + 128))
                ship[h] = jnp.where(dep == 0, acc[5][block], acc[0][block]).astype(BF16)
                for d in range(4):
                    rows[d, h] = acc[d + 1][block]


def finish(scale, rows_ref, ship_ref, out_ref):
    dep = lax.axis_index("depth")
    for d in range(4):
        rows = rows_ref[d]
        if d in (0, 3):
            rows = rows + jnp.where(dep == (0 if d == 3 else 1), ship_ref[...].astype(F32), 0.0)
        out_ref[:, d] = (scale * jnp.swapaxes(rows, 0, 1)).astype(BF16)


def reduce(scale_two, scale_three, parts_ref, m_ref, send_out, own_out, rows):
    total = jnp.sum(parts_ref[:, :18, :].astype(F32), axis=0)
    row = lax.broadcasted_iota(jnp.int32, (18, 128), 0)
    total = total * jnp.where(row < 4, scale_two, scale_three)
    own_out[...] = total
    rows[:18] = total
    rows[18:30] = m_ref[6:18]
    rows[30:] = jnp.zeros((2, 128), F32)
    send_out[...] = jnp.broadcast_to(rows[...].astype(BF16)[None], (128, 32, 128))


def update(full_ref, first_ref, own_ref, w2_ref, w3_ref, m2_ref, m3_ref, w2_out, w3_out, m2_out, m3_out, stage):
    w2 = w2_ref[...]
    w3 = w3_ref[...]
    grad = full_ref[:, :18, :].astype(F32)
    square = jnp.sum(grad * grad, axis=0)
    row = lax.broadcasted_iota(jnp.int32, (18, 128), 0)
    norm_two = jnp.sqrt(jnp.sum(jnp.where(row < 4, square, 0.0), keepdims=True))
    norm_three = jnp.sqrt(jnp.sum(jnp.where(row < 4, 0.0, square), keepdims=True))
    rate_two = LEARN * (TRUST * jnp.sqrt(jnp.sum(w2 * w2, keepdims=True)) / (norm_two + EPSILON))
    rate_three = LEARN * (TRUST * jnp.sqrt(jnp.sum(w3 * w3, keepdims=True)) / (norm_three + EPSILON))
    rate = jnp.where(row < 4, rate_two, rate_three)
    stage[:, :6, :] = MOMENTUM * first_ref[:, 18:, :].astype(F32)
    stage[:, 6:, :] = MOMENTUM * full_ref[:, 18:30, :].astype(F32)
    stage[...] += rate[None] * grad
    for b in range(13):
        rows = slice(128 * b, 128 * b + 128)
        w3_out[rows] = w3[rows] - jnp.transpose(stage[:, 4 + b, :])
    w3_out[1664:] = w3[1664:] - jnp.transpose(stage[:, 17, :])[:64]
    halves = []
    for half in range(2):
        blocks = [stage[pl.ds(half, 64, stride=2), b, :] for b in range(4)]
        halves.append(jnp.concatenate(blocks, axis=1)[:, :432])
    w2_out[...] = w2 - jnp.concatenate(halves, axis=1)
    own = rate * own_ref[...]
    for b in range(3):
        m2_out[pl.ds(128 * b, 128)] = MOMENTUM * m2_ref[pl.ds(128 * b, 128)] + own[b]
    m2_out[pl.ds(384, 48)] = MOMENTUM * m2_ref[pl.ds(384, 48)] + own[3, :48]
    for b in range(13):
        m3_out[pl.ds(128 * b, 128)] = MOMENTUM * m3_ref[pl.ds(128 * b, 128)] + own[4 + b]
    m3_out[pl.ds(1664, 64)] = MOMENTUM * m3_ref[pl.ds(1664, 64)] + own[17, :64]


def local(act_one, pre_two, cot_three, weight_two, weight_three, moment_two, moment_three):
    scale_two = (act_one.shape[1] * 27) ** (-0.5)
    scale_three = (pre_two.shape[1] * 27) ** (-0.5)
    volumes = lax.axis_size("dp")
    pre, act, cot = pre_two[0], act_one[0], cot_three[0]

    cot_rows, send_side, send_a, send_b, send_da, send_db = call(
        arrange,
        [((2, 128, 512), BF16), ((1024, 128), BF16), ((512, 128), BF16),
         ((512, 128), BF16), ((128, 128), BF16), ((128, 128), BF16)],
        [pltpu.VMEM((128, 2, 512), BF16), pltpu.VMEM((64, 4, 16, 128), BF16), pltpu.VMEM((32, 16, 128), BF16),
         pltpu.SemaphoreType.DMA((3,))],
        moved=4_000_000, far=3, limit=62,
    )(cot, pre, act)
    tall = lax.axis_size("height")
    swap = [(0, 1), (1, 0)]
    pairs_a = [(h, h ^ 1) for h in range(tall)]
    pairs_b = [(h, ((h + 1) ^ 1) - 1) for h in range(1, tall - 1)]
    cross_a, cross_b = (
        [(d * tall + i, (1 - d) * tall + j) for d in range(2) for i, j in pairs] for pairs in (pairs_a, pairs_b)
    )
    side = lax.ppermute(send_side, "depth", swap)
    got_a = lax.ppermute(send_a, "height", pairs_a)
    got_b = lax.ppermute(send_b, "height", pairs_b)
    got_da = lax.ppermute(send_da, ("depth", "height"), cross_a)
    got_db = lax.ppermute(send_db, ("depth", "height"), cross_b)

    pre_rows, pooled, acts, wide_two, wide_three, moments = call(
        prepare,
        [((4, 16, 64, 128), BF16), ((128, 512), BF16), ((16, 384, 128), BF16), ((192, 768), BF16), ((192, 1152), BF16), ((24, 128), F32)],
        [pltpu.VMEM((864, 64), F32)],
        flops=100_000_000, moved=8_000_000,
    )(pre, act, weight_two, weight_three.T, moment_two, moment_three)

    back, part_three = call(
        lambda *refs: coarse(scale_three, *refs),
        [((2, 64, 768), BF16), ((14, 128, 128), F32)],
        [pltpu.VMEM((3, 1152, 768), BF16), pltpu.VMEM((2, 64, 768), F32), pltpu.VMEM((3, 64, 1152), F32),
         pltpu.VMEM((1792, 128), F32)],
        flops=2_000_000_000, moved=4_000_000,
    )(cot_rows, side, got_a, got_b, got_da, got_db, wide_three, pooled)

    parts, = call(
        fine,
        [((128, 24, 128), BF16)],
        [pltpu.VMEM((4, 18, 64, 128), BF16), pltpu.VMEM((2, 10, 64, 128), F32), pltpu.VMEM((16, 96, 128), BF16), pltpu.VMEM((3, 96, 192), F32),
         pltpu.VMEM((944, 64), F32), pltpu.VMEM((128, 24, 128), F32)],
        flops=2_000_000_000, moved=6_000_000,
    )(back, pre_rows, got_a, got_b, acts, side, part_three, moments)

    parts = lax.all_to_all(parts, AXES, 0, 0, tiled=True)
    into_rows, ship = call(
        into,
        [((4, 16, 32, 128), F32), ((16, 32, 128), BF16)],
        [pltpu.VMEM((4, 18, 64, 128), BF16), pltpu.VMEM((2, 10, 64, 128), F32)],
        flops=4_000_000_000, moved=6_000_000,
    )(back, pre, got_a, got_b, wide_two)
    ship = lax.ppermute(ship, "depth", swap)
    parts, into_rows, ship = lax.optimization_barrier((parts, into_rows, ship))
    grad_input, = call(
        lambda *refs: finish(scale_two, *refs),
        [((32, 4, 16, 128), BF16)],
        moved=2_000_000,
    )(into_rows, ship)

    send, own = call(
        lambda *refs: reduce(scale_two / volumes, scale_three / volumes, *refs),
        [((128, 32, 128), BF16), ((18, 128), F32)],
        [pltpu.VMEM((32, 128), F32)],
        moved=2_000_000,
    )(parts, moments)
    own, w2, w3 = lax.optimization_barrier((own, weight_two, weight_three))
    full = lax.all_to_all(send, AXES, 0, 0, tiled=True)
    new_weight_two, new_weight_three, new_moment_two, new_moment_three = call(
        update,
        [(weight_two.shape, F32), (weight_three.shape[::-1], F32), (moment_two.shape, F32), (moment_three.shape, F32)],
        [pltpu.VMEM((128, 18, 128), F32)],
        moved=4_000_000,
    )(full, parts, own, w2, w3.T, moment_two, moment_three)
    return (grad_input[None], new_weight_two, new_weight_three.T, new_moment_two, new_moment_three)


def solution(mesh):
    in_specs = (
        P("dp", None, "depth", "height", None),
        P("dp", None, "depth", "height", None),
        P("dp", None, "depth", "height"),
        P(),
        P(),
        P(AXES),
        P(AXES),
    )
    out_specs = (
        P("dp", None, "depth", "height", None),
        P(),
        P(),
        P(AXES),
        P(AXES),
    )
    return jax.shard_map(local, mesh=mesh, in_specs=in_specs, out_specs=out_specs, check_vma=False)
```

```python
import jax
import jax.numpy as jnp
from jax import lax
from jax.experimental import pallas as pl
from jax.experimental.pallas import tpu as pltpu
from jax.sharding import PartitionSpec as P

SLOPE = 0.3
LEARN = 4.0
TRUST = 0.05
MOMENTUM = 0.9
EPSILON = 1e-06
AXES = ("dp", "depth", "height")
F32 = jnp.float32
BF16 = jnp.bfloat16


def call(body, outs, scratch=(), flops=0, moved=0, far=(), far_out=()):
    def run(*args):
        return pl.pallas_call(
            body,
            out_shape=[
                pltpu.HBM(shape, dtype) if i in far_out else jax.ShapeDtypeStruct(shape, dtype)
                for i, (shape, dtype) in enumerate(outs)
            ],
            in_specs=[pl.BlockSpec(memory_space=pltpu.HBM if i in far else pltpu.VMEM) for i in range(len(args))],
            out_specs=[pl.BlockSpec(memory_space=pltpu.HBM if i in far_out else pltpu.VMEM) for i in range(len(outs))],
            scratch_shapes=list(scratch),
            compiler_params=pltpu.CompilerParams(vmem_limit_bytes=20 * 1024 * 1024),
            cost_estimate=pl.CostEstimate(flops=flops, bytes_accessed=moved, transcendentals=0),
        )(*(pltpu.with_memory_space_constraint(x, pltpu.HBM) if i in far else x for i, x in enumerate(args)))

    return run


def dot_nt(a, b):
    return lax.dot_general(a, b, (((1,), (1,)), ((), ())), preferred_element_type=F32)


def dot_nn(a, b):
    return lax.dot_general(a, b, (((1,), (0,)), ((), ())), preferred_element_type=F32)


def shifted(x, amount):
    size = x.shape[-1]
    amount = amount % size
    if amount == 0:
        return x
    return jnp.concatenate([x[..., amount:], x[..., :amount]], axis=-1)


def arrange(cot_far, pre_far, act_far, cot_out, side_out, a_out, b_out, diag_a_out, diag_b_out,
            cot_ref, pre_ref, act_ref, sems):
    dep = lax.axis_index("depth")
    loads = [pltpu.make_async_copy(cot_far, cot_ref, sems.at[0])]
    loads += [pltpu.make_async_copy(act_far.at[:, 3 * (1 - dep)], act_ref, sems.at[1])]
    loads += [pltpu.make_async_copy(pre_far.at[:, d], pre_ref.at[:, d], sems.at[2 + d]) for d in range(4)]
    for load in loads:
        load.start()
    loads[0].wait()
    odd = lax.rem(lax.axis_index("height"), 2) == 1
    cots = [cot_ref[:, d, :] for d in range(2)]
    for d in range(2):
        cot_out[d] = cots[d]
        top, bottom = cots[d][:, :128], cots[d][:, 384:]
        a_out[128 * d : 128 * d + 128] = jnp.where(odd, top, bottom)
        b_out[128 * d : 128 * d + 128] = jnp.where(odd, bottom, top)
    near = jnp.where(dep == 0, cots[1], cots[0])
    diag_a_out[:128] = jnp.where(odd, near[:, :128], near[:, 384:])
    diag_a_out[128:] = jnp.zeros((384, 128), BF16)
    diag_b_out[...] = jnp.where(odd, near[:, 384:], near[:, :128])
    for t in range(4):
        side_out[128 * t : 128 * t + 128] = near[:, 128 * t : 128 * t + 128]
    loads[1].wait()
    layer = jnp.swapaxes(act_ref[...].astype(F32), 0, 1).astype(BF16)
    side_out[512:] = layer.reshape(512, 128)
    for d in range(4):
        loads[2 + d].wait()
        first, final = pre_ref[:, d, 0, :], pre_ref[:, d, 15, :]
        place = slice(256 + 64 * d, 320 + 64 * d)
        a_out[place] = jnp.where(odd, first, final)
        b_out[place] = jnp.where(odd, final, first)


def shifts(rows):
    lane = lax.broadcasted_iota(jnp.int32, rows.shape, rows.ndim - 1)
    before = jnp.where(lane < 127, shifted(rows, 1), 0.0)
    after = jnp.where(lane > 0, shifted(rows, -1), 0.0)
    return before, rows, after


def prepare(pre_ref, act_ref, w2_ref, w3_far, m2_ref, m3_ref, pre_out, pooled_out, act_out, w2_out, w3_out, m_out,
            t2, w3_ref, sems):
    loads = []
    for i in range(6):
        rows = slice(288 * i, 288 * i + 288)
        loads.append(pltpu.make_async_copy(w3_far.at[rows], w3_ref.at[rows], sems.at[i]))
        loads[i].start()
    for d in range(4):
        pre_out[d] = jnp.swapaxes(pre_ref[:, d].astype(F32), 0, 1).astype(BF16)
    m_out[...] = jnp.zeros((24, 128), F32)
    for b in range(3):
        m_out[b, :] = m2_ref[pl.ds(128 * b, 128)]
    m_out[3, :48] = m2_ref[pl.ds(384, 48)]
    for b in range(13):
        m_out[4 + b, :] = m3_ref[pl.ds(128 * b, 128)]
    m_out[17, :64] = m3_ref[pl.ds(1664, 64)]
    row = lax.broadcasted_iota(jnp.int32, (256, 128), 0)
    col = lax.broadcasted_iota(jnp.int32, (256, 128), 1)
    pool = jnp.where(row // 2 == col, 0.125, 0.0).astype(BF16)
    for d in range(2):
        for t in range(4):
            halves = []
            for half in range(2):
                total = None
                for i in range(2):
                    for j in range(2):
                        x = pre_out[2 * d + i, 4 * t + 2 * half + j].astype(F32)
                        x = jnp.where(x > 0, x, SLOPE * x)
                        total = x if total is None else total + x
                halves.append(total)
            total = jnp.concatenate(halves, axis=1)
            high = total.astype(BF16)
            low = (total - high.astype(F32)).astype(BF16)
            mean = dot_nn(high, pool) + dot_nn(low, pool)
            pooled_out[64 * d : 64 * d + 64, 128 * t : 128 * t + 128] = mean.astype(BF16)
    for d in range(4):
        rows = jnp.swapaxes(act_ref[:, d].astype(F32), 0, 1)
        for ow, value in enumerate(shifts(rows)):
            start = 96 * d + 32 * ow
            act_out[:, start : start + 32, :] = value.astype(BF16)
    t2[...] = jnp.transpose(w2_ref[...])
    for load in loads:
        load.wait()
    for kd in range(3):
        for oh in range(3):
            for ow in range(3):
                k = kd * 9 + (2 - oh) * 3 + (2 - ow)
                block = w3_ref[pl.ds(k, 64, stride=27), :].astype(BF16)
                tap = oh * 3 + ow
                w3_out[64 * kd : 64 * kd + 64, 128 * tap : 128 * tap + 128] = block
    zero = jnp.zeros((32, 64), F32)
    for kd in range(3):
        for ow in range(3):
            taps = []
            for oh in range(3):
                k = kd * 9 + (2 - oh) * 3 + (2 - ow)
                taps.append(t2[pl.ds(k, 32, stride=27), :])
            for r in range(2):
                blocks = taps + [zero] if r == 0 else [zero] + taps
                start = 64 * kd + 32 * r
                w2_out[start : start + 32, 256 * ow : 256 * ow + 256] = jnp.concatenate(blocks, axis=1).astype(BF16)


def coarse(scale, own_ref, side_ref, a_ref, da_ref, b_ref, db_ref, w3_ref, pooled_ref,
           back_out, grad_out, s_buf, back, parts, t3):
    dep = lax.axis_index("depth")
    hgt = lax.axis_index("height")
    odd = lax.rem(hgt, 2) == 1

    def slice_of(rows, a, b):
        return jnp.concatenate([jnp.where(odd, a, b)] + rows + [jnp.where(odd, b, a)], axis=1)

    column = lax.broadcasted_iota(jnp.int32, (128, 768), 1) % 64

    def taps(n, x):
        for ow in range(3):
            if ow == 0:
                moved = jnp.where(column > 0, shifted(x, -1), jnp.zeros_like(x))
            elif ow == 1:
                moved = x
            else:
                moved = jnp.where(column < 63, shifted(x, 1), jnp.zeros_like(x))
            for oh in range(3):
                tap = oh * 3 + ow
                s_buf[n, 128 * tap : 128 * tap + 128, :] = shifted(moved, (oh - 1) * 64)

    for z in range(2):
        rows = slice(128 * z, 128 * z + 128)
        taps(z, slice_of([own_ref[z]], a_ref[rows], b_ref[rows]))
    taps(2, slice_of([side_ref[128 * t : 128 * t + 128] for t in range(4)], da_ref[:128], db_ref[...]))
    y0 = dot_nn(w3_ref[64:192, :], s_buf[0])
    y1 = dot_nn(w3_ref[0:128, :], s_buf[1])
    back[0] = y0[:64] + y1[:64]
    back[1] = y0[64:] + y1[64:]
    kd = pl.multiple_of(128 * dep, 128)
    back[1 - dep] += dot_nn(w3_ref[pl.ds(kd, 64), :], s_buf[2])
    lane = lax.broadcasted_iota(jnp.int32, (64, 768), 1)
    keep = ((lane >= 128) | (hgt > 0)) & ((lane < 640) | (hgt < 7))
    for d in range(2):
        back_out[d] = jnp.where(keep, scale * back[d], 0.0).astype(BF16)
    r0 = dot_nt(pooled_ref[...], s_buf[0, :, 128:640])
    r1 = dot_nt(pooled_ref[...], s_buf[1, :, 128:640])
    parts[0] = r0[64:]
    parts[1] = r0[:64] + r1[64:]
    parts[2] = r1[:64]
    d = pl.multiple_of(64 * (1 - dep), 64)
    parts[2 * (1 - dep)] += dot_nt(pooled_ref[pl.ds(d, 64), :], s_buf[2, :, 128:640])
    for od in range(3):
        for oh in range(3):
            for ow in range(3):
                k = (2 - od) * 9 + (2 - oh) * 3 + (2 - ow)
                tap = oh * 3 + ow
                t3[pl.ds(k, 64, stride=27), :] = parts[od, :, 128 * tap : 128 * tap + 128]
    t3[1728:] = jnp.zeros((64, 128), F32)
    for b in range(14):
        grad_out[b] = jnp.transpose(t3[128 * b : 128 * b + 128, :])


def cotangent(back_ref, a_ref, b_ref, pre_rows, upper, z_out):
    odd = lax.rem(lax.axis_index("height"), 2) == 1
    row = lax.broadcasted_iota(jnp.int32, (128, 256), 0)
    col = lax.broadcasted_iota(jnp.int32, (128, 256), 1)
    spread = jnp.where(row == col // 2, 0.125, 0.0).astype(BF16)
    for t in range(6):
        x = back_ref[:, :, 128 * t : 128 * t + 128].reshape(128, 128)
        y = dot_nn(x, spread).reshape(2, 64, 256)
        if t > 0:
            upper[:, 2 * t - 1] = y[:, :, :128]
        if t < 5:
            upper[:, 2 * t] = y[:, :, 128:]
    for f in range(4):
        place = slice(256 + 64 * f, 320 + 64 * f)
        rows = pre_rows(f)
        for h in range(18):
            if h == 0:
                pre = jnp.where(odd, a_ref[place], b_ref[place])
            elif h == 17:
                pre = jnp.where(odd, b_ref[place], a_ref[place])
            else:
                pre = rows[h - 1]
            up = upper[f // 2, (h + 1) // 2]
            z_out[f, h] = jnp.where(pre.astype(F32) > 0, up, SLOPE * up).astype(BF16)


def fine(back_ref, pre_ref, a_ref, b_ref, act_ref, side_ref, three_ref,
         mine_out, theirs_out, z_out, upper, near, parts, t2, stage):
    dep = lax.axis_index("depth")
    cotangent(back_ref, a_ref, b_ref, lambda f: pre_ref.at[f], upper, z_out)
    layer = side_ref[512:].astype(F32).reshape(16, 32, 128)
    for ow, value in enumerate(shifts(layer)):
        near[:, 32 * ow : 32 * ow + 32, :] = value.astype(BF16)

    def correlate(z, lhs):
        total = None
        for h in range(4):
            left = jnp.concatenate([lhs(h + 4 * i) for i in range(4)], axis=1)
            right = jnp.concatenate(
                [z_out[z, h + 4 * i : h + 4 * i + 3].reshape(192, 128) for i in range(4)], axis=1
            )
            r = dot_nt(left, right)
            total = r if total is None else total + r
        return total

    sums = [None, None, None]
    for z in range(4):
        first, final = max(0, z - 1), min(3, z + 1)
        total = correlate(z, lambda h: act_ref[h, 96 * first : 96 * (final + 1), :])
        for d in range(first, final + 1):
            part = total[96 * (d - first) : 96 * (d - first + 1)]
            od = z - d + 1
            sums[od] = part if sums[od] is None else sums[od] + part
    for od in range(3):
        parts[od] = sums[od]
    parts[2 * dep] += correlate(3 * (1 - dep), lambda h: near[h])
    for od in range(3):
        for oh in range(3):
            for ow in range(3):
                k = (2 - od) * 9 + (2 - oh) * 3 + (2 - ow)
                t2[pl.ds(k, 32, stride=27), :] = parts[od, 32 * ow : 32 * ow + 32, 64 * oh : 64 * oh + 64]
    t2[864:] = jnp.zeros((80, 64), F32)
    tail = lax.broadcasted_iota(jnp.int32, (64, 128), 1) < 48
    for half in range(2):
        for b in range(4):
            start = 432 * half + 128 * b
            block = jnp.transpose(t2[start : start + 128, :])
            if b == 3:
                block = jnp.where(tail, block, 0.0)
            stage[pl.ds(half, 64, stride=2), b, :] = block
    for b in range(14):
        stage[:, 4 + b, :] = three_ref[b]
    stage[:, 18:, :] = jnp.zeros((128, 6, 128), F32)
    core = lax.rem(lax.axis_index("dp"), 2)
    for x in range(4):
        place = slice(16 * x, 16 * x + 16)
        mine_out[place] = stage[pl.ds(32 * x + 16 * core, 16)]
        theirs_out[place] = stage[pl.ds(32 * x + 16 * (1 - core), 16)].astype(BF16)


def combine(mine_ref, got_ref, parts_far, packed, sems):
    leave = []
    for i in range(4):
        piece = slice(16 * i, 16 * i + 16)
        packed[piece] = (mine_ref[piece] + got_ref[piece].astype(F32)).astype(BF16)
        leave.append(pltpu.make_async_copy(packed.at[piece], parts_far.at[piece], sems.at[i]))
        leave[i].start()
    for copy in leave:
        copy.wait()


def into(back_ref, pre_ref, a_ref, b_ref, w2_ref, rows_far, ship, z_ref, upper, rows, sems):
    dep = lax.axis_index("depth")
    cotangent(back_ref, a_ref, b_ref, lambda f: jnp.swapaxes(pre_ref[:, f].astype(F32), 0, 1), upper, z_ref)
    lane = lax.broadcasted_iota(jnp.int32, (256, 128), 1)
    leave = []
    for jp in range(4):
        acc = [None] * 6
        for z in range(4):
            blocks = []
            for j in (2 * jp, 2 * jp + 1):
                x = z_ref[z, 2 * j : 2 * j + 4].reshape(256, 128)
                left = jnp.where(lane > 0, shifted(x, -1), jnp.zeros_like(x))
                right = jnp.where(lane < 127, shifted(x, 1), jnp.zeros_like(x))
                blocks.append(jnp.concatenate([left, x, right], axis=0))
            y = dot_nn(w2_ref[...], jnp.concatenate(blocks, axis=1))
            for kd in range(3):
                d = z + kd
                part = y[64 * kd : 64 * kd + 64]
                acc[d] = part if acc[d] is None else acc[d] + part
        for j in range(2):
            for r in range(2):
                h = 4 * jp + 2 * j + r
                block = (slice(32 * r, 32 * r + 32), slice(128 * j, 128 * j + 128))
                ship[h] = jnp.where(dep == 0, acc[5][block], acc[0][block]).astype(BF16)
                for d in range(4):
                    rows[d, h] = acc[d + 1][block]
        piece = (slice(None), slice(4 * jp, 4 * jp + 4))
        leave.append(pltpu.make_async_copy(rows.at[piece], rows_far.at[piece], sems.at[jp]))
        leave[jp].start()
    for copy in leave:
        copy.wait()


def finish(scale, rows_ref, ship_ref, out_ref):
    dep = lax.axis_index("depth")
    for d in range(4):
        rows = rows_ref[d]
        if d in (0, 3):
            rows = rows + jnp.where(dep == (0 if d == 3 else 1), ship_ref[...].astype(F32), 0.0)
        out_ref[:, d] = (scale * jnp.swapaxes(rows, 0, 1)).astype(BF16)


def reduce(scale_two, scale_three, parts_ref, m_ref, send_far, own_out, rows, block, sems):
    total = jnp.sum(parts_ref[:, :18, :].astype(F32), axis=0)
    row = lax.broadcasted_iota(jnp.int32, (18, 128), 0)
    total = total * jnp.where(row < 4, scale_two, scale_three)
    own_out[...] = total
    rows[:18] = total
    rows[18:36] = m_ref[:18]
    rows[36:] = jnp.zeros((4, 128), F32)
    block[...] = jnp.broadcast_to(rows[...].astype(BF16)[None], (16, 40, 128))
    leave = [pltpu.make_async_copy(block, send_far.at[16 * i : 16 * i + 16], sems.at[i]) for i in range(4)]
    for copy in leave:
        copy.start()
    for copy in leave:
        copy.wait()


def update(full_ref, other_ref, own_ref, w2_ref, w3_ref, m2_ref, m3_ref, w2_out, w3_out, m2_out, m3_out, stage):
    w2 = w2_ref[...]
    w3 = w3_ref[...]
    both = full_ref, other_ref
    grads = [ref[:, :18, :].astype(F32) for ref in both]
    square = sum(jnp.sum(grad * grad, axis=0) for grad in grads)
    row = lax.broadcasted_iota(jnp.int32, (18, 128), 0)
    norm_two = jnp.sqrt(jnp.sum(jnp.where(row < 4, square, 0.0), keepdims=True))
    norm_three = jnp.sqrt(jnp.sum(jnp.where(row < 4, 0.0, square), keepdims=True))
    rate_two = LEARN * (TRUST * jnp.sqrt(jnp.sum(w2 * w2, keepdims=True)) / (norm_two + EPSILON))
    rate_three = LEARN * (TRUST * jnp.sqrt(jnp.sum(w3 * w3, keepdims=True)) / (norm_three + EPSILON))
    rate = jnp.where(row < 4, rate_two, rate_three)
    core = lax.rem(lax.axis_index("dp"), 2)
    for ref, grad, side in zip(both, grads, (core, 1 - core)):
        moved = MOMENTUM * ref[:, 18:36, :].astype(F32) + rate[None] * grad
        for x in range(4):
            stage[pl.ds(32 * x + 16 * side, 16)] = moved[16 * x : 16 * x + 16]
    for b in range(14):
        rows = slice(128 * b, min(128 * b + 128, 1728))
        w3_out[rows] = w3[rows] - jnp.transpose(stage[:, 4 + b, :])[: rows.stop - rows.start]
    halves = []
    for half in range(2):
        blocks = [stage[pl.ds(half, 64, stride=2), b, :] for b in range(4)]
        halves.append(jnp.concatenate(blocks, axis=1)[:, :432])
    w2_out[...] = w2 - jnp.concatenate(halves, axis=1)
    own = rate * own_ref[...]
    for b in range(3):
        m2_out[pl.ds(128 * b, 128)] = MOMENTUM * m2_ref[pl.ds(128 * b, 128)] + own[b]
    m2_out[pl.ds(384, 48)] = MOMENTUM * m2_ref[pl.ds(384, 48)] + own[3, :48]
    for b in range(13):
        m3_out[pl.ds(128 * b, 128)] = MOMENTUM * m3_ref[pl.ds(128 * b, 128)] + own[4 + b]
    m3_out[pl.ds(1664, 64)] = MOMENTUM * m3_ref[pl.ds(1664, 64)] + own[17, :64]


def local(act_one, pre_two, cot_three, weight_two, weight_three, moment_two, moment_three):
    scale_two = (act_one.shape[1] * 27) ** (-0.5)
    scale_three = (pre_two.shape[1] * 27) ** (-0.5)
    volumes = lax.axis_size("dp")
    pre, act, cot = pre_two[0], act_one[0], cot_three[0]

    cot_rows, send_side, send_a, send_b, send_da, send_db = call(
        arrange,
        [((2, 128, 512), BF16), ((1024, 128), BF16), ((512, 128), BF16),
         ((512, 128), BF16), ((512, 128), BF16), ((128, 128), BF16)],
        [pltpu.VMEM((128, 2, 512), BF16), pltpu.VMEM((64, 4, 16, 128), BF16), pltpu.VMEM((32, 16, 128), BF16),
         pltpu.SemaphoreType.DMA((6,))],
        moved=4_000_000, far=(0, 1, 2),
    )(cot, pre, act)
    tall = lax.axis_size("height")
    swap = [(0, 1), (1, 0)]
    pairs_a = [(h, h ^ 1) for h in range(tall)]
    pairs_b = [(h, ((h + 1) ^ 1) - 1) for h in range(1, tall - 1)]
    cross_a, cross_b = (
        [(d * tall + i, (1 - d) * tall + j) for d in range(2) for i, j in pairs] for pairs in (pairs_a, pairs_b)
    )
    side = lax.ppermute(send_side, "depth", swap)
    got_a = lax.ppermute(send_a, "height", pairs_a)
    got_da = lax.ppermute(send_da, ("depth", "height"), cross_a)
    got_b = lax.ppermute(send_b, "height", pairs_b)
    got_db = lax.ppermute(send_db, ("depth", "height"), cross_b)

    pre_rows, pooled, acts, wide_two, wide_three, moments = call(
        prepare,
        [((4, 16, 64, 128), BF16), ((128, 512), BF16), ((16, 384, 128), BF16), ((192, 768), BF16), ((192, 1152), BF16), ((24, 128), F32)],
        [pltpu.VMEM((864, 64), F32), pltpu.VMEM((1728, 128), F32), pltpu.SemaphoreType.DMA((6,))],
        flops=100_000_000, moved=8_000_000, far=(3,),
    )(pre, act, weight_two, weight_three.T, moment_two, moment_three)

    back, part_three = call(
        lambda *refs: coarse(scale_three, *refs),
        [((2, 64, 768), BF16), ((14, 128, 128), F32)],
        [pltpu.VMEM((3, 1152, 768), BF16), pltpu.VMEM((2, 64, 768), F32), pltpu.VMEM((3, 64, 1152), F32),
         pltpu.VMEM((1792, 128), F32)],
        flops=2_000_000_000, moved=4_000_000,
    )(cot_rows, side, got_a, got_da, got_b, got_db, wide_three, pooled)

    mine, theirs = call(
        fine,
        [((64, 24, 128), F32), ((64, 24, 128), BF16)],
        [pltpu.VMEM((4, 18, 64, 128), BF16), pltpu.VMEM((2, 10, 64, 128), F32), pltpu.VMEM((16, 96, 128), BF16), pltpu.VMEM((3, 96, 192), F32),
         pltpu.VMEM((944, 64), F32), pltpu.VMEM((128, 24, 128), F32)],
        flops=2_000_000_000, moved=6_000_000,
    )(back, pre_rows, got_a, got_b, acts, side, part_three)

    cores = [(i, i ^ 1) for i in range(lax.axis_size("dp"))]
    plane = lax.axis_size(("depth", "height"))
    groups = [[i * plane + j for i in range(k, lax.axis_size("dp"), 2) for j in range(plane)] for k in range(2)]
    got = lax.ppermute(theirs, "dp", cores)
    parts, = call(
        combine,
        [((64, 24, 128), BF16)],
        [pltpu.VMEM((64, 24, 128), BF16), pltpu.SemaphoreType.DMA((4,))],
        moved=2_000_000, far_out=(0,),
    )(mine, got)
    parts = lax.all_to_all(parts, AXES, 0, 0, axis_index_groups=groups, tiled=True)
    into_rows, ship = call(
        into,
        [((4, 16, 32, 128), F32), ((16, 32, 128), BF16)],
        [pltpu.VMEM((4, 18, 64, 128), BF16), pltpu.VMEM((2, 10, 64, 128), F32), pltpu.VMEM((4, 16, 32, 128), F32),
         pltpu.SemaphoreType.DMA((4,))],
        flops=4_000_000_000, moved=6_000_000, far_out=(0,),
    )(back, pre, got_a, got_b, wide_two)
    ship = lax.ppermute(ship, "depth", swap)
    parts, into_rows, ship = lax.optimization_barrier((parts, into_rows, ship))
    grad_input, = call(
        lambda *refs: finish(scale_two, *refs),
        [((32, 4, 16, 128), BF16)],
        moved=2_000_000,
    )(into_rows, ship)

    send, own = call(
        lambda *refs: reduce(scale_two / volumes, scale_three / volumes, *refs),
        [((64, 40, 128), BF16), ((18, 128), F32)],
        [pltpu.VMEM((40, 128), F32), pltpu.VMEM((16, 40, 128), BF16), pltpu.SemaphoreType.DMA((4,))],
        moved=2_000_000, far_out=(0,),
    )(parts, moments)
    own, w2, w3 = lax.optimization_barrier((own, weight_two, weight_three))
    full = lax.all_to_all(send, AXES, 0, 0, axis_index_groups=groups, tiled=True)
    other = lax.ppermute(full, "dp", cores)
    new_weight_two, new_weight_three, new_moment_two, new_moment_three = call(
        update,
        [(weight_two.shape, F32), (weight_three.shape[::-1], F32), (moment_two.shape, F32), (moment_three.shape, F32)],
        [pltpu.VMEM((128, 18, 128), F32)],
        moved=4_000_000,
    )(full, other, own, w2, w3.T, moment_two, moment_three)
    return (grad_input[None], new_weight_two, new_weight_three.T, new_moment_two, new_moment_three)


def solution(mesh):
    in_specs = (
        P("dp", None, "depth", "height", None),
        P("dp", None, "depth", "height", None),
        P("dp", None, "depth", "height"),
        P(),
        P(),
        P(AXES),
        P(AXES),
    )
    out_specs = (
        P("dp", None, "depth", "height", None),
        P(),
        P(),
        P(AXES),
        P(AXES),
    )
    return jax.shard_map(local, mesh=mesh, in_specs=in_specs, out_specs=out_specs, check_vma=False)
```

```python
import jax
import jax.numpy as jnp
from jax import lax
from jax.experimental import pallas as pl
from jax.experimental.pallas import tpu as pltpu
from jax.sharding import PartitionSpec as P

SLOPE = 0.3
LEARN = 4.0
TRUST = 0.05
MOMENTUM = 0.9
EPSILON = 1e-06
AXES = ("dp", "depth", "height")
F32 = jnp.float32
BF16 = jnp.bfloat16


def call(body, outs, scratch=(), flops=0, moved=0, far=(), far_out=()):
    def run(*args):
        return pl.pallas_call(
            body,
            out_shape=[
                pltpu.HBM(shape, dtype) if i in far_out else jax.ShapeDtypeStruct(shape, dtype)
                for i, (shape, dtype) in enumerate(outs)
            ],
            in_specs=[pl.BlockSpec(memory_space=pltpu.HBM if i in far else pltpu.VMEM) for i in range(len(args))],
            out_specs=[pl.BlockSpec(memory_space=pltpu.HBM if i in far_out else pltpu.VMEM) for i in range(len(outs))],
            scratch_shapes=list(scratch),
            compiler_params=pltpu.CompilerParams(vmem_limit_bytes=20 * 1024 * 1024),
            cost_estimate=pl.CostEstimate(flops=flops, bytes_accessed=moved, transcendentals=0),
        )(*(pltpu.with_memory_space_constraint(x, pltpu.HBM) if i in far else x for i, x in enumerate(args)))

    return run


def dot_nt(a, b):
    return lax.dot_general(a, b, (((1,), (1,)), ((), ())), preferred_element_type=F32)


def dot_nn(a, b):
    return lax.dot_general(a, b, (((1,), (0,)), ((), ())), preferred_element_type=F32)


def shifted(x, amount):
    size = x.shape[-1]
    amount = amount % size
    if amount == 0:
        return x
    return jnp.concatenate([x[..., amount:], x[..., :amount]], axis=-1)


def arrange(cot_far, pre_far, act_far, cot_out, side_out, a_out, b_out, diag_a_out, diag_b_out,
            cot_ref, pre_ref, act_ref, sems):
    dep = lax.axis_index("depth")
    loads = [pltpu.make_async_copy(cot_far, cot_ref, sems.at[0])]
    loads += [pltpu.make_async_copy(act_far.at[:, 3 * (1 - dep)], act_ref, sems.at[1])]
    loads += [pltpu.make_async_copy(pre_far.at[:, d], pre_ref.at[:, d], sems.at[2 + d]) for d in range(4)]
    for load in loads:
        load.start()
    loads[0].wait()
    odd = lax.rem(lax.axis_index("height"), 2) == 1
    cots = [cot_ref[:, d, :] for d in range(2)]
    for d in range(2):
        cot_out[d] = cots[d]
        top, bottom = cots[d][:, :128], cots[d][:, 384:]
        a_out[128 * d : 128 * d + 128] = jnp.where(odd, top, bottom)
        b_out[128 * d : 128 * d + 128] = jnp.where(odd, bottom, top)
    near = jnp.where(dep == 0, cots[1], cots[0])
    diag_a_out[:128] = jnp.where(odd, near[:, :128], near[:, 384:])
    diag_a_out[128:] = jnp.zeros((384, 128), BF16)
    diag_b_out[...] = jnp.where(odd, near[:, 384:], near[:, :128])
    for t in range(4):
        side_out[128 * t : 128 * t + 128] = near[:, 128 * t : 128 * t + 128]
    loads[1].wait()
    layer = jnp.swapaxes(act_ref[...].astype(F32), 0, 1).astype(BF16)
    side_out[512:] = layer.reshape(512, 128)
    for d in range(4):
        loads[2 + d].wait()
        first, final = pre_ref[:, d, 0, :], pre_ref[:, d, 15, :]
        place = slice(256 + 64 * d, 320 + 64 * d)
        a_out[place] = jnp.where(odd, first, final)
        b_out[place] = jnp.where(odd, final, first)


def shifts(rows):
    lane = lax.broadcasted_iota(jnp.int32, rows.shape, rows.ndim - 1)
    before = jnp.where(lane < 127, shifted(rows, 1), 0.0)
    after = jnp.where(lane > 0, shifted(rows, -1), 0.0)
    return before, rows, after


def prepare(pre_ref, act_ref, w2_ref, w3_far, m2_ref, m3_ref, pre_out, pooled_out, act_out, w2_out, w3_out, m_out,
            t2, w3_ref, sems):
    loads = []
    for i in range(6):
        rows = slice(288 * i, 288 * i + 288)
        loads.append(pltpu.make_async_copy(w3_far.at[rows], w3_ref.at[rows], sems.at[i]))
        loads[i].start()
    for d in range(4):
        pre_out[d] = jnp.swapaxes(pre_ref[:, d].astype(F32), 0, 1).astype(BF16)
    m_out[...] = jnp.zeros((24, 128), F32)
    for b in range(3):
        m_out[b, :] = m2_ref[pl.ds(128 * b, 128)]
    for b in range(13):
        m_out[3 + b, :] = m3_ref[pl.ds(128 * b, 128)]
    m_out[16, :64] = m3_ref[pl.ds(1664, 64)]
    m_out[16, 64:112] = m2_ref[pl.ds(384, 48)]
    row = lax.broadcasted_iota(jnp.int32, (256, 128), 0)
    col = lax.broadcasted_iota(jnp.int32, (256, 128), 1)
    pool = jnp.where(row // 2 == col, 0.125, 0.0).astype(BF16)
    for d in range(2):
        for t in range(4):
            halves = []
            for half in range(2):
                total = None
                for i in range(2):
                    for j in range(2):
                        x = pre_out[2 * d + i, 4 * t + 2 * half + j].astype(F32)
                        x = jnp.where(x > 0, x, SLOPE * x)
                        total = x if total is None else total + x
                halves.append(total)
            total = jnp.concatenate(halves, axis=1)
            high = total.astype(BF16)
            low = (total - high.astype(F32)).astype(BF16)
            mean = dot_nn(high, pool) + dot_nn(low, pool)
            pooled_out[64 * d : 64 * d + 64, 128 * t : 128 * t + 128] = mean.astype(BF16)
    for d in range(4):
        rows = jnp.swapaxes(act_ref[:, d].astype(F32), 0, 1)
        for ow, value in enumerate(shifts(rows)):
            start = 96 * d + 32 * ow
            act_out[:, start : start + 32, :] = value.astype(BF16)
    t2[...] = jnp.transpose(w2_ref[...])
    for load in loads:
        load.wait()
    for kd in range(3):
        for oh in range(3):
            for ow in range(3):
                k = kd * 9 + (2 - oh) * 3 + (2 - ow)
                block = w3_ref[pl.ds(k, 64, stride=27), :].astype(BF16)
                tap = oh * 3 + ow
                w3_out[64 * kd : 64 * kd + 64, 128 * tap : 128 * tap + 128] = block
    zero = jnp.zeros((32, 64), F32)
    for kd in range(3):
        for ow in range(3):
            taps = []
            for oh in range(3):
                k = kd * 9 + (2 - oh) * 3 + (2 - ow)
                taps.append(t2[pl.ds(k, 32, stride=27), :])
            for r in range(2):
                blocks = taps + [zero] if r == 0 else [zero] + taps
                start = 64 * kd + 32 * r
                w2_out[start : start + 32, 256 * ow : 256 * ow + 256] = jnp.concatenate(blocks, axis=1).astype(BF16)


def coarse(scale, own_ref, side_ref, a_ref, da_ref, b_ref, db_ref, w3_ref, pooled_ref,
           back_out, grad_out, s_buf, back, parts, t3):
    dep = lax.axis_index("depth")
    hgt = lax.axis_index("height")
    odd = lax.rem(hgt, 2) == 1

    def slice_of(rows, a, b):
        return jnp.concatenate([jnp.where(odd, a, b)] + rows + [jnp.where(odd, b, a)], axis=1)

    column = lax.broadcasted_iota(jnp.int32, (128, 768), 1) % 64

    def taps(n, x):
        for ow in range(3):
            if ow == 0:
                moved = jnp.where(column > 0, shifted(x, -1), jnp.zeros_like(x))
            elif ow == 1:
                moved = x
            else:
                moved = jnp.where(column < 63, shifted(x, 1), jnp.zeros_like(x))
            for oh in range(3):
                tap = oh * 3 + ow
                s_buf[n, 128 * tap : 128 * tap + 128, :] = shifted(moved, (oh - 1) * 64)

    for z in range(2):
        rows = slice(128 * z, 128 * z + 128)
        taps(z, slice_of([own_ref[z]], a_ref[rows], b_ref[rows]))
    taps(2, slice_of([side_ref[128 * t : 128 * t + 128] for t in range(4)], da_ref[:128], db_ref[...]))
    y0 = dot_nn(w3_ref[64:192, :], s_buf[0])
    y1 = dot_nn(w3_ref[0:128, :], s_buf[1])
    back[0] = y0[:64] + y1[:64]
    back[1] = y0[64:] + y1[64:]
    kd = pl.multiple_of(128 * dep, 128)
    back[1 - dep] += dot_nn(w3_ref[pl.ds(kd, 64), :], s_buf[2])
    lane = lax.broadcasted_iota(jnp.int32, (64, 768), 1)
    keep = ((lane >= 128) | (hgt > 0)) & ((lane < 640) | (hgt < 7))
    for d in range(2):
        back_out[d] = jnp.where(keep, scale * back[d], 0.0).astype(BF16)
    r0 = dot_nt(pooled_ref[...], s_buf[0, :, 128:640])
    r1 = dot_nt(pooled_ref[...], s_buf[1, :, 128:640])
    parts[0] = r0[64:]
    parts[1] = r0[:64] + r1[64:]
    parts[2] = r1[:64]
    d = pl.multiple_of(64 * (1 - dep), 64)
    parts[2 * (1 - dep)] += dot_nt(pooled_ref[pl.ds(d, 64), :], s_buf[2, :, 128:640])
    for od in range(3):
        for oh in range(3):
            for ow in range(3):
                k = (2 - od) * 9 + (2 - oh) * 3 + (2 - ow)
                tap = oh * 3 + ow
                t3[pl.ds(k, 64, stride=27), :] = parts[od, :, 128 * tap : 128 * tap + 128]
    t3[1728:] = jnp.zeros((64, 128), F32)
    for b in range(14):
        grad_out[b] = jnp.transpose(t3[128 * b : 128 * b + 128, :])


def cotangent(back_ref, a_ref, b_ref, pre_rows, upper, z_out):
    odd = lax.rem(lax.axis_index("height"), 2) == 1
    row = lax.broadcasted_iota(jnp.int32, (128, 256), 0)
    col = lax.broadcasted_iota(jnp.int32, (128, 256), 1)
    spread = jnp.where(row == col // 2, 0.125, 0.0).astype(BF16)
    for t in range(6):
        x = back_ref[:, :, 128 * t : 128 * t + 128].reshape(128, 128)
        y = dot_nn(x, spread).reshape(2, 64, 256)
        if t > 0:
            upper[:, 2 * t - 1] = y[:, :, :128]
        if t < 5:
            upper[:, 2 * t] = y[:, :, 128:]
    for f in range(4):
        place = slice(256 + 64 * f, 320 + 64 * f)
        rows = pre_rows(f)
        for h in range(18):
            if h == 0:
                pre = jnp.where(odd, a_ref[place], b_ref[place])
            elif h == 17:
                pre = jnp.where(odd, b_ref[place], a_ref[place])
            else:
                pre = rows[h - 1]
            up = upper[f // 2, (h + 1) // 2]
            z_out[f, h] = jnp.where(pre.astype(F32) > 0, up, SLOPE * up).astype(BF16)


def fine(back_ref, pre_ref, a_ref, b_ref, act_ref, side_ref, three_ref, m_ref,
         mine_out, theirs_out, z_out, upper, near, parts, t2, stage):
    dep = lax.axis_index("depth")
    cotangent(back_ref, a_ref, b_ref, lambda f: pre_ref.at[f], upper, z_out)
    layer = side_ref[512:].astype(F32).reshape(16, 32, 128)
    for ow, value in enumerate(shifts(layer)):
        near[:, 32 * ow : 32 * ow + 32, :] = value.astype(BF16)

    def correlate(z, lhs):
        total = None
        for h in range(4):
            left = jnp.concatenate([lhs(h + 4 * i) for i in range(4)], axis=1)
            right = jnp.concatenate(
                [z_out[z, h + 4 * i : h + 4 * i + 3].reshape(192, 128) for i in range(4)], axis=1
            )
            r = dot_nt(left, right)
            total = r if total is None else total + r
        return total

    sums = [None, None, None]
    for z in range(4):
        first, final = max(0, z - 1), min(3, z + 1)
        total = correlate(z, lambda h: act_ref[h, 96 * first : 96 * (final + 1), :])
        for d in range(first, final + 1):
            part = total[96 * (d - first) : 96 * (d - first + 1)]
            od = z - d + 1
            sums[od] = part if sums[od] is None else sums[od] + part
    for od in range(3):
        parts[od] = sums[od]
    parts[2 * dep] += correlate(3 * (1 - dep), lambda h: near[h])
    for od in range(3):
        for oh in range(3):
            for ow in range(3):
                k = (2 - od) * 9 + (2 - oh) * 3 + (2 - ow)
                t2[pl.ds(k, 32, stride=27), :] = parts[od, 32 * ow : 32 * ow + 32, 64 * oh : 64 * oh + 64]
    t2[864:] = jnp.zeros((80, 64), F32)
    tail = lax.broadcasted_iota(jnp.int32, (64, 128), 1) < 48
    for half in range(2):
        for b in range(4):
            start = 432 * half + 128 * b
            block = jnp.transpose(t2[start : start + 128, :])
            if b == 3:
                block = jnp.where(tail, block, 0.0)
            stage[pl.ds(half, 64, stride=2), b, :] = block
    for b in range(14):
        stage[:, 4 + b, :] = three_ref[b]
    stage[:, 18:21, :] = jnp.broadcast_to(m_ref[:3][None], (128, 3, 128))
    stage[:, 21:, :] = jnp.zeros((128, 3, 128), F32)
    core = lax.rem(lax.axis_index("dp"), 2)
    for x in range(4):
        place = slice(16 * x, 16 * x + 16)
        mine_out[place] = stage[pl.ds(32 * x + 16 * core, 16)]
        theirs_out[place] = stage[pl.ds(32 * x + 16 * (1 - core), 16)].astype(BF16)


def combine(mine_ref, got_ref, parts_far, packed, sems):
    leave = []
    for i in range(4):
        piece = slice(16 * i, 16 * i + 16)
        mine, got = mine_ref[piece], got_ref[piece].astype(F32)
        rows = [mine[:, :18] + got[:, :18], mine[:, 18:21], got[:, 18:21]]
        packed[piece] = jnp.concatenate(rows, axis=1).astype(BF16)
        leave.append(pltpu.make_async_copy(packed.at[piece], parts_far.at[piece], sems.at[i]))
        leave[i].start()
    for copy in leave:
        copy.wait()


def into(back_ref, pre_ref, a_ref, b_ref, w2_ref, rows_far, ship, z_ref, upper, rows, sems):
    dep = lax.axis_index("depth")
    cotangent(back_ref, a_ref, b_ref, lambda f: jnp.swapaxes(pre_ref[:, f].astype(F32), 0, 1), upper, z_ref)
    lane = lax.broadcasted_iota(jnp.int32, (256, 128), 1)
    leave = []
    for jp in range(4):
        acc = [None] * 6
        for z in range(4):
            blocks = []
            for j in (2 * jp, 2 * jp + 1):
                x = z_ref[z, 2 * j : 2 * j + 4].reshape(256, 128)
                left = jnp.where(lane > 0, shifted(x, -1), jnp.zeros_like(x))
                right = jnp.where(lane < 127, shifted(x, 1), jnp.zeros_like(x))
                blocks.append(jnp.concatenate([left, x, right], axis=0))
            y = dot_nn(w2_ref[...], jnp.concatenate(blocks, axis=1))
            for kd in range(3):
                d = z + kd
                part = y[64 * kd : 64 * kd + 64]
                acc[d] = part if acc[d] is None else acc[d] + part
        for j in range(2):
            for r in range(2):
                h = 4 * jp + 2 * j + r
                block = (slice(32 * r, 32 * r + 32), slice(128 * j, 128 * j + 128))
                ship[h] = jnp.where(dep == 0, acc[5][block], acc[0][block]).astype(BF16)
                for d in range(4):
                    rows[d, h] = acc[d + 1][block]
        piece = (slice(None), slice(4 * jp, 4 * jp + 4))
        leave.append(pltpu.make_async_copy(rows.at[piece], rows_far.at[piece], sems.at[jp]))
        leave[jp].start()
    for copy in leave:
        copy.wait()


def finish(scale, rows_ref, ship_ref, out_ref):
    dep = lax.axis_index("depth")
    for d in range(4):
        rows = rows_ref[d]
        if d in (0, 3):
            rows = rows + jnp.where(dep == (0 if d == 3 else 1), ship_ref[...].astype(F32), 0.0)
        out_ref[:, d] = (scale * jnp.swapaxes(rows, 0, 1)).astype(BF16)


def reduce(scale_two, scale_three, parts_ref, m_ref, send_far, own_out, rows, block, sems):
    total = jnp.sum(parts_ref[:, :18, :].astype(F32), axis=0)
    row = lax.broadcasted_iota(jnp.int32, (18, 128), 0)
    total = total * jnp.where(row < 4, scale_two, scale_three)
    own_out[...] = total
    rows[:18] = total
    rows[18:] = m_ref[3:17]
    block[...] = jnp.broadcast_to(rows[...].astype(BF16)[None], (16, 32, 128))
    leave = [pltpu.make_async_copy(block, send_far.at[16 * i : 16 * i + 16], sems.at[i]) for i in range(4)]
    for copy in leave:
        copy.start()
    for copy in leave:
        copy.wait()


def update(full_ref, other_ref, first_ref, own_ref, w2_ref, w3_ref, m2_ref, m3_ref, w2_out, w3_out, m2_out, m3_out, stage):
    w2 = w2_ref[...]
    w3 = w3_ref[...]
    both = full_ref, other_ref
    grads = [ref[:, :18, :].astype(F32) for ref in both]
    square = sum(jnp.sum(grad * grad, axis=0) for grad in grads)
    row = lax.broadcasted_iota(jnp.int32, (18, 128), 0)
    norm_two = jnp.sqrt(jnp.sum(jnp.where(row < 4, square, 0.0), keepdims=True))
    norm_three = jnp.sqrt(jnp.sum(jnp.where(row < 4, 0.0, square), keepdims=True))
    rate_two = LEARN * (TRUST * jnp.sqrt(jnp.sum(w2 * w2, keepdims=True)) / (norm_two + EPSILON))
    rate_three = LEARN * (TRUST * jnp.sqrt(jnp.sum(w3 * w3, keepdims=True)) / (norm_three + EPSILON))
    rate = jnp.where(row < 4, rate_two, rate_three)
    core = lax.rem(lax.axis_index("dp"), 2)
    lane = lax.broadcasted_iota(jnp.int32, (64, 128), 1)
    for n, (ref, grad, side) in enumerate(zip(both, grads, (core, 1 - core))):
        head = first_ref[:, 18 + 3 * n : 21 + 3 * n, :].astype(F32)
        rest = ref[:, 18:, :].astype(F32)
        tails = rest[:, 13, :]
        tail_two = jnp.where(lane < 48, shifted(tails, 64), 0.0)
        tail_three = jnp.where(lane < 64, tails, 0.0)
        moments = jnp.concatenate([head, tail_two[:, None], rest[:, :13], tail_three[:, None]], axis=1)
        moved = MOMENTUM * moments + rate[None] * grad
        for x in range(4):
            stage[pl.ds(32 * x + 16 * side, 16)] = moved[16 * x : 16 * x + 16]
    for b in range(14):
        rows = slice(128 * b, min(128 * b + 128, 1728))
        w3_out[rows] = w3[rows] - jnp.transpose(stage[:, 4 + b, :])[: rows.stop - rows.start]
    halves = []
    for half in range(2):
        blocks = [stage[pl.ds(half, 64, stride=2), b, :] for b in range(4)]
        halves.append(jnp.concatenate(blocks, axis=1)[:, :432])
    w2_out[...] = w2 - jnp.concatenate(halves, axis=1)
    own = rate * own_ref[...]
    for b in range(3):
        m2_out[pl.ds(128 * b, 128)] = MOMENTUM * m2_ref[pl.ds(128 * b, 128)] + own[b]
    m2_out[pl.ds(384, 48)] = MOMENTUM * m2_ref[pl.ds(384, 48)] + own[3, :48]
    for b in range(13):
        m3_out[pl.ds(128 * b, 128)] = MOMENTUM * m3_ref[pl.ds(128 * b, 128)] + own[4 + b]
    m3_out[pl.ds(1664, 64)] = MOMENTUM * m3_ref[pl.ds(1664, 64)] + own[17, :64]


def local(act_one, pre_two, cot_three, weight_two, weight_three, moment_two, moment_three):
    scale_two = (act_one.shape[1] * 27) ** (-0.5)
    scale_three = (pre_two.shape[1] * 27) ** (-0.5)
    volumes = lax.axis_size("dp")
    pre, act, cot = pre_two[0], act_one[0], cot_three[0]

    cot_rows, send_side, send_a, send_b, send_da, send_db = call(
        arrange,
        [((2, 128, 512), BF16), ((1024, 128), BF16), ((512, 128), BF16),
         ((512, 128), BF16), ((512, 128), BF16), ((128, 128), BF16)],
        [pltpu.VMEM((128, 2, 512), BF16), pltpu.VMEM((64, 4, 16, 128), BF16), pltpu.VMEM((32, 16, 128), BF16),
         pltpu.SemaphoreType.DMA((6,))],
        moved=4_000_000, far=(0, 1, 2),
    )(cot, pre, act)
    tall = lax.axis_size("height")
    swap = [(0, 1), (1, 0)]
    pairs_a = [(h, h ^ 1) for h in range(tall)]
    pairs_b = [(h, ((h + 1) ^ 1) - 1) for h in range(1, tall - 1)]
    cross_a, cross_b = (
        [(d * tall + i, (1 - d) * tall + j) for d in range(2) for i, j in pairs] for pairs in (pairs_a, pairs_b)
    )
    side = lax.ppermute(send_side, "depth", swap)
    got_a = lax.ppermute(send_a, "height", pairs_a)
    got_da = lax.ppermute(send_da, ("depth", "height"), cross_a)
    got_b = lax.ppermute(send_b, "height", pairs_b)
    got_db = lax.ppermute(send_db, ("depth", "height"), cross_b)

    pre_rows, pooled, acts, wide_two, wide_three, moments = call(
        prepare,
        [((4, 16, 64, 128), BF16), ((128, 512), BF16), ((16, 384, 128), BF16), ((192, 768), BF16), ((192, 1152), BF16), ((24, 128), F32)],
        [pltpu.VMEM((864, 64), F32), pltpu.VMEM((1728, 128), F32), pltpu.SemaphoreType.DMA((6,))],
        flops=100_000_000, moved=8_000_000, far=(3,),
    )(pre, act, weight_two, weight_three.T, moment_two, moment_three)

    back, part_three = call(
        lambda *refs: coarse(scale_three, *refs),
        [((2, 64, 768), BF16), ((14, 128, 128), F32)],
        [pltpu.VMEM((3, 1152, 768), BF16), pltpu.VMEM((2, 64, 768), F32), pltpu.VMEM((3, 64, 1152), F32),
         pltpu.VMEM((1792, 128), F32)],
        flops=2_000_000_000, moved=4_000_000,
    )(cot_rows, side, got_a, got_da, got_b, got_db, wide_three, pooled)

    mine, theirs = call(
        fine,
        [((64, 24, 128), F32), ((64, 24, 128), BF16)],
        [pltpu.VMEM((4, 18, 64, 128), BF16), pltpu.VMEM((2, 10, 64, 128), F32), pltpu.VMEM((16, 96, 128), BF16), pltpu.VMEM((3, 96, 192), F32),
         pltpu.VMEM((944, 64), F32), pltpu.VMEM((128, 24, 128), F32)],
        flops=2_000_000_000, moved=6_000_000,
    )(back, pre_rows, got_a, got_b, acts, side, part_three, moments)

    cores = [(i, i ^ 1) for i in range(lax.axis_size("dp"))]
    plane = lax.axis_size(("depth", "height"))
    groups = [[i * plane + j for i in range(k, lax.axis_size("dp"), 2) for j in range(plane)] for k in range(2)]
    got = lax.ppermute(theirs, "dp", cores)
    parts, = call(
        combine,
        [((64, 24, 128), BF16)],
        [pltpu.VMEM((64, 24, 128), BF16), pltpu.SemaphoreType.DMA((4,))],
        moved=2_000_000, far_out=(0,),
    )(mine, got)
    parts = lax.all_to_all(parts, AXES, 0, 0, axis_index_groups=groups, tiled=True)
    into_rows, ship = call(
        into,
        [((4, 16, 32, 128), F32), ((16, 32, 128), BF16)],
        [pltpu.VMEM((4, 18, 64, 128), BF16), pltpu.VMEM((2, 10, 64, 128), F32), pltpu.VMEM((4, 16, 32, 128), F32),
         pltpu.SemaphoreType.DMA((4,))],
        flops=4_000_000_000, moved=6_000_000, far_out=(0,),
    )(back, pre, got_a, got_b, wide_two)
    ship = lax.ppermute(ship, "depth", swap)
    parts, into_rows, ship = lax.optimization_barrier((parts, into_rows, ship))
    grad_input, = call(
        lambda *refs: finish(scale_two, *refs),
        [((32, 4, 16, 128), BF16)],
        moved=2_000_000,
    )(into_rows, ship)

    send, own = call(
        lambda *refs: reduce(scale_two / volumes, scale_three / volumes, *refs),
        [((64, 32, 128), BF16), ((18, 128), F32)],
        [pltpu.VMEM((32, 128), F32), pltpu.VMEM((16, 32, 128), BF16), pltpu.SemaphoreType.DMA((4,))],
        moved=2_000_000, far_out=(0,),
    )(parts, moments)
    own, w2, w3 = lax.optimization_barrier((own, weight_two, weight_three))
    full = lax.all_to_all(send, AXES, 0, 0, axis_index_groups=groups, tiled=True)
    other = lax.ppermute(full, "dp", cores)
    new_weight_two, new_weight_three, new_moment_two, new_moment_three = call(
        update,
        [(weight_two.shape, F32), (weight_three.shape[::-1], F32), (moment_two.shape, F32), (moment_three.shape, F32)],
        [pltpu.VMEM((128, 18, 128), F32)],
        moved=4_000_000,
    )(full, other, parts, own, w2, w3.T, moment_two, moment_three)
    return (grad_input[None], new_weight_two, new_weight_three.T, new_moment_two, new_moment_three)


def solution(mesh):
    in_specs = (
        P("dp", None, "depth", "height", None),
        P("dp", None, "depth", "height", None),
        P("dp", None, "depth", "height"),
        P(),
        P(),
        P(AXES),
        P(AXES),
    )
    out_specs = (
        P("dp", None, "depth", "height", None),
        P(),
        P(),
        P(AXES),
        P(AXES),
    )
    return jax.shard_map(local, mesh=mesh, in_specs=in_specs, out_specs=out_specs, check_vma=False)
```

```python
import jax
import jax.numpy as jnp
from jax import lax
from jax.experimental import pallas as pl
from jax.experimental.pallas import tpu as pltpu
from jax.sharding import PartitionSpec as P

SLOPE = 0.3
LEARN = 4.0
TRUST = 0.05
MOMENTUM = 0.9
EPSILON = 1e-06
AXES = ("dp", "depth", "height")
F32 = jnp.float32
BF16 = jnp.bfloat16


def call(body, outs, scratch=(), flops=0, moved=0, far=(), far_out=()):
    def run(*args):
        return pl.pallas_call(
            body,
            out_shape=[
                pltpu.HBM(shape, dtype) if i in far_out else jax.ShapeDtypeStruct(shape, dtype)
                for i, (shape, dtype) in enumerate(outs)
            ],
            in_specs=[pl.BlockSpec(memory_space=pltpu.HBM if i in far else pltpu.VMEM) for i in range(len(args))],
            out_specs=[pl.BlockSpec(memory_space=pltpu.HBM if i in far_out else pltpu.VMEM) for i in range(len(outs))],
            scratch_shapes=list(scratch),
            compiler_params=pltpu.CompilerParams(vmem_limit_bytes=20 * 1024 * 1024),
            cost_estimate=pl.CostEstimate(flops=flops, bytes_accessed=moved, transcendentals=0),
        )(*(pltpu.with_memory_space_constraint(x, pltpu.HBM) if i in far else x for i, x in enumerate(args)))

    return run


def dot_nt(a, b):
    return lax.dot_general(a, b, (((1,), (1,)), ((), ())), preferred_element_type=F32)


def dot_nn(a, b):
    return lax.dot_general(a, b, (((1,), (0,)), ((), ())), preferred_element_type=F32)


def shifted(x, amount):
    size = x.shape[-1]
    amount = amount % size
    if amount == 0:
        return x
    return jnp.concatenate([x[..., amount:], x[..., :amount]], axis=-1)


def arrange(cot_far, pre_far, act_far, w3_far, cot_out, side_out, a_out, b_out, diag_a_out, diag_b_out, w3_out,
            cot_ref, pre_ref, act_ref, sems):
    dep = lax.axis_index("depth")
    loads = [pltpu.make_async_copy(cot_far, cot_ref, sems.at[0])]
    loads += [pltpu.make_async_copy(act_far.at[:, 3 * (1 - dep)], act_ref, sems.at[1])]
    loads += [pltpu.make_async_copy(pre_far.at[:, d], pre_ref.at[:, d], sems.at[2 + d]) for d in range(4)]
    loads += [pltpu.make_async_copy(w3_far, w3_out, sems.at[6])]
    for load in loads:
        load.start()
    loads[0].wait()
    odd = lax.rem(lax.axis_index("height"), 2) == 1
    cots = [cot_ref[:, d, :] for d in range(2)]
    for d in range(2):
        cot_out[d] = cots[d]
        top, bottom = cots[d][:, :128], cots[d][:, 384:]
        a_out[128 * d : 128 * d + 128] = jnp.where(odd, top, bottom)
        b_out[128 * d : 128 * d + 128] = jnp.where(odd, bottom, top)
    near = jnp.where(dep == 0, cots[1], cots[0])
    diag_a_out[:128] = jnp.where(odd, near[:, :128], near[:, 384:])
    diag_a_out[128:] = jnp.zeros((384, 128), BF16)
    diag_b_out[...] = jnp.where(odd, near[:, 384:], near[:, :128])
    for t in range(4):
        side_out[128 * t : 128 * t + 128] = near[:, 128 * t : 128 * t + 128]
    loads[1].wait()
    layer = jnp.swapaxes(act_ref[...].astype(F32), 0, 1).astype(BF16)
    side_out[512:] = layer.reshape(512, 128)
    for d in range(4):
        loads[2 + d].wait()
        first, final = pre_ref[:, d, 0, :], pre_ref[:, d, 15, :]
        place = slice(256 + 64 * d, 320 + 64 * d)
        a_out[place] = jnp.where(odd, first, final)
        b_out[place] = jnp.where(odd, final, first)
    loads[6].wait()


def shifts(rows):
    lane = lax.broadcasted_iota(jnp.int32, rows.shape, rows.ndim - 1)
    before = jnp.where(lane < 127, shifted(rows, 1), 0.0)
    after = jnp.where(lane > 0, shifted(rows, -1), 0.0)
    return before, rows, after


def prepare(pre_ref, act_ref, w2_ref, w3_ref, m2_ref, m3_ref, pre_out, pooled_out, act_out, w2_out, w3_out, m_out,
            t2):
    for d in range(4):
        pre_out[d] = jnp.swapaxes(pre_ref[:, d].astype(F32), 0, 1).astype(BF16)
    m_out[...] = jnp.zeros((24, 128), F32)
    for b in range(3):
        m_out[b, :] = m2_ref[pl.ds(128 * b, 128)]
    for b in range(13):
        m_out[3 + b, :] = m3_ref[pl.ds(128 * b, 128)]
    m_out[16, :64] = m3_ref[pl.ds(1664, 64)]
    m_out[16, 64:112] = m2_ref[pl.ds(384, 48)]
    row = lax.broadcasted_iota(jnp.int32, (256, 128), 0)
    col = lax.broadcasted_iota(jnp.int32, (256, 128), 1)
    pool = jnp.where(row // 2 == col, 0.125, 0.0).astype(BF16)
    for d in range(2):
        for t in range(4):
            halves = []
            for half in range(2):
                total = None
                for i in range(2):
                    for j in range(2):
                        x = pre_out[2 * d + i, 4 * t + 2 * half + j].astype(F32)
                        x = jnp.maximum(x, SLOPE * x)
                        total = x if total is None else total + x
                halves.append(total)
            total = jnp.concatenate(halves, axis=1)
            high = total.astype(BF16)
            low = (total - high.astype(F32)).astype(BF16)
            mean = dot_nn(high, pool) + dot_nn(low, pool)
            pooled_out[64 * d : 64 * d + 64, 128 * t : 128 * t + 128] = mean.astype(BF16)
    for d in range(4):
        rows = jnp.swapaxes(act_ref[:, d].astype(F32), 0, 1)
        for ow, value in enumerate(shifts(rows)):
            start = 96 * d + 32 * ow
            act_out[:, start : start + 32, :] = value.astype(BF16)
    t2[...] = jnp.transpose(w2_ref[...])
    for kd in range(3):
        for oh in range(3):
            for ow in range(3):
                k = kd * 9 + (2 - oh) * 3 + (2 - ow)
                block = w3_ref[pl.ds(k, 64, stride=27), :].astype(BF16)
                tap = oh * 3 + ow
                w3_out[64 * kd : 64 * kd + 64, 128 * tap : 128 * tap + 128] = block
    zero = jnp.zeros((32, 64), F32)
    for kd in range(3):
        for ow in range(3):
            taps = []
            for oh in range(3):
                k = kd * 9 + (2 - oh) * 3 + (2 - ow)
                taps.append(t2[pl.ds(k, 32, stride=27), :])
            for r in range(2):
                blocks = taps + [zero] if r == 0 else [zero] + taps
                start = 64 * kd + 32 * r
                w2_out[start : start + 32, 256 * ow : 256 * ow + 256] = jnp.concatenate(blocks, axis=1).astype(BF16)


def coarse(scale, own_ref, side_ref, a_ref, da_ref, b_ref, db_ref, w3_ref, pooled_ref,
           back_out, grad_out, s_buf, back, parts, t3):
    dep = lax.axis_index("depth")
    hgt = lax.axis_index("height")
    odd = lax.rem(hgt, 2) == 1

    def slice_of(rows, a, b):
        return jnp.concatenate([jnp.where(odd, a, b)] + rows + [jnp.where(odd, b, a)], axis=1)

    column = lax.broadcasted_iota(jnp.int32, (128, 768), 1) % 64

    def taps(n, x):
        for ow in range(3):
            if ow == 0:
                moved = jnp.where(column > 0, shifted(x, -1), jnp.zeros_like(x))
            elif ow == 1:
                moved = x
            else:
                moved = jnp.where(column < 63, shifted(x, 1), jnp.zeros_like(x))
            for oh in range(3):
                tap = oh * 3 + ow
                s_buf[n, 128 * tap : 128 * tap + 128, :] = shifted(moved, (oh - 1) * 64)

    for z in range(2):
        rows = slice(128 * z, 128 * z + 128)
        taps(z, slice_of([own_ref[z]], a_ref[rows], b_ref[rows]))
    taps(2, slice_of([side_ref[128 * t : 128 * t + 128] for t in range(4)], da_ref[:128], db_ref[...]))
    y0 = dot_nn(w3_ref[64:192, :], s_buf[0])
    y1 = dot_nn(w3_ref[0:128, :], s_buf[1])
    back[0] = y0[:64] + y1[:64]
    back[1] = y0[64:] + y1[64:]
    kd = pl.multiple_of(128 * dep, 128)
    back[1 - dep] += dot_nn(w3_ref[pl.ds(kd, 64), :], s_buf[2])
    lane = lax.broadcasted_iota(jnp.int32, (64, 768), 1)
    keep = ((lane >= 128) | (hgt > 0)) & ((lane < 640) | (hgt < 7))
    for d in range(2):
        back_out[d] = jnp.where(keep, scale * back[d], 0.0).astype(BF16)
    r0 = dot_nt(pooled_ref[...], s_buf[0, :, 128:640])
    r1 = dot_nt(pooled_ref[...], s_buf[1, :, 128:640])
    parts[0] = r0[64:]
    parts[1] = r0[:64] + r1[64:]
    parts[2] = r1[:64]
    d = pl.multiple_of(64 * (1 - dep), 64)
    parts[2 * (1 - dep)] += dot_nt(pooled_ref[pl.ds(d, 64), :], s_buf[2, :, 128:640])
    for od in range(3):
        for oh in range(3):
            for ow in range(3):
                k = (2 - od) * 9 + (2 - oh) * 3 + (2 - ow)
                tap = oh * 3 + ow
                t3[pl.ds(k, 64, stride=27), :] = parts[od, :, 128 * tap : 128 * tap + 128]
    t3[1728:] = jnp.zeros((64, 128), F32)
    for b in range(14):
        grad_out[b] = jnp.transpose(t3[128 * b : 128 * b + 128, :])


def cotangent(back_ref, a_ref, b_ref, pre_rows, upper, z_out):
    odd = lax.rem(lax.axis_index("height"), 2) == 1
    row = lax.broadcasted_iota(jnp.int32, (128, 256), 0)
    col = lax.broadcasted_iota(jnp.int32, (128, 256), 1)
    spread = jnp.where(row == col // 2, 0.125, 0.0).astype(BF16)
    for t in range(6):
        x = back_ref[:, :, 128 * t : 128 * t + 128].reshape(128, 128)
        y = dot_nn(x, spread).reshape(2, 64, 256)
        if t > 0:
            upper[:, 2 * t - 1] = y[:, :, :128]
        if t < 5:
            upper[:, 2 * t] = y[:, :, 128:]
    for f in range(4):
        place = slice(256 + 64 * f, 320 + 64 * f)
        rows = pre_rows(f)
        for h in range(18):
            if h == 0:
                pre = jnp.where(odd, a_ref[place], b_ref[place])
            elif h == 17:
                pre = jnp.where(odd, b_ref[place], a_ref[place])
            else:
                pre = rows[h - 1]
            up = upper[f // 2, (h + 1) // 2]
            z_out[f, h] = jnp.where(pre.astype(F32) > 0, up, SLOPE * up).astype(BF16)


def fine(back_ref, pre_ref, a_ref, b_ref, act_ref, side_ref, three_ref, m_ref,
         mine_out, theirs_out, z_out, upper, near, parts, t2, stage, small):
    dep = lax.axis_index("depth")
    cotangent(back_ref, a_ref, b_ref, lambda f: pre_ref.at[f], upper, z_out)
    layer = side_ref[512:].astype(F32).reshape(16, 32, 128)
    for ow, value in enumerate(shifts(layer)):
        near[:, 32 * ow : 32 * ow + 32, :] = value.astype(BF16)

    def correlate(z, lhs):
        total = None
        for h in range(4):
            left = jnp.concatenate([lhs(h + 4 * i) for i in range(4)], axis=1)
            right = jnp.concatenate(
                [z_out[z, h + 4 * i : h + 4 * i + 3].reshape(192, 128) for i in range(4)], axis=1
            )
            r = dot_nt(left, right)
            total = r if total is None else total + r
        return total

    sums = [None, None, None]
    for z in range(4):
        first, final = max(0, z - 1), min(3, z + 1)
        total = correlate(z, lambda h: act_ref[h, 96 * first : 96 * (final + 1), :])
        for d in range(first, final + 1):
            part = total[96 * (d - first) : 96 * (d - first + 1)]
            od = z - d + 1
            sums[od] = part if sums[od] is None else sums[od] + part
    for od in range(3):
        parts[od] = sums[od]
    parts[2 * dep] += correlate(3 * (1 - dep), lambda h: near[h])
    for od in range(3):
        for oh in range(3):
            for ow in range(3):
                k = (2 - od) * 9 + (2 - oh) * 3 + (2 - ow)
                t2[pl.ds(k, 32, stride=27), :] = parts[od, 32 * ow : 32 * ow + 32, 64 * oh : 64 * oh + 64]
    t2[864:] = jnp.zeros((80, 64), F32)
    tail = lax.broadcasted_iota(jnp.int32, (64, 128), 1) < 48
    core = lax.rem(lax.axis_index("dp"), 2)
    for half in range(2):
        for b in range(4):
            start = 432 * half + 128 * b
            block = jnp.transpose(t2[start : start + 128, :])
            if b == 3:
                block = jnp.where(tail, block, 0.0)
            small[b, pl.ds(half, 64, stride=2), :] = block
    for out, side in ((mine_out, core), (stage, 1 - core)):
        for x in range(4):
            rows = pl.ds(pl.multiple_of(32 * x + 16 * side, 16), 16)
            place = slice(16 * x, 16 * x + 16)
            for b in range(4):
                out[place, b, :] = small[b, rows, :]
            for b in range(14):
                out[place, 4 + b, :] = three_ref[b, rows, :]
        out[:, 18:21, :] = jnp.broadcast_to(m_ref[:3][None], (64, 3, 128))
        out[:, 21:, :] = jnp.zeros((64, 3, 128), F32)
    theirs_out[...] = stage[...].astype(BF16)


def combine(mine_ref, got_ref, parts_far, packed, sems):
    leave = []
    for i in range(4):
        piece = slice(16 * i, 16 * i + 16)
        mine, got = mine_ref[piece], got_ref[piece].astype(F32)
        rows = [mine[:, :18] + got[:, :18], mine[:, 18:21], got[:, 18:21]]
        packed[piece] = jnp.concatenate(rows, axis=1).astype(BF16)
        leave.append(pltpu.make_async_copy(packed.at[piece], parts_far.at[piece], sems.at[i]))
        leave[i].start()
    for copy in leave:
        copy.wait()


def into(back_ref, pre_ref, a_ref, b_ref, w2_ref, rows_far, ship, z_ref, upper, rows, sems):
    dep = lax.axis_index("depth")
    cotangent(back_ref, a_ref, b_ref, lambda f: jnp.swapaxes(pre_ref[:, f].astype(F32), 0, 1), upper, z_ref)
    lane = lax.broadcasted_iota(jnp.int32, (256, 128), 1)
    leave = []
    for jp in range(4):
        acc = [None] * 6
        for z in range(4):
            blocks = []
            for j in (2 * jp, 2 * jp + 1):
                x = z_ref[z, 2 * j : 2 * j + 4].reshape(256, 128)
                left = jnp.where(lane > 0, shifted(x, -1), jnp.zeros_like(x))
                right = jnp.where(lane < 127, shifted(x, 1), jnp.zeros_like(x))
                blocks.append(jnp.concatenate([left, x, right], axis=0))
            y = dot_nn(w2_ref[...], jnp.concatenate(blocks, axis=1))
            for kd in range(3):
                d = z + kd
                part = y[64 * kd : 64 * kd + 64]
                acc[d] = part if acc[d] is None else acc[d] + part
        for j in range(2):
            for r in range(2):
                h = 4 * jp + 2 * j + r
                block = (slice(32 * r, 32 * r + 32), slice(128 * j, 128 * j + 128))
                ship[h] = jnp.where(dep == 0, acc[5][block], acc[0][block]).astype(BF16)
                for d in range(4):
                    rows[d, h] = acc[d + 1][block]
        piece = (slice(None), slice(4 * jp, 4 * jp + 4))
        leave.append(pltpu.make_async_copy(rows.at[piece], rows_far.at[piece], sems.at[jp]))
        leave[jp].start()
    for copy in leave:
        copy.wait()


def finish(scale, rows_ref, ship_ref, out_ref):
    dep = lax.axis_index("depth")
    for d in range(4):
        rows = rows_ref[d]
        if d in (0, 3):
            rows = rows + jnp.where(dep == (0 if d == 3 else 1), ship_ref[...].astype(F32), 0.0)
        out_ref[:, d] = (scale * jnp.swapaxes(rows, 0, 1)).astype(BF16)


def reduce(scale_two, scale_three, parts_ref, m_ref, send_far, own_out, rows, block, sems):
    total = jnp.sum(parts_ref[:, :18, :].astype(F32), axis=0)
    row = lax.broadcasted_iota(jnp.int32, (18, 128), 0)
    total = total * jnp.where(row < 4, scale_two, scale_three)
    own_out[...] = total
    rows[:18] = total
    rows[18:] = m_ref[3:17]
    block[...] = jnp.broadcast_to(rows[...].astype(BF16)[None], (16, 32, 128))
    leave = [pltpu.make_async_copy(block, send_far.at[16 * i : 16 * i + 16], sems.at[i]) for i in range(4)]
    for copy in leave:
        copy.start()
    for copy in leave:
        copy.wait()


def update(full_ref, other_ref, first_ref, own_ref, w2_ref, w3_ref, m2_ref, m3_ref, w2_out, w3_out, m2_out, m3_out, stage):
    w2 = w2_ref[...]
    w3 = w3_ref[...]
    both = full_ref, other_ref
    grads = [ref[:, :18, :].astype(F32) for ref in both]
    square = sum(jnp.sum(grad * grad, axis=0) for grad in grads)
    row = lax.broadcasted_iota(jnp.int32, (18, 128), 0)
    norm_two = jnp.sqrt(jnp.sum(jnp.where(row < 4, square, 0.0), keepdims=True))
    norm_three = jnp.sqrt(jnp.sum(jnp.where(row < 4, 0.0, square), keepdims=True))
    rate_two = LEARN * (TRUST * jnp.sqrt(jnp.sum(w2 * w2, keepdims=True)) / (norm_two + EPSILON))
    rate_three = LEARN * (TRUST * jnp.sqrt(jnp.sum(w3 * w3, keepdims=True)) / (norm_three + EPSILON))
    rate = jnp.where(row < 4, rate_two, rate_three)
    core = lax.rem(lax.axis_index("dp"), 2)
    lane = lax.broadcasted_iota(jnp.int32, (64, 128), 1)
    for n, (ref, grad, side) in enumerate(zip(both, grads, (core, 1 - core))):
        head = first_ref[:, 18 + 3 * n : 21 + 3 * n, :].astype(F32)
        rest = ref[:, 18:, :].astype(F32)
        tails = rest[:, 13, :]
        tail_two = jnp.where(lane < 48, shifted(tails, 64), 0.0)
        tail_three = jnp.where(lane < 64, tails, 0.0)
        moments = jnp.concatenate([head, tail_two[:, None], rest[:, :13], tail_three[:, None]], axis=1)
        moved = MOMENTUM * moments + rate[None] * grad
        for x in range(4):
            stage[pl.ds(32 * x + 16 * side, 16)] = moved[16 * x : 16 * x + 16]
    for b in range(14):
        rows = slice(128 * b, min(128 * b + 128, 1728))
        w3_out[rows] = w3[rows] - jnp.transpose(stage[:, 4 + b, :])[: rows.stop - rows.start]
    halves = []
    for half in range(2):
        blocks = [stage[pl.ds(half, 64, stride=2), b, :] for b in range(4)]
        halves.append(jnp.concatenate(blocks, axis=1)[:, :432])
    w2_out[...] = w2 - jnp.concatenate(halves, axis=1)
    own = rate * own_ref[...]
    for b in range(3):
        m2_out[pl.ds(128 * b, 128)] = MOMENTUM * m2_ref[pl.ds(128 * b, 128)] + own[b]
    m2_out[pl.ds(384, 48)] = MOMENTUM * m2_ref[pl.ds(384, 48)] + own[3, :48]
    for b in range(13):
        m3_out[pl.ds(128 * b, 128)] = MOMENTUM * m3_ref[pl.ds(128 * b, 128)] + own[4 + b]
    m3_out[pl.ds(1664, 64)] = MOMENTUM * m3_ref[pl.ds(1664, 64)] + own[17, :64]


def local(act_one, pre_two, cot_three, weight_two, weight_three, moment_two, moment_three):
    scale_two = (act_one.shape[1] * 27) ** (-0.5)
    scale_three = (pre_two.shape[1] * 27) ** (-0.5)
    volumes = lax.axis_size("dp")
    pre, act, cot = pre_two[0], act_one[0], cot_three[0]

    cot_rows, send_side, send_a, send_b, send_da, send_db, w3_near = call(
        arrange,
        [((2, 128, 512), BF16), ((1024, 128), BF16), ((512, 128), BF16),
         ((512, 128), BF16), ((512, 128), BF16), ((128, 128), BF16),
         ((1728, 128), F32)],
        [pltpu.VMEM((128, 2, 512), BF16), pltpu.VMEM((64, 4, 16, 128), BF16), pltpu.VMEM((32, 16, 128), BF16),
         pltpu.SemaphoreType.DMA((7,))],
        moved=4_000_000, far=(0, 1, 2, 3),
    )(cot, pre, act, weight_three.T)
    tall = lax.axis_size("height")
    swap = [(0, 1), (1, 0)]
    pairs_a = [(h, h ^ 1) for h in range(tall)]
    pairs_b = [(h, ((h + 1) ^ 1) - 1) for h in range(1, tall - 1)]
    cross_a, cross_b = (
        [(d * tall + i, (1 - d) * tall + j) for d in range(2) for i, j in pairs] for pairs in (pairs_a, pairs_b)
    )
    side = lax.ppermute(send_side, "depth", swap)
    got_a = lax.ppermute(send_a, "height", pairs_a)
    got_da = lax.ppermute(send_da, ("depth", "height"), cross_a)
    got_b = lax.ppermute(send_b, "height", pairs_b)
    got_db = lax.ppermute(send_db, ("depth", "height"), cross_b)

    pre_rows, pooled, acts, wide_two, wide_three, moments = call(
        prepare,
        [((4, 16, 64, 128), BF16), ((128, 512), BF16), ((16, 384, 128), BF16), ((192, 768), BF16), ((192, 1152), BF16), ((24, 128), F32)],
        [pltpu.VMEM((864, 64), F32)],
        flops=100_000_000, moved=8_000_000,
    )(pre, act, weight_two, w3_near, moment_two, moment_three)

    back, part_three = call(
        lambda *refs: coarse(scale_three, *refs),
        [((2, 64, 768), BF16), ((14, 128, 128), F32)],
        [pltpu.VMEM((3, 1152, 768), BF16), pltpu.VMEM((2, 64, 768), F32), pltpu.VMEM((3, 64, 1152), F32),
         pltpu.VMEM((1792, 128), F32)],
        flops=2_000_000_000, moved=4_000_000,
    )(cot_rows, side, got_a, got_da, got_b, got_db, wide_three, pooled)

    mine, theirs = call(
        fine,
        [((64, 24, 128), F32), ((64, 24, 128), BF16)],
        [pltpu.VMEM((4, 18, 64, 128), BF16), pltpu.VMEM((2, 10, 64, 128), F32), pltpu.VMEM((16, 96, 128), BF16), pltpu.VMEM((3, 96, 192), F32),
         pltpu.VMEM((944, 64), F32), pltpu.VMEM((64, 24, 128), F32), pltpu.VMEM((4, 128, 128), F32)],
        flops=2_000_000_000, moved=6_000_000,
    )(back, pre_rows, got_a, got_b, acts, side, part_three, moments)

    cores = [(i, i ^ 1) for i in range(lax.axis_size("dp"))]
    plane = lax.axis_size(("depth", "height"))
    groups = [[i * plane + j for i in range(k, lax.axis_size("dp"), 2) for j in range(plane)] for k in range(2)]
    got = lax.ppermute(theirs, "dp", cores)
    parts, = call(
        combine,
        [((64, 24, 128), BF16)],
        [pltpu.VMEM((64, 24, 128), BF16), pltpu.SemaphoreType.DMA((4,))],
        moved=2_000_000, far_out=(0,),
    )(mine, got)
    parts = lax.all_to_all(parts, AXES, 0, 0, axis_index_groups=groups, tiled=True)
    into_rows, ship = call(
        into,
        [((4, 16, 32, 128), F32), ((16, 32, 128), BF16)],
        [pltpu.VMEM((4, 18, 64, 128), BF16), pltpu.VMEM((2, 10, 64, 128), F32), pltpu.VMEM((4, 16, 32, 128), F32),
         pltpu.SemaphoreType.DMA((4,))],
        flops=4_000_000_000, moved=6_000_000, far_out=(0,),
    )(back, pre, got_a, got_b, wide_two)
    ship = lax.ppermute(ship, "depth", swap)
    parts, into_rows, ship = lax.optimization_barrier((parts, into_rows, ship))
    grad_input, = call(
        lambda *refs: finish(scale_two, *refs),
        [((32, 4, 16, 128), BF16)],
        moved=2_000_000,
    )(into_rows, ship)

    send, own = call(
        lambda *refs: reduce(scale_two / volumes, scale_three / volumes, *refs),
        [((64, 32, 128), BF16), ((18, 128), F32)],
        [pltpu.VMEM((32, 128), F32), pltpu.VMEM((16, 32, 128), BF16), pltpu.SemaphoreType.DMA((4,))],
        moved=2_000_000, far_out=(0,),
    )(parts, moments)
    own, w2, w3 = lax.optimization_barrier((own, weight_two, weight_three))
    full = lax.all_to_all(send, AXES, 0, 0, axis_index_groups=groups, tiled=True)
    other = lax.ppermute(full, "dp", cores)
    new_weight_two, new_weight_three, new_moment_two, new_moment_three = call(
        update,
        [(weight_two.shape, F32), (weight_three.shape[::-1], F32), (moment_two.shape, F32), (moment_three.shape, F32)],
        [pltpu.VMEM((128, 18, 128), F32)],
        moved=4_000_000,
    )(full, other, parts, own, w2, w3.T, moment_two, moment_three)
    return (grad_input[None], new_weight_two, new_weight_three.T, new_moment_two, new_moment_three)


def solution(mesh):
    in_specs = (
        P("dp", None, "depth", "height", None),
        P("dp", None, "depth", "height", None),
        P("dp", None, "depth", "height"),
        P(),
        P(),
        P(AXES),
        P(AXES),
    )
    out_specs = (
        P("dp", None, "depth", "height", None),
        P(),
        P(),
        P(AXES),
        P(AXES),
    )
    return jax.shard_map(local, mesh=mesh, in_specs=in_specs, out_specs=out_specs, check_vma=False)
```

```python
import jax
import jax.numpy as jnp
from jax import lax
from jax.experimental import pallas as pl
from jax.experimental.pallas import tpu as pltpu
from jax.sharding import PartitionSpec as P

SLOPE = 0.3
LEARN = 4.0
TRUST = 0.05
MOMENTUM = 0.9
EPSILON = 1e-06
AXES = ("dp", "depth", "height")
F32 = jnp.float32
BF16 = jnp.bfloat16


def call(body, outs, scratch=(), flops=0, moved=0, far=(), far_out=()):
    def run(*args):
        return pl.pallas_call(
            body,
            out_shape=[
                pltpu.HBM(shape, dtype) if i in far_out else jax.ShapeDtypeStruct(shape, dtype)
                for i, (shape, dtype) in enumerate(outs)
            ],
            in_specs=[pl.BlockSpec(memory_space=pltpu.HBM if i in far else pltpu.VMEM) for i in range(len(args))],
            out_specs=[pl.BlockSpec(memory_space=pltpu.HBM if i in far_out else pltpu.VMEM) for i in range(len(outs))],
            scratch_shapes=list(scratch),
            compiler_params=pltpu.CompilerParams(vmem_limit_bytes=20 * 1024 * 1024),
            cost_estimate=pl.CostEstimate(flops=flops, bytes_accessed=moved, transcendentals=0),
        )(*(pltpu.with_memory_space_constraint(x, pltpu.HBM) if i in far else x for i, x in enumerate(args)))

    return run


def dot_nt(a, b):
    return lax.dot_general(a, b, (((1,), (1,)), ((), ())), preferred_element_type=F32)


def dot_nn(a, b):
    return lax.dot_general(a, b, (((1,), (0,)), ((), ())), preferred_element_type=F32)


def shifted(x, amount):
    size = x.shape[-1]
    amount = amount % size
    if amount == 0:
        return x
    return jnp.concatenate([x[..., amount:], x[..., :amount]], axis=-1)


def arrange(cot_far, pre_far, act_far, w3_far, cot_out, side_out, a_out, b_out, diag_a_out, diag_b_out, w3_out,
            cot_ref, pre_ref, act_ref, sems):
    dep = lax.axis_index("depth")
    loads = [pltpu.make_async_copy(cot_far, cot_ref, sems.at[0])]
    loads += [pltpu.make_async_copy(act_far.at[:, 3 * (1 - dep)], act_ref, sems.at[1])]
    loads += [pltpu.make_async_copy(pre_far.at[:, d], pre_ref.at[:, d], sems.at[2 + d]) for d in range(4)]
    loads += [pltpu.make_async_copy(w3_far, w3_out.at[:1728], sems.at[6])]
    for load in loads:
        load.start()
    loads[0].wait()
    odd = lax.rem(lax.axis_index("height"), 2) == 1
    cots = [cot_ref[:, d, :] for d in range(2)]
    for d in range(2):
        cot_out[d] = cots[d]
        top, bottom = cots[d][:, :128], cots[d][:, 384:]
        a_out[128 * d : 128 * d + 128] = jnp.where(odd, top, bottom)
        b_out[128 * d : 128 * d + 128] = jnp.where(odd, bottom, top)
    near = jnp.where(dep == 0, cots[1], cots[0])
    diag_a_out[:128] = jnp.where(odd, near[:, :128], near[:, 384:])
    diag_a_out[128:] = jnp.zeros((384, 128), BF16)
    diag_b_out[...] = jnp.where(odd, near[:, 384:], near[:, :128])
    for t in range(4):
        side_out[128 * t : 128 * t + 128] = near[:, 128 * t : 128 * t + 128]
    loads[1].wait()
    layer = jnp.swapaxes(act_ref[...].astype(F32), 0, 1).astype(BF16)
    side_out[512:] = layer.reshape(512, 128)
    for d in range(4):
        loads[2 + d].wait()
        first, final = pre_ref[:, d, 0, :], pre_ref[:, d, 15, :]
        place = slice(256 + 64 * d, 320 + 64 * d)
        a_out[place] = jnp.where(odd, first, final)
        b_out[place] = jnp.where(odd, final, first)
    loads[6].wait()


def shifts(rows):
    lane = lax.broadcasted_iota(jnp.int32, rows.shape, rows.ndim - 1)
    before = jnp.where(lane < 127, shifted(rows, 1), 0.0)
    after = jnp.where(lane > 0, shifted(rows, -1), 0.0)
    return before, rows, after


def prepare(pre_ref, act_ref, w2_ref, w3_ref, m2_ref, m3_ref, pre_out, pooled_out, act_out, w2_out, w3_out, m_out,
            t2):
    for d in range(4):
        pre_out[d] = jnp.swapaxes(pre_ref[:, d].astype(F32), 0, 1).astype(BF16)
    m_out[...] = jnp.zeros((24, 128), F32)
    for b in range(3):
        m_out[b, :] = m2_ref[pl.ds(128 * b, 128)]
    for b in range(13):
        m_out[3 + b, :] = m3_ref[pl.ds(128 * b, 128)]
    m_out[16, :64] = m3_ref[pl.ds(1664, 64)]
    m_out[16, 64:112] = m2_ref[pl.ds(384, 48)]
    row = lax.broadcasted_iota(jnp.int32, (256, 128), 0)
    col = lax.broadcasted_iota(jnp.int32, (256, 128), 1)
    pool = jnp.where(row // 2 == col, 0.125, 0.0).astype(BF16)
    for d in range(2):
        for t in range(4):
            halves = []
            for half in range(2):
                total = None
                for i in range(2):
                    for j in range(2):
                        x = pre_out[2 * d + i, 4 * t + 2 * half + j].astype(F32)
                        x = jnp.maximum(x, SLOPE * x)
                        total = x if total is None else total + x
                halves.append(total)
            total = jnp.concatenate(halves, axis=1)
            high = total.astype(BF16)
            low = (total - high.astype(F32)).astype(BF16)
            mean = dot_nn(high, pool) + dot_nn(low, pool)
            pooled_out[64 * d : 64 * d + 64, 128 * t : 128 * t + 128] = mean.astype(BF16)
    for d in range(4):
        rows = jnp.swapaxes(act_ref[:, d].astype(F32), 0, 1)
        for ow, value in enumerate(shifts(rows)):
            start = 96 * d + 32 * ow
            act_out[:, start : start + 32, :] = value.astype(BF16)
    t2[:864] = jnp.transpose(w2_ref[...])
    for kd in range(3):
        for oh in range(3):
            for ow in range(3):
                k = kd * 9 + (2 - oh) * 3 + (2 - ow)
                block = w3_ref[pl.ds(k, 64, stride=27), :].astype(BF16)
                tap = oh * 3 + ow
                w3_out[64 * kd : 64 * kd + 64, 128 * tap : 128 * tap + 128] = block
    zero = jnp.zeros((32, 64), F32)
    for kd in range(3):
        for ow in range(3):
            taps = []
            for oh in range(3):
                k = kd * 9 + (2 - oh) * 3 + (2 - ow)
                taps.append(t2[pl.ds(k, 32, stride=27), :])
            for r in range(2):
                blocks = taps + [zero] if r == 0 else [zero] + taps
                start = 64 * kd + 32 * r
                w2_out[start : start + 32, 256 * ow : 256 * ow + 256] = jnp.concatenate(blocks, axis=1).astype(BF16)


def coarse(scale, own_ref, side_ref, a_ref, da_ref, b_ref, db_ref, w3_ref, pooled_ref,
           back_out, grad_out, s_buf, back, parts, t3):
    dep = lax.axis_index("depth")
    hgt = lax.axis_index("height")
    odd = lax.rem(hgt, 2) == 1

    def slice_of(rows, a, b):
        return jnp.concatenate([jnp.where(odd, a, b)] + rows + [jnp.where(odd, b, a)], axis=1)

    column = lax.broadcasted_iota(jnp.int32, (128, 768), 1) % 64

    def taps(n, x):
        for ow in range(3):
            if ow == 0:
                moved = jnp.where(column > 0, shifted(x, -1), jnp.zeros_like(x))
            elif ow == 1:
                moved = x
            else:
                moved = jnp.where(column < 63, shifted(x, 1), jnp.zeros_like(x))
            for oh in range(3):
                tap = oh * 3 + ow
                s_buf[n, 128 * tap : 128 * tap + 128, :] = shifted(moved, (oh - 1) * 64)

    for z in range(2):
        rows = slice(128 * z, 128 * z + 128)
        taps(z, slice_of([own_ref[z]], a_ref[rows], b_ref[rows]))
    taps(2, slice_of([side_ref[128 * t : 128 * t + 128] for t in range(4)], da_ref[:128], db_ref[...]))
    y0 = dot_nn(w3_ref[64:192, :], s_buf[0])
    y1 = dot_nn(w3_ref[0:128, :], s_buf[1])
    back[0] = y0[:64] + y1[:64]
    back[1] = y0[64:] + y1[64:]
    kd = pl.multiple_of(128 * dep, 128)
    back[1 - dep] += dot_nn(w3_ref[pl.ds(kd, 64), :], s_buf[2])
    lane = lax.broadcasted_iota(jnp.int32, (64, 768), 1)
    keep = ((lane >= 128) | (hgt > 0)) & ((lane < 640) | (hgt < 7))
    for d in range(2):
        back_out[d] = jnp.where(keep, scale * back[d], 0.0).astype(BF16)
    r0 = dot_nt(pooled_ref[...], s_buf[0, :, 128:640])
    r1 = dot_nt(pooled_ref[...], s_buf[1, :, 128:640])
    parts[0] = r0[64:]
    parts[1] = r0[:64] + r1[64:]
    parts[2] = r1[:64]
    d = pl.multiple_of(64 * (1 - dep), 64)
    parts[2 * (1 - dep)] += dot_nt(pooled_ref[pl.ds(d, 64), :], s_buf[2, :, 128:640])
    for od in range(3):
        for oh in range(3):
            for ow in range(3):
                k = (2 - od) * 9 + (2 - oh) * 3 + (2 - ow)
                tap = oh * 3 + ow
                t3[pl.ds(k, 64, stride=27), :] = parts[od, :, 128 * tap : 128 * tap + 128]
    t3[1728:] = jnp.zeros((64, 128), F32)
    for b in range(14):
        grad_out[b] = jnp.transpose(t3[128 * b : 128 * b + 128, :])


def cotangent(back_ref, a_ref, b_ref, pre_rows, upper, z_out):
    odd = lax.rem(lax.axis_index("height"), 2) == 1
    row = lax.broadcasted_iota(jnp.int32, (128, 256), 0)
    col = lax.broadcasted_iota(jnp.int32, (128, 256), 1)
    spread = jnp.where(row == col // 2, 0.125, 0.0).astype(BF16)
    for t in range(6):
        x = back_ref[:, :, 128 * t : 128 * t + 128].reshape(128, 128)
        y = dot_nn(x, spread).reshape(2, 64, 256)
        if t > 0:
            upper[:, 2 * t - 1] = y[:, :, :128]
        if t < 5:
            upper[:, 2 * t] = y[:, :, 128:]
    for f in range(4):
        place = slice(256 + 64 * f, 320 + 64 * f)
        rows = pre_rows(f)
        for h in range(18):
            if h == 0:
                pre = jnp.where(odd, a_ref[place], b_ref[place])
            elif h == 17:
                pre = jnp.where(odd, b_ref[place], a_ref[place])
            else:
                pre = rows[h - 1]
            up = upper[f // 2, (h + 1) // 2]
            z_out[f, h] = jnp.where(pre.astype(F32) > 0, up, SLOPE * up).astype(BF16)


def fine(back_ref, pre_ref, a_ref, b_ref, act_ref, side_ref, three_ref, m_ref,
         mine_out, theirs_out, z_out, upper, near, parts, t2, stage, small):
    dep = lax.axis_index("depth")
    cotangent(back_ref, a_ref, b_ref, lambda f: pre_ref.at[f], upper, z_out)
    layer = side_ref[512:].astype(F32).reshape(16, 32, 128)
    for ow, value in enumerate(shifts(layer)):
        near[:, 32 * ow : 32 * ow + 32, :] = value.astype(BF16)

    def correlate(z, lhs):
        total = None
        for h in range(4):
            left = jnp.concatenate([lhs(h + 4 * i) for i in range(4)], axis=1)
            right = jnp.concatenate(
                [z_out[z, h + 4 * i : h + 4 * i + 3].reshape(192, 128) for i in range(4)], axis=1
            )
            r = dot_nt(left, right)
            total = r if total is None else total + r
        return total

    sums = [None, None, None]
    for z in range(4):
        first, final = max(0, z - 1), min(3, z + 1)
        total = correlate(z, lambda h: act_ref[h, 96 * first : 96 * (final + 1), :])
        for d in range(first, final + 1):
            part = total[96 * (d - first) : 96 * (d - first + 1)]
            od = z - d + 1
            sums[od] = part if sums[od] is None else sums[od] + part
    for od in range(3):
        parts[od] = sums[od]
    parts[2 * dep] += correlate(3 * (1 - dep), lambda h: near[h])
    for od in range(3):
        for oh in range(3):
            for ow in range(3):
                k = (2 - od) * 9 + (2 - oh) * 3 + (2 - ow)
                t2[pl.ds(k, 32, stride=27), :] = parts[od, 32 * ow : 32 * ow + 32, 64 * oh : 64 * oh + 64]
    t2[864:] = jnp.zeros((80, 64), F32)
    tail = lax.broadcasted_iota(jnp.int32, (64, 128), 1) < 48
    core = lax.rem(lax.axis_index("dp"), 2)
    for half in range(2):
        for b in range(4):
            start = 432 * half + 128 * b
            block = jnp.transpose(t2[start : start + 128, :])
            if b == 3:
                block = jnp.where(tail, block, 0.0)
            small[b, pl.ds(half, 64, stride=2), :] = block
    for out, side in ((mine_out, core), (stage, 1 - core)):
        for x in range(4):
            rows = pl.ds(pl.multiple_of(32 * x + 16 * side, 16), 16)
            place = slice(16 * x, 16 * x + 16)
            for b in range(4):
                out[place, b, :] = small[b, rows, :]
            for b in range(14):
                out[place, 4 + b, :] = three_ref[b, rows, :]
        out[:, 18:21, :] = jnp.broadcast_to(m_ref[:3][None], (64, 3, 128))
        out[:, 21:, :] = jnp.zeros((64, 3, 128), F32)
    theirs_out[...] = stage[...].astype(BF16)


def combine(mine_ref, got_ref, parts_far, packed, sems):
    leave = []
    for i in range(4):
        piece = slice(16 * i, 16 * i + 16)
        mine, got = mine_ref[piece], got_ref[piece].astype(F32)
        rows = [mine[:, :18] + got[:, :18], mine[:, 18:21], got[:, 18:21]]
        packed[piece] = jnp.concatenate(rows, axis=1).astype(BF16)
        leave.append(pltpu.make_async_copy(packed.at[piece], parts_far.at[piece], sems.at[i]))
        leave[i].start()
    for copy in leave:
        copy.wait()


def into(back_ref, pre_ref, a_ref, b_ref, w2_ref, rows_far, ship, z_ref, upper, rows, sems):
    dep = lax.axis_index("depth")
    cotangent(back_ref, a_ref, b_ref, lambda f: jnp.swapaxes(pre_ref[:, f].astype(F32), 0, 1), upper, z_ref)
    lane = lax.broadcasted_iota(jnp.int32, (256, 128), 1)
    leave = []
    for jp in range(4):
        acc = [None] * 6
        for z in range(4):
            blocks = []
            for j in (2 * jp, 2 * jp + 1):
                x = z_ref[z, 2 * j : 2 * j + 4].reshape(256, 128)
                left = jnp.where(lane > 0, shifted(x, -1), jnp.zeros_like(x))
                right = jnp.where(lane < 127, shifted(x, 1), jnp.zeros_like(x))
                blocks.append(jnp.concatenate([left, x, right], axis=0))
            y = dot_nn(w2_ref[...], jnp.concatenate(blocks, axis=1))
            for kd in range(3):
                d = z + kd
                part = y[64 * kd : 64 * kd + 64]
                acc[d] = part if acc[d] is None else acc[d] + part
        for j in range(2):
            for r in range(2):
                h = 4 * jp + 2 * j + r
                block = (slice(32 * r, 32 * r + 32), slice(128 * j, 128 * j + 128))
                ship[h] = jnp.where(dep == 0, acc[5][block], acc[0][block]).astype(BF16)
                for d in range(4):
                    rows[d, h] = acc[d + 1][block]
        piece = (slice(None), slice(4 * jp, 4 * jp + 4))
        leave.append(pltpu.make_async_copy(rows.at[piece], rows_far.at[piece], sems.at[jp]))
        leave[jp].start()
    for copy in leave:
        copy.wait()


def finish(scale, rows_ref, ship_ref, out_ref):
    dep = lax.axis_index("depth")
    for d in range(4):
        rows = rows_ref[d]
        if d in (0, 3):
            rows = rows + jnp.where(dep == (0 if d == 3 else 1), ship_ref[...].astype(F32), 0.0)
        out_ref[:, d] = (scale * jnp.swapaxes(rows, 0, 1)).astype(BF16)


def reduce(scale_two, scale_three, parts_ref, m_ref, send_far, own_out, rows, block, sems):
    total = jnp.sum(parts_ref[:, :18, :].astype(F32), axis=0)
    row = lax.broadcasted_iota(jnp.int32, (18, 128), 0)
    total = total * jnp.where(row < 4, scale_two, scale_three)
    own_out[...] = total
    rows[:18] = total
    rows[18:] = m_ref[3:17]
    block[...] = jnp.broadcast_to(rows[...].astype(BF16)[None], (16, 32, 128))
    leave = [pltpu.make_async_copy(block, send_far.at[16 * i : 16 * i + 16], sems.at[i]) for i in range(4)]
    for copy in leave:
        copy.start()
    for copy in leave:
        copy.wait()


def update(full_ref, other_ref, first_ref, own_ref, w2_ref, w3_ref, m2_ref, m3_ref, w2_out, w3_out, m2_out, m3_out, stage):
    w2 = w2_ref[...]
    w3 = w3_ref[...]
    both = full_ref, other_ref
    grads = [ref[:, :18, :].astype(F32) for ref in both]
    square = sum(jnp.sum(grad * grad, axis=0) for grad in grads)
    row = lax.broadcasted_iota(jnp.int32, (18, 128), 0)
    norm_two = jnp.sqrt(jnp.sum(jnp.where(row < 4, square, 0.0), keepdims=True))
    norm_three = jnp.sqrt(jnp.sum(jnp.where(row < 4, 0.0, square), keepdims=True))
    rate_two = LEARN * (TRUST * jnp.sqrt(jnp.sum(w2 * w2, keepdims=True)) / (norm_two + EPSILON))
    rate_three = LEARN * (TRUST * jnp.sqrt(jnp.sum(w3 * w3, keepdims=True)) / (norm_three + EPSILON))
    rate = jnp.where(row < 4, rate_two, rate_three)
    core = lax.rem(lax.axis_index("dp"), 2)
    lane = lax.broadcasted_iota(jnp.int32, (64, 128), 1)
    for n, (ref, grad, side) in enumerate(zip(both, grads, (core, 1 - core))):
        head = first_ref[:, 18 + 3 * n : 21 + 3 * n, :].astype(F32)
        rest = ref[:, 18:, :].astype(F32)
        tails = rest[:, 13, :]
        tail_two = jnp.where(lane < 48, shifted(tails, 64), 0.0)
        tail_three = jnp.where(lane < 64, tails, 0.0)
        moments = jnp.concatenate([head, tail_two[:, None], rest[:, :13], tail_three[:, None]], axis=1)
        moved = MOMENTUM * moments + rate[None] * grad
        for x in range(4):
            stage[pl.ds(32 * x + 16 * side, 16)] = moved[16 * x : 16 * x + 16]
    for b in range(14):
        rows = slice(128 * b, min(128 * b + 128, 1728))
        w3_out[rows] = w3[rows] - jnp.transpose(stage[:128, 4 + b, :])[: rows.stop - rows.start]
    halves = []
    for half in range(2):
        blocks = [stage[pl.ds(half, 64, stride=2), b, :] for b in range(4)]
        halves.append(jnp.concatenate(blocks, axis=1)[:, :432])
    w2_out[...] = w2 - jnp.concatenate(halves, axis=1)
    own = rate * own_ref[...]
    for b in range(3):
        m2_out[pl.ds(128 * b, 128)] = MOMENTUM * m2_ref[pl.ds(128 * b, 128)] + own[b]
    m2_out[pl.ds(384, 48)] = MOMENTUM * m2_ref[pl.ds(384, 48)] + own[3, :48]
    for b in range(13):
        m3_out[pl.ds(128 * b, 128)] = MOMENTUM * m3_ref[pl.ds(128 * b, 128)] + own[4 + b]
    m3_out[pl.ds(1664, 64)] = MOMENTUM * m3_ref[pl.ds(1664, 64)] + own[17, :64]


def local(act_one, pre_two, cot_three, weight_two, weight_three, moment_two, moment_three):
    scale_two = (act_one.shape[1] * 27) ** (-0.5)
    scale_three = (pre_two.shape[1] * 27) ** (-0.5)
    volumes = lax.axis_size("dp")
    pre, act, cot = pre_two[0], act_one[0], cot_three[0]

    cot_rows, send_side, send_a, send_b, send_da, send_db, w3_near = call(
        arrange,
        [((2, 128, 512), BF16), ((1024, 128), BF16), ((512, 128), BF16),
         ((512, 128), BF16), ((512, 128), BF16), ((128, 128), BF16),
         ((1792, 128), F32)],
        [pltpu.VMEM((128, 2, 512), BF16), pltpu.VMEM((64, 4, 16, 128), BF16), pltpu.VMEM((32, 16, 128), BF16),
         pltpu.SemaphoreType.DMA((7,))],
        moved=4_000_000, far=(0, 1, 2, 3),
    )(cot, pre, act, weight_three.T)
    tall = lax.axis_size("height")
    swap = [(0, 1), (1, 0)]
    pairs_a = [(h, h ^ 1) for h in range(tall)]
    pairs_b = [(h, ((h + 1) ^ 1) - 1) for h in range(1, tall - 1)]
    cross_a, cross_b = (
        [(d * tall + i, (1 - d) * tall + j) for d in range(2) for i, j in pairs] for pairs in (pairs_a, pairs_b)
    )
    side = lax.ppermute(send_side, "depth", swap)
    got_a = lax.ppermute(send_a, "height", pairs_a)
    got_da = lax.ppermute(send_da, ("depth", "height"), cross_a)
    got_b = lax.ppermute(send_b, "height", pairs_b)
    got_db = lax.ppermute(send_db, ("depth", "height"), cross_b)

    pre_rows, pooled, acts, wide_two, wide_three, moments = call(
        prepare,
        [((4, 16, 64, 128), BF16), ((128, 512), BF16), ((16, 384, 128), BF16), ((192, 768), BF16), ((192, 1152), BF16), ((24, 128), F32)],
        [pltpu.VMEM((896, 64), F32)],
        flops=100_000_000, moved=8_000_000,
    )(pre, act, weight_two, w3_near, moment_two, moment_three)

    back, part_three = call(
        lambda *refs: coarse(scale_three, *refs),
        [((2, 64, 768), BF16), ((14, 128, 128), F32)],
        [pltpu.VMEM((3, 1152, 768), BF16), pltpu.VMEM((2, 64, 768), F32), pltpu.VMEM((3, 64, 1152), F32),
         pltpu.VMEM((1792, 128), F32)],
        flops=2_000_000_000, moved=4_000_000,
    )(cot_rows, side, got_a, got_da, got_b, got_db, wide_three, pooled)

    mine, theirs = call(
        fine,
        [((64, 24, 128), F32), ((64, 24, 128), BF16)],
        [pltpu.VMEM((4, 18, 64, 128), BF16), pltpu.VMEM((2, 10, 64, 128), F32), pltpu.VMEM((16, 96, 128), BF16), pltpu.VMEM((3, 96, 192), F32),
         pltpu.VMEM((944, 64), F32), pltpu.VMEM((64, 24, 128), F32), pltpu.VMEM((4, 136, 128), F32)],
        flops=2_000_000_000, moved=6_000_000,
    )(back, pre_rows, got_a, got_b, acts, side, part_three, moments)

    cores = [(i, i ^ 1) for i in range(lax.axis_size("dp"))]
    plane = lax.axis_size(("depth", "height"))
    groups = [[i * plane + j for i in range(k, lax.axis_size("dp"), 2) for j in range(plane)] for k in range(2)]
    got = lax.ppermute(theirs, "dp", cores)
    parts, = call(
        combine,
        [((64, 24, 128), BF16)],
        [pltpu.VMEM((64, 24, 128), BF16), pltpu.SemaphoreType.DMA((4,))],
        moved=2_000_000, far_out=(0,),
    )(mine, got)
    parts = lax.all_to_all(parts, AXES, 0, 0, axis_index_groups=groups, tiled=True)
    into_rows, ship = call(
        into,
        [((4, 16, 32, 128), F32), ((16, 32, 128), BF16)],
        [pltpu.VMEM((4, 18, 64, 128), BF16), pltpu.VMEM((2, 10, 64, 128), F32), pltpu.VMEM((4, 16, 32, 128), F32),
         pltpu.SemaphoreType.DMA((4,))],
        flops=4_000_000_000, moved=6_000_000, far_out=(0,),
    )(back, pre, got_a, got_b, wide_two)
    ship = lax.ppermute(ship, "depth", swap)
    parts, into_rows, ship = lax.optimization_barrier((parts, into_rows, ship))
    grad_input, = call(
        lambda *refs: finish(scale_two, *refs),
        [((32, 4, 16, 128), BF16)],
        moved=2_000_000,
    )(into_rows, ship)

    send, own = call(
        lambda *refs: reduce(scale_two / volumes, scale_three / volumes, *refs),
        [((64, 32, 128), BF16), ((18, 128), F32)],
        [pltpu.VMEM((32, 128), F32), pltpu.VMEM((16, 32, 128), BF16), pltpu.SemaphoreType.DMA((4,))],
        moved=2_000_000, far_out=(0,),
    )(parts, moments)
    own, w2, w3 = lax.optimization_barrier((own, weight_two, weight_three))
    full = lax.all_to_all(send, AXES, 0, 0, axis_index_groups=groups, tiled=True)
    other = lax.ppermute(full, "dp", cores)
    new_weight_two, new_weight_three, new_moment_two, new_moment_three = call(
        update,
        [(weight_two.shape, F32), (weight_three.shape[::-1], F32), (moment_two.shape, F32), (moment_three.shape, F32)],
        [pltpu.VMEM((136, 18, 128), F32)],
        moved=4_000_000,
    )(full, other, parts, own, w2, w3.T, moment_two, moment_three)
    return (grad_input[None], new_weight_two, new_weight_three.T, new_moment_two, new_moment_three)


def solution(mesh):
    in_specs = (
        P("dp", None, "depth", "height", None),
        P("dp", None, "depth", "height", None),
        P("dp", None, "depth", "height"),
        P(),
        P(),
        P(AXES),
        P(AXES),
    )
    out_specs = (
        P("dp", None, "depth", "height", None),
        P(),
        P(),
        P(AXES),
        P(AXES),
    )
    return jax.shard_map(local, mesh=mesh, in_specs=in_specs, out_specs=out_specs, check_vma=False)
```

```python
import jax
import jax.numpy as jnp
from jax import lax
from jax.experimental import pallas as pl
from jax.experimental.pallas import tpu as pltpu
from jax.sharding import PartitionSpec as P

SLOPE = 0.3
LEARN = 4.0
TRUST = 0.05
MOMENTUM = 0.9
EPSILON = 1e-06
AXES = ("dp", "depth", "height")
F32 = jnp.float32
BF16 = jnp.bfloat16


def call(body, outs, scratch=(), flops=0, moved=0, far=(), far_out=()):
    def run(*args):
        return pl.pallas_call(
            body,
            out_shape=[
                pltpu.HBM(shape, dtype) if i in far_out else jax.ShapeDtypeStruct(shape, dtype)
                for i, (shape, dtype) in enumerate(outs)
            ],
            in_specs=[pl.BlockSpec(memory_space=pltpu.HBM if i in far else pltpu.VMEM) for i in range(len(args))],
            out_specs=[pl.BlockSpec(memory_space=pltpu.HBM if i in far_out else pltpu.VMEM) for i in range(len(outs))],
            scratch_shapes=list(scratch),
            compiler_params=pltpu.CompilerParams(vmem_limit_bytes=20 * 1024 * 1024),
            cost_estimate=pl.CostEstimate(flops=flops, bytes_accessed=moved, transcendentals=0),
        )(*(pltpu.with_memory_space_constraint(x, pltpu.HBM) if i in far else x for i, x in enumerate(args)))

    return run


def dot_nt(a, b):
    return lax.dot_general(a, b, (((1,), (1,)), ((), ())), preferred_element_type=F32)


def dot_nn(a, b):
    return lax.dot_general(a, b, (((1,), (0,)), ((), ())), preferred_element_type=F32)


def shifted(x, amount):
    size = x.shape[-1]
    amount = amount % size
    if amount == 0:
        return x
    return jnp.concatenate([x[..., amount:], x[..., :amount]], axis=-1)


def arrange(cot_far, pre_far, act_far, w3_far, cot_out, side_out, a_out, b_out, diag_a_out, diag_b_out, w3_out,
            cot_ref, pre_ref, act_ref, sems):
    dep = lax.axis_index("depth")
    loads = [pltpu.make_async_copy(cot_far, cot_ref, sems.at[0])]
    loads += [pltpu.make_async_copy(act_far.at[:, 3 * (1 - dep)], act_ref, sems.at[1])]
    loads += [pltpu.make_async_copy(pre_far.at[:, d], pre_ref.at[:, d], sems.at[2 + d]) for d in range(4)]
    loads += [pltpu.make_async_copy(w3_far, w3_out.at[:1728], sems.at[6])]
    for load in loads:
        load.start()
    loads[0].wait()
    odd = lax.rem(lax.axis_index("height"), 2) == 1
    cots = [cot_ref[:, d, :] for d in range(2)]
    for d in range(2):
        cot_out[d] = cots[d]
        top, bottom = cots[d][:, :128], cots[d][:, 384:]
        a_out[128 * d : 128 * d + 128] = jnp.where(odd, top, bottom)
        b_out[128 * d : 128 * d + 128] = jnp.where(odd, bottom, top)
    near = jnp.where(dep == 0, cots[1], cots[0])
    diag_a_out[:128] = jnp.where(odd, near[:, :128], near[:, 384:])
    diag_a_out[128:] = jnp.zeros((384, 128), BF16)
    diag_b_out[...] = jnp.where(odd, near[:, 384:], near[:, :128])
    for t in range(4):
        side_out[128 * t : 128 * t + 128] = near[:, 128 * t : 128 * t + 128]
    loads[1].wait()
    layer = jnp.swapaxes(act_ref[...].astype(F32), 0, 1).astype(BF16)
    side_out[512:] = layer.reshape(512, 128)
    for d in range(4):
        loads[2 + d].wait()
        first, final = pre_ref[:, d, 0, :], pre_ref[:, d, 15, :]
        place = slice(256 + 64 * d, 320 + 64 * d)
        a_out[place] = jnp.where(odd, first, final)
        b_out[place] = jnp.where(odd, final, first)
    loads[6].wait()


def shifts(rows):
    lane = lax.broadcasted_iota(jnp.int32, rows.shape, rows.ndim - 1)
    before = jnp.where(lane < 127, shifted(rows, 1), 0.0)
    after = jnp.where(lane > 0, shifted(rows, -1), 0.0)
    return before, rows, after


def prepare(pre_ref, act_ref, w2_ref, w3_ref, m2_ref, m3_ref, pre_out, pooled_out, act_out, w2_out, w3_out, m_out,
            t2):
    for d in range(4):
        pre_out[d] = jnp.swapaxes(pre_ref[:, d].astype(F32), 0, 1).astype(BF16)
    m_out[...] = jnp.zeros((24, 128), F32)
    for b in range(3):
        m_out[b, :] = m2_ref[pl.ds(128 * b, 128)]
    for b in range(13):
        m_out[3 + b, :] = m3_ref[pl.ds(128 * b, 128)]
    m_out[16, :64] = m3_ref[pl.ds(1664, 64)]
    m_out[16, 64:112] = m2_ref[pl.ds(384, 48)]
    row = lax.broadcasted_iota(jnp.int32, (256, 128), 0)
    col = lax.broadcasted_iota(jnp.int32, (256, 128), 1)
    pool = jnp.where(row // 2 == col, 0.125, 0.0).astype(BF16)
    for d in range(2):
        for t in range(4):
            halves = []
            for half in range(2):
                total = None
                for i in range(2):
                    for j in range(2):
                        x = pre_out[2 * d + i, 4 * t + 2 * half + j].astype(F32)
                        x = jnp.maximum(x, SLOPE * x)
                        total = x if total is None else total + x
                halves.append(total)
            total = jnp.concatenate(halves, axis=1)
            high = total.astype(BF16)
            low = (total - high.astype(F32)).astype(BF16)
            mean = dot_nn(high, pool) + dot_nn(low, pool)
            pooled_out[64 * d : 64 * d + 64, 128 * t : 128 * t + 128] = mean.astype(BF16)
    for d in range(4):
        rows = jnp.swapaxes(act_ref[:, d].astype(F32), 0, 1)
        for ow, value in enumerate(shifts(rows)):
            start = 96 * d + 32 * ow
            act_out[:, start : start + 32, :] = value.astype(BF16)
    t2[:864] = jnp.transpose(w2_ref[...])
    for kd in range(3):
        for oh in range(3):
            for ow in range(3):
                k = kd * 9 + (2 - oh) * 3 + (2 - ow)
                block = w3_ref[pl.ds(k, 64, stride=27), :].astype(BF16)
                tap = oh * 3 + ow
                w3_out[64 * kd : 64 * kd + 64, 128 * tap : 128 * tap + 128] = block
    zero = jnp.zeros((32, 64), F32)
    for kd in range(3):
        for ow in range(3):
            taps = []
            for oh in range(3):
                k = kd * 9 + (2 - oh) * 3 + (2 - ow)
                taps.append(t2[pl.ds(k, 32, stride=27), :])
            for r in range(2):
                blocks = taps + [zero] if r == 0 else [zero] + taps
                start = 64 * kd + 32 * r
                w2_out[start : start + 32, 256 * ow : 256 * ow + 256] = jnp.concatenate(blocks, axis=1).astype(BF16)


def coarse(scale, own_ref, side_ref, a_ref, da_ref, b_ref, db_ref, w3_ref, pooled_ref,
           back_out, grad_out, s_buf, back, parts, t3):
    dep = lax.axis_index("depth")
    hgt = lax.axis_index("height")
    odd = lax.rem(hgt, 2) == 1

    def slice_of(rows, a, b):
        return jnp.concatenate([jnp.where(odd, a, b)] + rows + [jnp.where(odd, b, a)], axis=1)

    column = lax.broadcasted_iota(jnp.int32, (128, 768), 1) % 64

    def taps(n, x):
        for ow in range(3):
            if ow == 0:
                moved = jnp.where(column > 0, shifted(x, -1), jnp.zeros_like(x))
            elif ow == 1:
                moved = x
            else:
                moved = jnp.where(column < 63, shifted(x, 1), jnp.zeros_like(x))
            for oh in range(3):
                tap = oh * 3 + ow
                s_buf[n, 128 * tap : 128 * tap + 128, :] = shifted(moved, (oh - 1) * 64)

    for z in range(2):
        rows = slice(128 * z, 128 * z + 128)
        taps(z, slice_of([own_ref[z]], a_ref[rows], b_ref[rows]))
    taps(2, slice_of([side_ref[128 * t : 128 * t + 128] for t in range(4)], da_ref[:128], db_ref[...]))
    y0 = dot_nn(w3_ref[64:192, :], s_buf[0])
    y1 = dot_nn(w3_ref[0:128, :], s_buf[1])
    back[0] = y0[:64] + y1[:64]
    back[1] = y0[64:] + y1[64:]
    kd = pl.multiple_of(128 * dep, 128)
    back[1 - dep] += dot_nn(w3_ref[pl.ds(kd, 64), :], s_buf[2])
    lane = lax.broadcasted_iota(jnp.int32, (64, 768), 1)
    keep = ((lane >= 128) | (hgt > 0)) & ((lane < 640) | (hgt < 7))
    for d in range(2):
        back_out[d] = jnp.where(keep, scale * back[d], 0.0).astype(BF16)
    r0 = dot_nt(pooled_ref[...], s_buf[0, :, 128:640])
    r1 = dot_nt(pooled_ref[...], s_buf[1, :, 128:640])
    parts[0] = r0[64:]
    parts[1] = r0[:64] + r1[64:]
    parts[2] = r1[:64]
    d = pl.multiple_of(64 * (1 - dep), 64)
    parts[2 * (1 - dep)] += dot_nt(pooled_ref[pl.ds(d, 64), :], s_buf[2, :, 128:640])
    for od in range(3):
        for oh in range(3):
            for ow in range(3):
                k = (2 - od) * 9 + (2 - oh) * 3 + (2 - ow)
                tap = oh * 3 + ow
                t3[pl.ds(k, 64, stride=27), :] = parts[od, :, 128 * tap : 128 * tap + 128]
    t3[1728:] = jnp.zeros((64, 128), F32)
    for b in range(14):
        grad_out[b] = jnp.transpose(t3[128 * b : 128 * b + 128, :])


def cotangent(back_ref, a_ref, b_ref, pre_rows, upper, z_out):
    odd = lax.rem(lax.axis_index("height"), 2) == 1
    row = lax.broadcasted_iota(jnp.int32, (128, 256), 0)
    col = lax.broadcasted_iota(jnp.int32, (128, 256), 1)
    spread = jnp.where(row == col // 2, 0.125, 0.0).astype(BF16)
    for t in range(6):
        x = back_ref[:, :, 128 * t : 128 * t + 128].reshape(128, 128)
        y = dot_nn(x, spread).reshape(2, 64, 256)
        if t > 0:
            upper[:, 2 * t - 1] = y[:, :, :128]
        if t < 5:
            upper[:, 2 * t] = y[:, :, 128:]
    for f in range(4):
        place = slice(256 + 64 * f, 320 + 64 * f)
        rows = pre_rows(f)
        for h in range(18):
            if h == 0:
                pre = jnp.where(odd, a_ref[place], b_ref[place])
            elif h == 17:
                pre = jnp.where(odd, b_ref[place], a_ref[place])
            else:
                pre = rows[h - 1]
            up = upper[f // 2, (h + 1) // 2]
            z_out[f, h] = jnp.where(pre.astype(F32) > 0, up, SLOPE * up).astype(BF16)


def fine(back_ref, pre_ref, a_ref, b_ref, act_ref, side_ref, three_ref, m_ref,
         mine_out, theirs_out, z_out, upper, near, parts, t2, stage, small):
    dep = lax.axis_index("depth")
    cotangent(back_ref, a_ref, b_ref, lambda f: pre_ref.at[f], upper, z_out)
    layer = side_ref[512:].astype(F32).reshape(16, 32, 128)
    for ow, value in enumerate(shifts(layer)):
        near[:, 32 * ow : 32 * ow + 32, :] = value.astype(BF16)

    def correlate(z, lhs):
        left = jnp.concatenate([lhs(h) for h in range(16)], axis=1)
        right = jnp.concatenate([z_out[z, h : h + 3].reshape(192, 128) for h in range(16)], axis=1)
        return dot_nt(left, right)

    sums = [None, None, None]
    for z in range(4):
        first, final = max(0, z - 1), min(3, z + 1)
        total = correlate(z, lambda h: act_ref[h, 96 * first : 96 * (final + 1), :])
        for d in range(first, final + 1):
            part = total[96 * (d - first) : 96 * (d - first + 1)]
            od = z - d + 1
            sums[od] = part if sums[od] is None else sums[od] + part
    for od in range(3):
        parts[od] = sums[od]
    parts[2 * dep] += correlate(3 * (1 - dep), lambda h: near[h])
    for od in range(3):
        for oh in range(3):
            for ow in range(3):
                k = (2 - od) * 9 + (2 - oh) * 3 + (2 - ow)
                t2[pl.ds(k, 32, stride=27), :] = parts[od, 32 * ow : 32 * ow + 32, 64 * oh : 64 * oh + 64]
    t2[864:] = jnp.zeros((80, 64), F32)
    tail = lax.broadcasted_iota(jnp.int32, (64, 128), 1) < 48
    core = lax.rem(lax.axis_index("dp"), 2)
    for half in range(2):
        for b in range(4):
            start = 432 * half + 128 * b
            block = jnp.transpose(t2[start : start + 128, :])
            if b == 3:
                block = jnp.where(tail, block, 0.0)
            small[b, pl.ds(half, 64, stride=2), :] = block
    for out, side in ((mine_out, core), (stage, 1 - core)):
        for x in range(4):
            rows = pl.ds(pl.multiple_of(32 * x + 16 * side, 16), 16)
            place = slice(16 * x, 16 * x + 16)
            for b in range(4):
                out[place, b, :] = small[b, rows, :]
            for b in range(14):
                out[place, 4 + b, :] = three_ref[b, rows, :]
        out[:, 18:21, :] = jnp.broadcast_to(m_ref[:3][None], (64, 3, 128))
        out[:, 21:, :] = jnp.zeros((64, 3, 128), F32)
    theirs_out[...] = stage[...].astype(BF16)


def combine(mine_ref, got_ref, parts_far, packed, sems):
    leave = []
    for i in range(4):
        piece = slice(16 * i, 16 * i + 16)
        mine, got = mine_ref[piece], got_ref[piece].astype(F32)
        rows = [mine[:, :18] + got[:, :18], mine[:, 18:21], got[:, 18:21]]
        packed[piece] = jnp.concatenate(rows, axis=1).astype(BF16)
        leave.append(pltpu.make_async_copy(packed.at[piece], parts_far.at[piece], sems.at[i]))
        leave[i].start()
    for copy in leave:
        copy.wait()


def into(back_ref, pre_ref, a_ref, b_ref, w2_ref, rows_far, ship, z_ref, upper, rows, sems):
    dep = lax.axis_index("depth")
    cotangent(back_ref, a_ref, b_ref, lambda f: jnp.swapaxes(pre_ref[:, f].astype(F32), 0, 1), upper, z_ref)
    lane = lax.broadcasted_iota(jnp.int32, (256, 128), 1)
    leave = []
    for jp in range(4):
        acc = [None] * 6
        for z in range(4):
            blocks = []
            for j in (2 * jp, 2 * jp + 1):
                x = z_ref[z, 2 * j : 2 * j + 4].reshape(256, 128)
                left = jnp.where(lane > 0, shifted(x, -1), jnp.zeros_like(x))
                right = jnp.where(lane < 127, shifted(x, 1), jnp.zeros_like(x))
                blocks.append(jnp.concatenate([left, x, right], axis=0))
            y = dot_nn(w2_ref[...], jnp.concatenate(blocks, axis=1))
            for kd in range(3):
                d = z + kd
                part = y[64 * kd : 64 * kd + 64]
                acc[d] = part if acc[d] is None else acc[d] + part
        for j in range(2):
            for r in range(2):
                h = 4 * jp + 2 * j + r
                block = (slice(32 * r, 32 * r + 32), slice(128 * j, 128 * j + 128))
                ship[h] = jnp.where(dep == 0, acc[5][block], acc[0][block]).astype(BF16)
                for d in range(4):
                    rows[d, h] = acc[d + 1][block]
        piece = (slice(None), slice(4 * jp, 4 * jp + 4))
        leave.append(pltpu.make_async_copy(rows.at[piece], rows_far.at[piece], sems.at[jp]))
        leave[jp].start()
    for copy in leave:
        copy.wait()


def finish(scale, rows_ref, ship_ref, out_ref):
    dep = lax.axis_index("depth")
    for d in range(4):
        rows = rows_ref[d]
        if d in (0, 3):
            rows = rows + jnp.where(dep == (0 if d == 3 else 1), ship_ref[...].astype(F32), 0.0)
        out_ref[:, d] = (scale * jnp.swapaxes(rows, 0, 1)).astype(BF16)


def reduce(scale_two, scale_three, parts_ref, m_ref, send_far, own_out, rows, block, sems):
    total = jnp.sum(parts_ref[:, :18, :].astype(F32), axis=0)
    row = lax.broadcasted_iota(jnp.int32, (18, 128), 0)
    total = total * jnp.where(row < 4, scale_two, scale_three)
    own_out[...] = total
    rows[:18] = total
    rows[18:] = m_ref[3:17]
    block[...] = jnp.broadcast_to(rows[...].astype(BF16)[None], (16, 32, 128))
    leave = [pltpu.make_async_copy(block, send_far.at[16 * i : 16 * i + 16], sems.at[i]) for i in range(4)]
    for copy in leave:
        copy.start()
    for copy in leave:
        copy.wait()


def update(full_ref, other_ref, first_ref, own_ref, w2_ref, w3_ref, m2_ref, m3_ref, w2_out, w3_out, m2_out, m3_out, stage):
    w2 = w2_ref[...]
    w3 = w3_ref[...]
    both = full_ref, other_ref
    grads = [ref[:, :18, :].astype(F32) for ref in both]
    square = sum(jnp.sum(grad * grad, axis=0) for grad in grads)
    row = lax.broadcasted_iota(jnp.int32, (18, 128), 0)
    norm_two = jnp.sqrt(jnp.sum(jnp.where(row < 4, square, 0.0), keepdims=True))
    norm_three = jnp.sqrt(jnp.sum(jnp.where(row < 4, 0.0, square), keepdims=True))
    rate_two = LEARN * (TRUST * jnp.sqrt(jnp.sum(w2 * w2, keepdims=True)) / (norm_two + EPSILON))
    rate_three = LEARN * (TRUST * jnp.sqrt(jnp.sum(w3 * w3, keepdims=True)) / (norm_three + EPSILON))
    rate = jnp.where(row < 4, rate_two, rate_three)
    core = lax.rem(lax.axis_index("dp"), 2)
    lane = lax.broadcasted_iota(jnp.int32, (64, 128), 1)
    for n, (ref, grad, side) in enumerate(zip(both, grads, (core, 1 - core))):
        head = first_ref[:, 18 + 3 * n : 21 + 3 * n, :].astype(F32)
        rest = ref[:, 18:, :].astype(F32)
        tails = rest[:, 13, :]
        tail_two = jnp.where(lane < 48, shifted(tails, 64), 0.0)
        tail_three = jnp.where(lane < 64, tails, 0.0)
        moments = jnp.concatenate([head, tail_two[:, None], rest[:, :13], tail_three[:, None]], axis=1)
        moved = MOMENTUM * moments + rate[None] * grad
        for x in range(4):
            stage[pl.ds(32 * x + 16 * side, 16)] = moved[16 * x : 16 * x + 16]
    for b in range(14):
        rows = slice(128 * b, min(128 * b + 128, 1728))
        w3_out[rows] = w3[rows] - jnp.transpose(stage[:128, 4 + b, :])[: rows.stop - rows.start]
    halves = []
    for half in range(2):
        blocks = [stage[pl.ds(half, 64, stride=2), b, :] for b in range(4)]
        halves.append(jnp.concatenate(blocks, axis=1)[:, :432])
    w2_out[...] = w2 - jnp.concatenate(halves, axis=1)
    own = rate * own_ref[...]
    for b in range(3):
        m2_out[pl.ds(128 * b, 128)] = MOMENTUM * m2_ref[pl.ds(128 * b, 128)] + own[b]
    m2_out[pl.ds(384, 48)] = MOMENTUM * m2_ref[pl.ds(384, 48)] + own[3, :48]
    for b in range(13):
        m3_out[pl.ds(128 * b, 128)] = MOMENTUM * m3_ref[pl.ds(128 * b, 128)] + own[4 + b]
    m3_out[pl.ds(1664, 64)] = MOMENTUM * m3_ref[pl.ds(1664, 64)] + own[17, :64]


def local(act_one, pre_two, cot_three, weight_two, weight_three, moment_two, moment_three):
    scale_two = (act_one.shape[1] * 27) ** (-0.5)
    scale_three = (pre_two.shape[1] * 27) ** (-0.5)
    volumes = lax.axis_size("dp")
    pre, act, cot = pre_two[0], act_one[0], cot_three[0]

    cot_rows, send_side, send_a, send_b, send_da, send_db, w3_near = call(
        arrange,
        [((2, 128, 512), BF16), ((1024, 128), BF16), ((512, 128), BF16),
         ((512, 128), BF16), ((512, 128), BF16), ((128, 128), BF16),
         ((1792, 128), F32)],
        [pltpu.VMEM((128, 2, 512), BF16), pltpu.VMEM((64, 4, 16, 128), BF16), pltpu.VMEM((32, 16, 128), BF16),
         pltpu.SemaphoreType.DMA((7,))],
        moved=4_000_000, far=(0, 1, 2, 3),
    )(cot, pre, act, weight_three.T)
    tall = lax.axis_size("height")
    swap = [(0, 1), (1, 0)]
    pairs_a = [(h, h ^ 1) for h in range(tall)]
    pairs_b = [(h, ((h + 1) ^ 1) - 1) for h in range(1, tall - 1)]
    cross_a, cross_b = (
        [(d * tall + i, (1 - d) * tall + j) for d in range(2) for i, j in pairs] for pairs in (pairs_a, pairs_b)
    )
    side = lax.ppermute(send_side, "depth", swap)
    got_a = lax.ppermute(send_a, "height", pairs_a)
    got_da = lax.ppermute(send_da, ("depth", "height"), cross_a)
    got_b = lax.ppermute(send_b, "height", pairs_b)
    got_db = lax.ppermute(send_db, ("depth", "height"), cross_b)

    pre_rows, pooled, acts, wide_two, wide_three, moments = call(
        prepare,
        [((4, 16, 64, 128), BF16), ((128, 512), BF16), ((16, 384, 128), BF16), ((192, 768), BF16), ((192, 1152), BF16), ((24, 128), F32)],
        [pltpu.VMEM((896, 64), F32)],
        flops=100_000_000, moved=8_000_000,
    )(pre, act, weight_two, w3_near, moment_two, moment_three)

    back, part_three = call(
        lambda *refs: coarse(scale_three, *refs),
        [((2, 64, 768), BF16), ((14, 128, 128), F32)],
        [pltpu.VMEM((3, 1152, 768), BF16), pltpu.VMEM((2, 64, 768), F32), pltpu.VMEM((3, 64, 1152), F32),
         pltpu.VMEM((1792, 128), F32)],
        flops=2_000_000_000, moved=4_000_000,
    )(cot_rows, side, got_a, got_da, got_b, got_db, wide_three, pooled)

    mine, theirs = call(
        fine,
        [((64, 24, 128), F32), ((64, 24, 128), BF16)],
        [pltpu.VMEM((4, 18, 64, 128), BF16), pltpu.VMEM((2, 10, 64, 128), F32), pltpu.VMEM((16, 96, 128), BF16), pltpu.VMEM((3, 96, 192), F32),
         pltpu.VMEM((944, 64), F32), pltpu.VMEM((64, 24, 128), F32), pltpu.VMEM((4, 136, 128), F32)],
        flops=2_000_000_000, moved=6_000_000,
    )(back, pre_rows, got_a, got_b, acts, side, part_three, moments)

    cores = [(i, i ^ 1) for i in range(lax.axis_size("dp"))]
    plane = lax.axis_size(("depth", "height"))
    groups = [[i * plane + j for i in range(k, lax.axis_size("dp"), 2) for j in range(plane)] for k in range(2)]
    got = lax.ppermute(theirs, "dp", cores)
    parts, = call(
        combine,
        [((64, 24, 128), BF16)],
        [pltpu.VMEM((64, 24, 128), BF16), pltpu.SemaphoreType.DMA((4,))],
        moved=2_000_000, far_out=(0,),
    )(mine, got)
    parts = lax.all_to_all(parts, AXES, 0, 0, axis_index_groups=groups, tiled=True)
    into_rows, ship = call(
        into,
        [((4, 16, 32, 128), F32), ((16, 32, 128), BF16)],
        [pltpu.VMEM((4, 18, 64, 128), BF16), pltpu.VMEM((2, 10, 64, 128), F32), pltpu.VMEM((4, 16, 32, 128), F32),
         pltpu.SemaphoreType.DMA((4,))],
        flops=4_000_000_000, moved=6_000_000, far_out=(0,),
    )(back, pre, got_a, got_b, wide_two)
    ship = lax.ppermute(ship, "depth", swap)
    parts, into_rows, ship = lax.optimization_barrier((parts, into_rows, ship))
    grad_input, = call(
        lambda *refs: finish(scale_two, *refs),
        [((32, 4, 16, 128), BF16)],
        moved=2_000_000,
    )(into_rows, ship)

    send, own = call(
        lambda *refs: reduce(scale_two / volumes, scale_three / volumes, *refs),
        [((64, 32, 128), BF16), ((18, 128), F32)],
        [pltpu.VMEM((32, 128), F32), pltpu.VMEM((16, 32, 128), BF16), pltpu.SemaphoreType.DMA((4,))],
        moved=2_000_000, far_out=(0,),
    )(parts, moments)
    own, w2, w3 = lax.optimization_barrier((own, weight_two, weight_three))
    full = lax.all_to_all(send, AXES, 0, 0, axis_index_groups=groups, tiled=True)
    other = lax.ppermute(full, "dp", cores)
    new_weight_two, new_weight_three, new_moment_two, new_moment_three = call(
        update,
        [(weight_two.shape, F32), (weight_three.shape[::-1], F32), (moment_two.shape, F32), (moment_three.shape, F32)],
        [pltpu.VMEM((136, 18, 128), F32)],
        moved=4_000_000,
    )(full, other, parts, own, w2, w3.T, moment_two, moment_three)
    return (grad_input[None], new_weight_two, new_weight_three.T, new_moment_two, new_moment_three)


def solution(mesh):
    in_specs = (
        P("dp", None, "depth", "height", None),
        P("dp", None, "depth", "height", None),
        P("dp", None, "depth", "height"),
        P(),
        P(),
        P(AXES),
        P(AXES),
    )
    out_specs = (
        P("dp", None, "depth", "height", None),
        P(),
        P(),
        P(AXES),
        P(AXES),
    )
    return jax.shard_map(local, mesh=mesh, in_specs=in_specs, out_specs=out_specs, check_vma=False)
```
